128 devices in a mesh: seq: 4 (over x), ctx: 16 (over z, y), dp: 2 (over core).
Axes of the slice: x: 4, y: 4, z: 4, core: 2. Of those that a mesh axis runs over, the one named last changes fastest.
Arguments:
- tokens: bfloat16 [2, 8192, 768], P('dp', ('seq', 'ctx')), may hold values from -6 to 6
- qkv_weight: bfloat16 [768, 2304], P(('seq', 'ctx', 'dp')), may hold values from -0.3125 to 0.3125
- out_weight: bfloat16 [768, 768], P(('seq', 'ctx', 'dp')), may hold values from -0.875 to 0.875
- router_weight: bfloat16 [768, 32], P(('seq', 'ctx', 'dp')), may hold values from -0.15625 to 0.15625
- attn_gain: bfloat16 [768], P(('seq', 'ctx', 'dp')), may hold values from 0.5 to 1.5
- ffn_gain: bfloat16 [768], P(('seq', 'ctx', 'dp')), may hold values from 0.5 to 1.5
- query_bias: bfloat16 [768], P(('seq', 'ctx', 'dp')), may hold values from -3 to 3
- value_bias: bfloat16 [768], P(('seq', 'ctx', 'dp')), may hold values from -0.8984375 to 0.8984375
- out_bias: bfloat16 [768], P(('seq', 'ctx', 'dp')), may hold values from -1.1953125 to 1.1953125
- expert_in: bfloat16 [32, 768, 3072], P(('ctx', 'dp'), None, 'seq'), may hold values from -0.21875 to 0.21875
- expert_out: bfloat16 [32, 768, 3072], P(('ctx', 'dp'), None, 'seq'), may hold values from -0.109375 to 0.109375
- expert_ids: int32 [2, 8192, 2], P('dp', ('seq', 'ctx')), may hold values from 0 to 31, all different within a row; in each aligned block of 128 rows (0 to 127, 128 to 255, ..., all dimensions but the last counted through in order) at most 9 rows name the same one
- cotangent: bfloat16 [2, 8192, 768], P('dp', ('seq', 'ctx')), may hold values from -6 to 6
Outputs:
- mixed: bfloat16 [2, 8192, 768], P('dp', ('seq', 'ctx'))
- input_grad: bfloat16 [2, 8192, 768], P('dp', ('seq', 'ctx'))
- qkv_grad: float32 [768, 2304], P(('seq', 'ctx', 'dp'))
- out_grad: float32 [768, 768], P(('seq', 'ctx', 'dp'))
- router_grad: float32 [768, 32], P(('seq', 'ctx', 'dp'))
- attn_gain_grad: float32 [768], P(('seq', 'ctx', 'dp'))
- ffn_gain_grad: float32 [768], P(('seq', 'ctx', 'dp'))
- query_bias_grad: float32 [768], P(('seq', 'ctx', 'dp'))
- value_bias_grad: float32 [768], P(('seq', 'ctx', 'dp'))
- out_bias_grad: float32 [768], P(('seq', 'ctx', 'dp'))
- expert_in_grad: float32 [32, 768, 3072], P(('ctx', 'dp'), None, 'seq')
- expert_out_grad: float32 [32, 768, 3072], P(('ctx', 'dp'), None, 'seq')
The draws below stay inside these ranges and needn't reach their ends.
Inputs may be any that keep to these rules, and one draw needn't show every extreme that they name: `expert_ids`: in the 128 rows of one device, no expert is named by more than 9 of the 2 choices of its tokens, and in every draw some expert is named exactly 9 times there; a token's 2 experts differ.
All inputs are finite; a program needn't handle non-finite values.
Results may differ from the reference program's by a relative error of at most 0.024.
Values may be sent and summed in bfloat16 or wider, within the bound.
No kernel may reach another device: no remote copies, remote signals or barrier semaphores. Data moves between devices by JAX's collectives and lax.ppermute only.
A program may use at most 128 MiB of HBM per device.

```python
import math
import jax
import jax.numpy as jnp
import numpy as np
from jax import lax

D = 768
H = 12
HD = 64
FF = 3072
TOPK = 2
TOK_DEV = 128
SEQ_LEN = 8192
SEQS = 2
EXPERTS = 32
CAP = 9
N_SEQ = 4


def level_of(rng, extent, split, least, high):
    def one(position, blocks):
        heights = jax.random.uniform(jax.random.fold_in(jax.random.fold_in(rng, 6), position), (blocks,), jnp.float32, least / len(split), high / len(split))
        return jnp.repeat(jnp.exp(heights), extent[position] // blocks).reshape((-1,) + (1,) * (len(extent) - position - 1))

    level = one(*split[0])
    for cut in split[1:]:
        level = level * one(*cut)
    return level


def deal_out(own_key, own, number, rows, number_of, top, most, skew):
    ranking = jax.random.permutation(own_key, number_of)
    heavy_load, common = portions_of(number_of, rows * top, most, skew, True), portions_of(number_of, rows * top, most, skew, False)
    places = jnp.arange(number_of)

    def named(lengths, turn):
        used = int((lengths > 0).sum())
        fixed = max(1, used // 4)
        shifted = fixed + (places - fixed + turn * (used - fixed)) % max(1, number_of - fixed)
        return jnp.zeros((number_of,), jnp.int32).at[ranking[jnp.where(places < fixed, places, shifted)]].set(jnp.asarray(lengths, jnp.int32))

    lengths = jnp.where(number % 4 == 0, named(heavy_load, number // 4), named(common, number - number // 4 - 1))
    mixed = jax.random.permutation(jax.random.fold_in(own, 3), number_of)
    giver, receiver = mixed[0:number_of // 2 * 2:2], mixed[1:number_of // 2 * 2:2]
    margin = jnp.minimum(lengths[giver] - 1, most - lengths[receiver]) // 2
    margin = jnp.where((giver == ranking[0]) | (receiver == ranking[0]) | (lengths[receiver] == 0), 0, jnp.maximum(margin, 0))
    shifted = jax.random.randint(jax.random.fold_in(own, 4), (number_of // 2,), 0, 1 << 20) % (margin + 1)
    lengths = lengths.at[giver].add(-shifted).at[receiver].add(shifted)
    members = jnp.searchsorted(jnp.cumsum(lengths), jnp.arange(rows * top), side="right").astype(jnp.int32)
    listing = members.reshape(top, rows).T
    listing = listing[jax.random.permutation(jax.random.fold_in(own, 1), rows)]
    turn = jax.random.randint(jax.random.fold_in(own, 2), (rows, 1), 0, top)
    return jnp.take_along_axis(listing, (jnp.arange(top)[None, :] + turn) % top, axis=1)


def portions_of(amount, total, bound, lean, full):
    portions = [(1 << 20) // math.isqrt(grade ** lean) + 1 for grade in range(1, amount + 1)]
    largest = bound if full else min(bound, max(-(-total // amount), total * portions[0] // sum(portions)))
    least = 1 if total - largest >= amount - 1 else 0
    given, rest = [largest] + [least] * (amount - 1), total - largest - least * (amount - 1)
    while rest > 0:
        free = [i for i in range(1, amount) if given[i] < largest] or [i for i in range(1, amount) if given[i] < bound]
        whole, remaining = sum([portions[i] for i in free]), rest
        for i in free:
            extra = min(bound - given[i], max(1, remaining * portions[i] // whole), rest)
            given[i] = given[i] + extra
            rest = rest - extra
    return np.array(given)


def normal_values(stream_key, extent, scale, limit, shards=(), kind=jnp.bfloat16):
    gain = level_of(stream_key, extent, shards, -0.22, 0.18) if shards else 1.0
    values = jax.random.normal(stream_key, extent, jnp.float32) * scale * gain
    return jnp.minimum(jnp.maximum(values, -limit), limit).astype(kind)


def setup_inputs(seed: int = 0) -> dict:
    streams_of = jax.random.split(jax.random.key(seed), 14)
    tokens = normal_values(streams_of[0], (SEQS, SEQ_LEN, D), 1.0, 6.0, ((0, 2), (1, 64)))
    qkv_weight = normal_values(streams_of[1], (D, 3 * D), (D // 2) ** -0.5, 0.3125, ((0, 128),))
    out_weight = normal_values(streams_of[2], (D, D), (D // 16) ** -0.5, 0.875, ((0, 128),))
    router_weight = normal_values(streams_of[3], (D, EXPERTS), (2 * D) ** -0.5, 0.15625, ((0, 128),))
    attn_gain = jnp.clip(1.0 + 0.1 * jax.random.normal(streams_of[4], (D,), jnp.float32), 0.5, 1.5).astype(jnp.bfloat16)
    ffn_gain = jnp.clip(1.0 + 0.1 * jax.random.normal(streams_of[5], (D,), jnp.float32), 0.5, 1.5).astype(jnp.bfloat16)
    query_bias = normal_values(streams_of[6], (D,), 0.5, 3.0, ((0, 128),))
    value_bias = normal_values(streams_of[7], (D,), 0.15, 0.8984375, ((0, 128),))
    out_bias = normal_values(streams_of[8], (D,), 0.2, 1.1953125, ((0, 128),))
    expert_in = normal_values(streams_of[9], (EXPERTS, D, FF), D ** -0.5, 0.21875, ((0, 32), (2, 4)))
    expert_out = normal_values(streams_of[10], (EXPERTS, D, FF), FF ** -0.5, 0.109375, ((0, 32), (2, 4)))
    expert_ids_keys = jax.random.split(jax.random.fold_in(streams_of[11], 1), SEQS * SEQ_LEN // TOK_DEV)
    expert_ids_turns = jax.random.permutation(jax.random.fold_in(streams_of[11], 3), SEQS * SEQ_LEN // TOK_DEV)
    expert_ids = jax.vmap(lambda own, number: deal_out(jax.random.fold_in(streams_of[11], 2), own, number, TOK_DEV, EXPERTS, TOPK, CAP, 1))(expert_ids_keys, expert_ids_turns).reshape((SEQS, SEQ_LEN, TOPK))
    cotangent = normal_values(streams_of[12], (SEQS, SEQ_LEN, D), 1.0, 6.0, ((0, 2), (1, 64)))
    return {"tokens": tokens, "qkv_weight": qkv_weight, "out_weight": out_weight, "router_weight": router_weight, "attn_gain": attn_gain, "ffn_gain": ffn_gain, "query_bias": query_bias, "value_bias": value_bias, "out_bias": out_bias, "expert_in": expert_in, "expert_out": expert_out, "expert_ids": expert_ids, "cotangent": cotangent}


EPS = 1e-06
MASKED = -1e+30
PRECISE = lax.Precision.HIGHEST

@jax.custom_vjp
def low(v):
    return lax.optimization_barrier(v.astype(jnp.bfloat16)).astype(jnp.float32)

@jax.custom_vjp
def low_back(v):
    return v

def low_keep(v):
    return (low(v), None)

def low_pass(kept, grad):
    return (grad,)

def back_keep(v):
    return (v, None)

def back_low(kept, grad):
    return (low(grad),)
low.defvjp(low_keep, low_pass)
low_back.defvjp(back_keep, back_low)

def normed(values, gains):
    return values * lax.rsqrt(lax.optimization_barrier(jnp.mean(values * values, axis=-1, keepdims=True)) + EPS) * gains

def softened(scores):
    highest = lax.optimization_barrier(jnp.max(scores, axis=-1, keepdims=True))
    weights = jnp.exp(scores - highest)
    return weights / lax.optimization_barrier(jnp.sum(weights, axis=-1, keepdims=True))

def attend_sequence(pieces):
    queries, key_rows, value_rows = pieces
    block_rows = N_SEQ * TOK_DEV
    key_position = jnp.arange(SEQ_LEN, dtype=jnp.int32)

    def one_block(element):
        query_block, query_position = element
        scores = jnp.einsum('qhd,khd->hqk', query_block, key_rows, precision=PRECISE) * HD ** (-0.5)
        scores = low_back(scores)
        scores = jnp.where(key_position[None, None, :] <= query_position[None, :, None], scores, MASKED)
        probs = low(softened(scores))
        return jnp.einsum('hqk,khd->qhd', probs, value_rows, precision=PRECISE)
    query_blocks = queries.reshape(SEQ_LEN // block_rows, block_rows, H, HD)
    position_blocks = key_position.reshape(SEQ_LEN // block_rows, block_rows)
    result = lax.map(jax.checkpoint(one_block), (query_blocks, position_blocks))
    return result.reshape(SEQ_LEN, H, HD)

def expert_block(element):
    rows_in, inner, outer = element
    pre_act = low_back(jnp.dot(rows_in, inner, precision=PRECISE))
    activated = low(jax.nn.gelu(pre_act, approximate=True))
    return jnp.dot(activated, outer.T, precision=PRECISE)

def places_of(expert_ids):
    flat = expert_ids.reshape(-1, TOK_DEV * TOPK).astype(jnp.int32)
    onehot = (flat[..., None] == jnp.arange(EXPERTS, dtype=jnp.int32)[None, None, :]).astype(jnp.int32)
    slots = lax.optimization_barrier(jnp.sum((jnp.cumsum(onehot, axis=1) - 1) * onehot, axis=-1))
    blocks = flat.shape[0]
    block_id = jnp.arange(blocks, dtype=jnp.int32)[:, None]
    return (flat * (blocks * CAP) + block_id * CAP + slots).reshape(-1).astype(jnp.int32)

def reference(tokens, qkv_weight, out_weight, router_weight, attn_gain, ffn_gain, query_bias, value_bias, out_bias, expert_in, expert_out, expert_ids, cotangent):
    target = places_of(expert_ids)
    blocks = SEQS * SEQ_LEN // TOK_DEV
    routes = expert_ids.reshape(-1, TOPK).astype(jnp.int32)

    def forward(inputs, w_qkv, w_out, w_router, gain_one, gain_two, bias_query, bias_value, bias_out, inner, outer):
        rows = inputs.reshape(-1, D)
        first_in = low(normed(rows, gain_one))
        projected = jnp.dot(first_in, w_qkv, precision=PRECISE)
        queries = low_back(low(projected[:, :D] + bias_query))
        key_rows = low_back(low(projected[:, D:2 * D]))
        value_rows = low_back(low(projected[:, 2 * D:] + bias_value))
        shaped = (queries.reshape(SEQS, SEQ_LEN, H, HD), key_rows.reshape(SEQS, SEQ_LEN, H, HD), value_rows.reshape(SEQS, SEQ_LEN, H, HD))
        attended = lax.map(attend_sequence, shaped).reshape(-1, D)
        attended = low_back(low(attended))
        middle = rows + low_back(jnp.dot(attended, w_out, precision=PRECISE) + bias_out)
        second_in = low(normed(middle, gain_two))
        logits = low_back(jnp.dot(second_in, w_router, precision=PRECISE))
        gates = softened(jnp.take_along_axis(logits, routes, axis=1))
        buffer = jnp.zeros((EXPERTS * blocks * CAP, D), jnp.float32).at[target].set(jnp.repeat(second_in, TOPK, axis=0))
        buffer = low_back(buffer).reshape(EXPERTS, blocks * CAP, D)
        produced = lax.map(jax.checkpoint(expert_block), (buffer, inner, outer))
        produced = low_back(low(produced)).reshape(-1, D)
        picked = produced[target].reshape(-1, TOPK, D)
        return (middle + lax.optimization_barrier(jnp.sum(gates[..., None] * picked, axis=1))).reshape(inputs.shape)
    primals = tuple((item_array.astype(jnp.float32) for item_array in (tokens, qkv_weight, out_weight, router_weight, attn_gain, ffn_gain, query_bias, value_bias, out_bias, expert_in, expert_out)))
    mixed, pullback = jax.vjp(forward, *primals)
    grads = pullback(cotangent.astype(jnp.float32))
    return (mixed.astype(jnp.bfloat16), grads[0].astype(jnp.bfloat16), grads[1], grads[2], grads[3], grads[4], grads[5], grads[6], grads[7], grads[8], grads[9], grads[10])
```

```python
import functools

import jax
import jax.numpy as jnp
import numpy as np
from jax import lax
from jax.experimental import pallas as pl
from jax.experimental.pallas import tpu as pltpu
from jax.sharding import PartitionSpec as P

H = 12
HD = 64
TOPK = 2
D = 768
T = 128
NS = 4
HL = H // NS
HW = HL * HD
QR = NS * T
CD = 32
CAP = 9
SLOTS = 24
ROWS = CD * SLOTS
LINES = CD * CAP
PACK = 208

EPS = 1e-06
MASKED = -1e30
BF = jnp.bfloat16
F32 = jnp.float32

VMEM = pl.BlockSpec(memory_space=pltpu.VMEM)
SMEM = pl.BlockSpec(memory_space=pltpu.SMEM)


def dot(former, latter, former_dim, latter_dim):
    return lax.dot_general(
        former,
        latter,
        (((former_dim,), (latter_dim,)), ((), ())),
        preferred_element_type=F32,
    )


def params(**more):
    return pltpu.CompilerParams(vmem_limit_bytes=56 * 1024 * 1024, **more)


def shift_seq(values, steps):
    return lax.ppermute(values, "seq", [(i, (i + steps) % NS) for i in range(NS)])


def shift_z(values, steps):
    pairs = [(z * NS + y, (z + steps) % NS * NS + y) for z in range(NS) for y in range(NS)]
    return lax.ppermute(values, "ctx", pairs)


def shift_y(values, steps):
    pairs = [(z * NS + y, z * NS + (y + steps) % NS) for z in range(NS) for y in range(NS)]
    return lax.ppermute(values, "ctx", pairs)


def collect(values, shift):
    return [values] + [shift(values, -i) for i in range(1, NS)]


def deliver(pieces, shift):
    return [pieces[0]] + [shift(pieces[i], i) for i in range(1, NS)]


def swap_seq(values):
    return lax.all_to_all(values, "seq", split_axis=0, concat_axis=0, tiled=True)


def swap_experts(values):
    return lax.all_to_all(values, ("ctx", "dp"), split_axis=0, concat_axis=0, tiled=True)


def gather_seq(values):
    place = lax.axis_index("seq")
    whole = jnp.zeros((NS,) + values.shape, values.dtype)
    for i, piece in enumerate(collect(values, shift_seq)):
        whole = lax.dynamic_update_slice(whole, piece[None], ((place + i) % NS, 0, 0))
    return whole


def scatter_seq(values):
    place = lax.axis_index("seq")
    pieces = [
        lax.dynamic_slice(values, ((place + i) % NS, 0, 0), (1,) + values.shape[1:])[0]
        for i in range(NS)
    ]
    return deliver(pieces, shift_seq)


def tile_of(refs, rows, j):
    return jnp.concatenate([ref[rows, j * T : (j + 1) * T] for ref in refs], axis=1)


def causal_tile(place_ref):
    z, y = place_ref[0], place_ref[1]
    k_index = lax.broadcasted_iota(jnp.int32, (QR, QR), 0)
    q_index = lax.broadcasted_iota(jnp.int32, (QR, QR), 1)
    k_place = z * QR + (((y + (k_index >> 7)) & 3) << 7) + (k_index & 127)
    q_place = (((z + (q_index >> 7)) & 3) << 9) + y * T + (q_index & 127)
    return k_place <= q_place


def split3(values):
    high = values.astype(BF).astype(F32)
    middle = (values - high).astype(BF).astype(F32)
    return high, middle, values - high - middle


def attend_kernel(place_ref, *refs):
    q_refs, kv_refs, o_refs = refs[0:4], refs[4:8], refs[8:12]
    lse_ref, bias_ref = refs[12], refs[13]
    bias_ref[...] = jnp.where(causal_tile(place_ref), 0.0, MASKED)

    def head(h, carry):
        rows = pl.ds(pl.multiple_of(h * HD, HD), HD)
        v_rows = pl.ds(pl.multiple_of(HW + h * HD, HD), HD)
        for j in range(NS):
            q_tile = tile_of(q_refs, rows, j)
            top = total = acc = None
            for jp in range(j + 1):
                k_tile = tile_of(kv_refs, rows, jp)
                v_tile = tile_of(kv_refs, v_rows, jp)
                scores = dot(k_tile, q_tile, 0, 0)
                if jp == j:
                    scores = jnp.where(bias_ref[...] < 0.0, MASKED, scores)
                here = jnp.max(scores, axis=0, keepdims=True)
                if jp == 0:
                    top = here
                    probs = jnp.exp(scores - top)
                    total = jnp.sum(probs, axis=0, keepdims=True)
                    acc = dot(v_tile, probs.astype(BF), 1, 0)
                else:
                    higher = jnp.maximum(top, here)
                    fade = jnp.exp(top - higher)
                    probs = jnp.exp(scores - higher)
                    total = total * fade + jnp.sum(probs, axis=0, keepdims=True)
                    acc = acc * fade + dot(v_tile, probs.astype(BF), 1, 0)
                    top = higher
            out = (acc / total).astype(BF)
            lse = top + jnp.log(total)
            for i in range(NS):
                o_refs[i][rows, j * T : (j + 1) * T] = out[:, i * T : (i + 1) * T]
                lse_ref[h, i : i + 1, j * T : (j + 1) * T] = lse[:, i * T : (i + 1) * T]
        return carry

    lax.fori_loop(0, HL, head, 0)
    for i in range(NS):
        logs = jnp.concatenate([lse_ref[h, i : i + 1, :] for h in range(HL)], axis=0)
        high, middle, low = split3(logs)
        rest = jnp.zeros((PACK - HW - 3 * HL, QR), F32)
        o_refs[i][HW:PACK, :] = jnp.concatenate([high, middle, low, rest], axis=0).astype(BF)


def attend(place, queries, keyvals):
    return pl.pallas_call(
        attend_kernel,
        out_shape=[jax.ShapeDtypeStruct((PACK, QR), BF)] * NS,
        in_specs=[SMEM] + [VMEM] * 8,
        out_specs=[VMEM] * NS,
        scratch_shapes=[pltpu.VMEM((HL, 8, QR), F32), pltpu.VMEM((QR, QR), F32)],
        compiler_params=params(),
        cost_estimate=pl.CostEstimate(
            flops=4 * 30 * QR * QR * HD, bytes_accessed=4 << 20, transcendentals=30 * QR * QR
        ),
        name="attend",
    )(place, *queries, *keyvals)


def lse_of(stats):
    return stats[0:HL] + stats[HL : 2 * HL] + stats[2 * HL : 3 * HL]


def merge_kernel(*refs):
    parts, o_ref, stat_ref = refs[0:4], refs[4], refs[5]
    logs = [lse_of(part[HW:PACK, :].astype(F32)) for part in parts]
    top = functools.reduce(jnp.maximum, logs)
    lse = top + jnp.log(functools.reduce(jnp.add, [jnp.exp(log - top) for log in logs]))
    shares = [jnp.exp(log - lse) for log in logs]
    for h in range(HL):
        rows = slice(h * HD, (h + 1) * HD)
        o_ref[rows, :] = functools.reduce(
            jnp.add,
            [part[rows, :].astype(F32) * share[h : h + 1] for part, share in zip(parts, shares)],
        ).astype(BF)
    stat_ref[...] = jnp.concatenate([lse, jnp.zeros((8 - HL, QR), F32)], axis=0)


def merge(parts):
    return pl.pallas_call(
        merge_kernel,
        out_shape=[jax.ShapeDtypeStruct((HW, QR), BF), jax.ShapeDtypeStruct((8, QR), F32)],
        in_specs=[VMEM] * 4,
        out_specs=[VMEM] * 2,
        compiler_params=params(),
        name="merge",
    )(*parts)


def grad_heads_kernel(db_ref, w_ref, o_ref, lse_ref, out_ref):
    grads = dot(w_ref[...], db_ref[...], 1, 1).astype(BF)
    out_ref[0:HW, :] = grads
    product = grads.astype(F32) * o_ref[...].astype(F32)
    delta = jnp.concatenate(
        [jnp.sum(product[h * HD : (h + 1) * HD], axis=0, keepdims=True) for h in range(HL)], axis=0
    )
    high, middle, low = split3(lse_ref[0:HL, :])
    d_high, d_middle, unused = split3(delta)
    rest = jnp.zeros((PACK - HW - 5 * HL, QR), F32)
    out_ref[HW:PACK, :] = jnp.concatenate(
        [high, middle, low, d_high, d_middle, rest], axis=0
    ).astype(BF)


def grad_heads(rows, weight, attended, lse):
    return pl.pallas_call(
        grad_heads_kernel,
        out_shape=jax.ShapeDtypeStruct((PACK, QR), BF),
        in_specs=[VMEM] * 4,
        out_specs=VMEM,
        compiler_params=params(),
        name="grad_heads",
    )(rows, weight, attended, lse)


def attend_back_kernel(place_ref, *refs):
    q_refs, kv_refs, do_refs = refs[0:4], refs[4:8], refs[8:12]
    dq_refs, dkv_refs = refs[12:16], refs[16:20]
    lse_ref, delta_ref, bias_ref, dq_ref = refs[20:24]
    bias_ref[...] = jnp.where(causal_tile(place_ref), 0.0, MASKED)
    for i in range(NS):
        stats = do_refs[i][HW:PACK, :].astype(F32)
        logs = lse_of(stats)
        deltas = stats[3 * HL : 4 * HL] + stats[4 * HL : 5 * HL]
        for h in range(HL):
            lse_ref[h, i : i + 1, :] = logs[h : h + 1]
            delta_ref[h, i : i + 1, :] = deltas[h : h + 1]

    def head(h, carry):
        rows = pl.ds(pl.multiple_of(h * HD, HD), HD)
        v_rows = pl.ds(pl.multiple_of(HW + h * HD, HD), HD)

        def stat(ref, j):
            return jnp.concatenate(
                [ref[h, i : i + 1, j * T : (j + 1) * T] for i in range(NS)], axis=1
            )

        for jp in range(NS):
            k_tile = tile_of(kv_refs, rows, jp)
            v_tile = tile_of(kv_refs, v_rows, jp)
            dk = dv = None
            for j in range(jp, NS):
                q_tile = tile_of(q_refs, rows, j)
                do_tile = tile_of(do_refs, rows, j)
                scores = dot(k_tile, q_tile, 0, 0)
                if jp == j:
                    scores = jnp.where(bias_ref[...] < 0.0, MASKED, scores)
                probs = jnp.exp(scores - stat(lse_ref, j))
                slopes = dot(v_tile, do_tile, 0, 0)
                ds = (probs * (slopes - stat(delta_ref, j))).astype(BF)
                dv_here = dot(do_tile, probs.astype(BF), 1, 1)
                dk_here = dot(q_tile, ds, 1, 1)
                dq_here = dot(k_tile, ds, 1, 0)
                dv = dv_here if dv is None else dv + dv_here
                dk = dk_here if dk is None else dk + dk_here
                if jp == 0:
                    dq_ref[j] = dq_here
                else:
                    dq_ref[j] += dq_here
            dk, dv = dk.astype(BF), dv.astype(BF)
            for i in range(NS):
                dkv_refs[i][rows, jp * T : (jp + 1) * T] = dk[:, i * T : (i + 1) * T]
                dkv_refs[i][v_rows, jp * T : (jp + 1) * T] = dv[:, i * T : (i + 1) * T]
        for j in range(NS):
            dq = (dq_ref[j] * HD ** (-0.5)).astype(BF)
            for i in range(NS):
                dq_refs[i][rows, j * T : (j + 1) * T] = dq[:, i * T : (i + 1) * T]
        return carry

    lax.fori_loop(0, HL, head, 0)


def attend_back(place, queries, keyvals, grads):
    out = pl.pallas_call(
        attend_back_kernel,
        out_shape=[jax.ShapeDtypeStruct((HW, QR), BF)] * NS
        + [jax.ShapeDtypeStruct((2 * HW, QR), BF)] * NS,
        in_specs=[SMEM] + [VMEM] * 12,
        out_specs=[VMEM] * 8,
        scratch_shapes=[
            pltpu.VMEM((HL, 8, QR), F32),
            pltpu.VMEM((HL, 8, QR), F32),
            pltpu.VMEM((QR, QR), F32),
            pltpu.VMEM((NS, HD, QR), F32),
        ],
        compiler_params=params(),
        cost_estimate=pl.CostEstimate(
            flops=10 * 30 * QR * QR * HD, bytes_accessed=6 << 20, transcendentals=30 * QR * QR
        ),
        name="attend_back",
    )(place, *queries, *keyvals, *grads)
    return out[0:NS], out[NS:]


def pick_rows(target, offset):
    lines = lax.broadcasted_iota(jnp.int32, (T, ROWS), 1)
    return (lines == target + offset).astype(F32).astype(BF)


def norm_two(middle):
    factor = lax.rsqrt(jnp.mean(middle * middle, axis=-1, keepdims=True) + EPS)
    return middle * factor, factor


def route_kernel(
    x_ref, branch_ref, small_ref, router_ref, ids_ref, cot_ref,
    out_ref, m_ref, a_ref, gate_ref, target_ref,
):
    branch = functools.reduce(jnp.add, [branch_ref[i].astype(F32) for i in range(NS)])
    middle = x_ref[...].astype(F32) + branch + small_ref[2:3, :]
    unit, factor = norm_two(middle)
    second = (unit * small_ref[1:2, :]).astype(BF)
    logits = dot(second, router_ref[...], 1, 0)
    cols = lax.broadcasted_iota(jnp.int32, (T, CD), 1)
    named = [(ids_ref[:, k : k + 1] == cols).astype(F32) for k in range(TOPK)]
    earlier = lax.broadcasted_iota(jnp.int32, (T, T), 1) < lax.broadcasted_iota(
        jnp.int32, (T, T), 0
    )
    counts = dot(earlier.astype(F32).astype(BF), (named[0] + named[1]).astype(BF), 1, 0)
    chosen = [jnp.sum(name * logits, axis=1, keepdims=True) for name in named]
    top = jnp.maximum(chosen[0], chosen[1])
    raw = [jnp.exp(value - top) for value in chosen]
    gates = [value / (raw[0] + raw[1]) for value in raw]
    slots = [jnp.sum(name * counts, axis=1, keepdims=True).astype(jnp.int32) for name in named]
    targets = [ids_ref[:, k : k + 1] * SLOTS + slots[k] for k in range(TOPK)]
    grads = cot_ref[...].astype(F32)
    places = jnp.concatenate(
        [pick_rows(targets[0], 0) + pick_rows(targets[1], 0)]
        + [pick_rows(targets[k], CAP) for k in range(TOPK)],
        axis=0,
    )
    values = jnp.concatenate([second] + [(gates[k] * grads).astype(BF) for k in range(TOPK)], axis=0)
    out_ref[...] = dot(places, values, 0, 0).astype(BF)
    m_ref[...] = middle
    a_ref[...] = second
    gate_ref[...] = jnp.concatenate(gates, axis=1)
    target_ref[...] = jnp.concatenate(targets, axis=1)


def route(rows, branch, small, router, ids, cotangent):
    return pl.pallas_call(
        route_kernel,
        out_shape=[
            jax.ShapeDtypeStruct((ROWS, D), BF),
            jax.ShapeDtypeStruct((T, D), F32),
            jax.ShapeDtypeStruct((T, D), BF),
            jax.ShapeDtypeStruct((T, TOPK), F32),
            jax.ShapeDtypeStruct((T, TOPK), jnp.int32),
        ],
        in_specs=[VMEM] * 6,
        out_specs=[VMEM] * 5,
        compiler_params=params(),
        name="route",
    )(rows, branch, small, router, ids, cotangent)


GELU_A = float(np.sqrt(2.0 / np.pi))
GELU_B = 0.044715


def expert_kernel(
    rows_ref, pick_ref, win_ref, wout_ref, out_ref, gin_ref, gout_ref, a_ref, dy_ref, y_ref, da_ref
):
    step = pl.program_id(0)

    @pl.when(step == 0)
    def first():
        both = dot(pick_ref[...], rows_ref[...], 1, 0).astype(BF)
        a_ref[...] = both[0:LINES]
        dy_ref[...] = both[LINES:]

    rows, grads = a_ref[...], dy_ref[...]
    inner, outer = win_ref[0], wout_ref[0]
    pre = dot(rows, inner, 1, 0)
    square = pre * pre
    bent = jnp.tanh(GELU_A * pre * (1.0 + GELU_B * square))
    act = (0.5 * pre * (1.0 + bent)).astype(BF)
    slope = 0.5 * (1.0 + bent) + 0.5 * pre * (1.0 - bent * bent) * (
        GELU_A * (1.0 + 3.0 * GELU_B * square)
    )
    pre_grad = (dot(grads, outer, 1, 0) * slope).astype(BF)
    made = dot(act, outer, 1, 1)
    back = dot(pre_grad, inner, 1, 1)
    gin_ref[0] = dot(rows, pre_grad, 0, 0).astype(BF)
    gout_ref[0] = dot(grads, act, 0, 0).astype(BF)

    @pl.when(step == 0)
    def start():
        y_ref[...] = made
        da_ref[...] = back

    @pl.when(step > 0)
    def more():
        y_ref[...] += made
        da_ref[...] += back

    @pl.when(step == pl.num_programs(0) - 1)
    def last():
        both = jnp.concatenate([y_ref[...].astype(BF), da_ref[...].astype(BF)], axis=0)
        out_ref[...] = dot(pick_ref[...], both, 0, 0).astype(BF)


def expert_pick():
    lines = np.arange(LINES)
    pick = np.zeros((2 * LINES, ROWS), np.float32)
    pick[lines, lines // CAP * SLOTS + lines % CAP] = 1.0
    pick[LINES + lines, lines // CAP * SLOTS + CAP + lines % CAP] = 1.0
    return pick


def expert(rows, inner, outer):
    tile = 384
    halves = D // tile

    def weight_spec():
        return pl.BlockSpec((1, D, tile), lambda i: (i // halves, 0, i % halves))

    def whole(*shape):
        return pl.BlockSpec(shape, lambda i: (0, 0))

    return pl.pallas_call(
        expert_kernel,
        grid=(NS * halves,),
        out_shape=[
            jax.ShapeDtypeStruct((ROWS, D), BF),
            jax.ShapeDtypeStruct((NS, D, D), BF),
            jax.ShapeDtypeStruct((NS, D, D), BF),
        ],
        in_specs=[whole(ROWS, D), whole(2 * LINES, ROWS), weight_spec(), weight_spec()],
        out_specs=[whole(ROWS, D), weight_spec(), weight_spec()],
        scratch_shapes=[
            pltpu.VMEM((LINES, D), BF),
            pltpu.VMEM((LINES, D), BF),
            pltpu.VMEM((LINES, D), F32),
            pltpu.VMEM((LINES, D), F32),
        ],
        compiler_params=params(dimension_semantics=("arbitrary",)),
        cost_estimate=pl.CostEstimate(
            flops=12 * LINES * D * 4 * D, bytes_accessed=20 << 20, transcendentals=LINES * 4 * D
        ),
        name="expert",
    )(rows, jnp.asarray(expert_pick(), BF), inner, outer)


def settle_kernel(
    back_ref, m_ref, a_ref, gate_ref, target_ref, ids_ref, cot_ref, small_ref, router_ref,
    mixed_ref, db_ref, dm_ref, rg_ref, sums_ref,
):
    back = back_ref[...]
    targets = [target_ref[:, k : k + 1] for k in range(TOPK)]
    picked = [dot(pick_rows(target, 0), back, 1, 0) for target in targets]
    returned = dot(pick_rows(targets[0], CAP) + pick_rows(targets[1], CAP), back, 1, 0)
    middle = m_ref[...]
    grads = cot_ref[...].astype(F32)
    gates = [gate_ref[:, k : k + 1] for k in range(TOPK)]
    mixed_ref[...] = (middle + gates[0] * picked[0] + gates[1] * picked[1]).astype(BF)
    gate_grads = [jnp.sum(grads * value, axis=1, keepdims=True) for value in picked]
    mean = gates[0] * gate_grads[0] + gates[1] * gate_grads[1]
    cols = lax.broadcasted_iota(jnp.int32, (T, CD), 1)
    logit_grad = functools.reduce(
        jnp.add,
        [
            jnp.where(ids_ref[:, k : k + 1] == cols, gates[k] * (gate_grads[k] - mean), 0.0)
            for k in range(TOPK)
        ],
    ).astype(BF)
    rg_ref[...] = dot(a_ref[...], logit_grad, 0, 0)
    second_grad = dot(logit_grad, router_ref[...], 1, 1) + returned
    unit, factor = norm_two(middle)
    weighted = second_grad * small_ref[1:2, :]
    whole = grads + factor * (weighted - unit * jnp.mean(weighted * unit, axis=-1, keepdims=True))
    dm_ref[...] = whole
    rounded = whole.astype(BF)
    db_ref[...] = rounded
    sums_ref[...] = jnp.concatenate(
        [
            jnp.sum(second_grad * unit, axis=0, keepdims=True),
            jnp.sum(rounded.astype(F32), axis=0, keepdims=True),
            jnp.zeros((6, D), F32),
        ],
        axis=0,
    )


def settle(back, middle, second, gates, targets, ids, cotangent, small, router):
    return pl.pallas_call(
        settle_kernel,
        out_shape=[
            jax.ShapeDtypeStruct((T, D), BF),
            jax.ShapeDtypeStruct((T, D), BF),
            jax.ShapeDtypeStruct((T, D), F32),
            jax.ShapeDtypeStruct((D, CD), F32),
            jax.ShapeDtypeStruct((8, D), F32),
        ],
        in_specs=[VMEM] * 9,
        out_specs=[VMEM] * 5,
        compiler_params=params(),
        name="settle",
    )(back, middle, second, gates, targets, ids, cotangent, small, router)


def order_constant():
    order = np.zeros((D, D), np.float32)
    for g in range(D):
        s, rest = divmod(g, HW)
        c, i = divmod(rest, 6)
        order[g, c * 24 + s * 6 + i] = 1.0
    return order


def spread(rows, width):
    return jnp.pad(rows, [(0, 0)] * (rows.ndim - 1) + [(0, width - rows.shape[-1])])


def per_device(
    tokens,
    qkv_weight,
    out_weight,
    router_weight,
    attn_gain,
    ffn_gain,
    query_bias,
    value_bias,
    out_bias,
    expert_in,
    expert_out,
    expert_ids,
    cotangent,
):
    order = jnp.asarray(order_constant(), BF)
    ctx = lax.axis_index("ctx")
    place = jnp.stack([ctx // NS, ctx % NS]).astype(jnp.int32)
    rows = tokens.reshape(T, D)
    ids = expert_ids.reshape(T, TOPK)
    cot = cotangent.reshape(T, D)

    inner = lax.all_gather(expert_in[0], "seq", axis=0, tiled=False)
    outer = lax.all_gather(expert_out[0], "seq", axis=0, tiled=False)

    columns = qkv_weight.reshape(6, 3, NS, HW).transpose(2, 0, 1, 3).reshape(NS, 6, 3 * HW)
    extras = jnp.concatenate(
        [router_weight, attn_gain[:, None], ffn_gain[:, None], out_bias[:, None]], axis=1
    )
    sent = spread(
        jnp.concatenate([columns, jnp.broadcast_to(extras[None], (NS, 6, CD + 3))], axis=2), D
    )
    arrived = swap_seq(sent).reshape(NS * 6, D)
    mine = jnp.concatenate(
        [arrived, out_weight, spread(query_bias[None], D), spread(value_bias[None], D)], axis=0
    )
    everything = swap_experts(jnp.broadcast_to(mine[None], (CD, 32, D)))
    weights = everything[:, :24].reshape(D, D)
    sorted_weights = dot(order, weights, 1, 0).astype(BF)
    qkv = sorted_weights[:, : 3 * HW]
    router = sorted_weights[:, 3 * HW : 3 * HW + CD]
    small = dot(weights[:, 3 * HW + CD : 3 * HW + CD + 8], order, 0, 1)
    out_mine = everything[:, 24:30].reshape(HW, D)
    bias = jnp.concatenate(
        [
            everything[:, 30, :6].reshape(HW),
            jnp.zeros((HW,), BF),
            everything[:, 31, :6].reshape(HW),
        ]
    ).astype(F32)

    stream = gather_seq(rows).reshape(QR, D).astype(F32)
    factor = lax.rsqrt(jnp.mean(stream * stream, axis=-1, keepdims=True) + EPS)
    unit = stream * factor
    first_in = (unit * small[0:1]).astype(BF)
    projected = (dot(qkv, first_in, 0, 1) + bias[:, None]).astype(BF)
    queries = collect(projected[:HW] * jnp.asarray(HD ** (-0.5), BF), shift_z)
    keyvals = collect(projected[HW:], shift_y)
    attended, lse = merge(deliver(attend(place, queries, keyvals), shift_z))
    branch = swap_seq(dot(attended, out_mine, 0, 0).astype(BF).reshape(NS, T, D))

    outgoing, middle, second, gates, targets = route(rows, branch, small, router, ids, cot)
    received = swap_experts(outgoing.reshape(CD, SLOTS, D)).reshape(ROWS, D)
    made, inner_grad, outer_grad = expert(received, inner, outer)
    returned = swap_experts(made.reshape(CD, SLOTS, D)).reshape(ROWS, D)
    inner_grad = lax.psum_scatter(inner_grad, "seq", scatter_dimension=0, tiled=False)
    outer_grad = lax.psum_scatter(outer_grad, "seq", scatter_dimension=0, tiled=False)
    mixed, branch_grad, middle_grad, router_grad, sums = settle(
        returned, middle, second, gates, targets, ids, cot, small, router
    )

    branch_grads = gather_seq(branch_grad).reshape(QR, D)
    out_grad = dot(attended, branch_grads, 1, 0)
    heads_grad = collect(grad_heads(branch_grads, out_mine, attended, lse), shift_z)
    query_parts, keyval_parts = attend_back(place, queries, keyvals, heads_grad)
    query_grad = sum(part.astype(F32) for part in deliver(query_parts, shift_z))
    keyval_grad = sum(part.astype(F32) for part in deliver(keyval_parts, shift_y))
    projected_grad = jnp.concatenate([query_grad, keyval_grad], axis=0).astype(BF)

    first_grad = dot(projected_grad, qkv, 0, 1)
    gain_grad = jnp.sum(first_grad * unit, axis=0, keepdims=True)
    parts = scatter_seq(first_grad.astype(BF).reshape(NS, T, D))
    mine_grad = sum(part.astype(F32) for part in parts)
    own = rows.astype(F32)
    own_factor = lax.rsqrt(jnp.mean(own * own, axis=-1, keepdims=True) + EPS)
    own_unit = own * own_factor
    weighted = mine_grad * small[0:1]
    input_grad = middle_grad + own_factor * (
        weighted - own_unit * jnp.mean(weighted * own_unit, axis=-1, keepdims=True)
    )

    arrived_in = dot(first_in, order, 1, 0).astype(BF)
    qkv_grad = dot(arrived_in, projected_grad, 0, 1).astype(BF)
    lines = jnp.concatenate([gain_grad, sums[0:2]], axis=0).astype(BF)
    extra_grads = jnp.concatenate(
        [dot(order, router_grad.astype(BF), 0, 0), dot(order, lines, 0, 1)], axis=1
    ).astype(BF)
    main = spread(jnp.concatenate([qkv_grad, extra_grads], axis=1), D).reshape(CD, 24, D)
    bias_grads = jnp.sum(projected_grad.astype(F32), axis=1).astype(BF)
    grads = jnp.concatenate(
        [
            main,
            out_grad.astype(BF).reshape(CD, 6, D),
            spread(bias_grads[:HW].reshape(CD, 1, 6), D),
            spread(bias_grads[2 * HW :].reshape(CD, 1, 6), D),
        ],
        axis=1,
    )
    totals = jnp.sum(swap_experts(grads).astype(F32), axis=0)
    dealt = swap_seq(totals[:24].reshape(NS, 6, D))
    extra = jnp.sum(dealt[:, :, 3 * HW : 3 * HW + CD + 3], axis=0)
    whole_qkv = dealt[:, :, : 3 * HW].reshape(NS, 6, 3, HW).transpose(1, 2, 0, 3).reshape(6, 3 * D)
    return (
        mixed.reshape(tokens.shape),
        input_grad.astype(BF).reshape(tokens.shape),
        whole_qkv,
        totals[24:30],
        extra[:, :CD],
        extra[:, CD],
        extra[:, CD + 1],
        totals[30, :6],
        totals[31, :6],
        extra[:, CD + 2],
        inner_grad.astype(F32)[None],
        outer_grad.astype(F32)[None],
    )


def solution(mesh):
    return jax.shard_map(
        per_device,
        mesh=mesh,
        in_specs=(
            P("dp", ("seq", "ctx"), None),
            P(("seq", "ctx", "dp"), None),
            P(("seq", "ctx", "dp"), None),
            P(("seq", "ctx", "dp"), None),
            P(("seq", "ctx", "dp")),
            P(("seq", "ctx", "dp")),
            P(("seq", "ctx", "dp")),
            P(("seq", "ctx", "dp")),
            P(("seq", "ctx", "dp")),
            P(("ctx", "dp"), None, "seq"),
            P(("ctx", "dp"), None, "seq"),
            P("dp", ("seq", "ctx"), None),
            P("dp", ("seq", "ctx"), None),
        ),
        out_specs=(
            P("dp", ("seq", "ctx"), None),
            P("dp", ("seq", "ctx"), None),
            P(("seq", "ctx", "dp"), None),
            P(("seq", "ctx", "dp"), None),
            P(("seq", "ctx", "dp"), None),
            P(("seq", "ctx", "dp")),
            P(("seq", "ctx", "dp")),
            P(("seq", "ctx", "dp")),
            P(("seq", "ctx", "dp")),
            P(("seq", "ctx", "dp")),
            P(("ctx", "dp"), None, "seq"),
            P(("ctx", "dp"), None, "seq"),
        ),
        check_vma=False,
    )
```

```python
import functools

import jax
import jax.numpy as jnp
import numpy as np
from jax import lax
from jax.experimental import pallas as pl
from jax.experimental.pallas import tpu as pltpu
from jax.sharding import PartitionSpec as P

H = 12
HD = 64
TOPK = 2
D = 768
T = 128
NS = 4
HL = H // NS
HW = HL * HD
QR = NS * T
CD = 32
CAP = 9
SLOTS = 24
ROWS = CD * SLOTS
LINES = CD * CAP
LINES_ALL = 8 * 4 * CD
HALF = D // 2
PACK = 208

EPS = 1e-06
MASKED = -1e30
BF = jnp.bfloat16
F32 = jnp.float32

VMEM = pl.BlockSpec(memory_space=pltpu.VMEM)
SMEM = pl.BlockSpec(memory_space=pltpu.SMEM)


def dot(former, latter, former_dim, latter_dim):
    return lax.dot_general(
        former,
        latter,
        (((former_dim,), (latter_dim,)), ((), ())),
        preferred_element_type=F32,
    )


def params(**more):
    return pltpu.CompilerParams(vmem_limit_bytes=56 * 1024 * 1024, **more)


def jump(values, axis, steps):
    pairs = []
    for x in range(NS):
        for z in range(NS):
            for y in range(NS):
                for core in range(2):
                    far = {"x": x, "z": z, "y": y}
                    far[axis] += -steps if core else steps
                    there = (far["x"] % NS * NS + far["z"] % NS) * NS + far["y"] % NS
                    pairs.append((((x * NS + z) * NS + y) * 2 + core, there * 2 + core))
    return lax.ppermute(values, ("seq", "ctx", "dp"), pairs)


def collect(values, axis):
    return [values] + [jump(values, axis, k) for k in range(1, NS)]


def deliver(pieces, axis):
    return [pieces[0]] + [jump(pieces[k], axis, -k) for k in range(1, NS)]


def deliver_sum(pieces, axis, beside=()):
    middle = jump(pieces[2], axis, 1)
    first = jump(pieces[1], axis, -1)
    onward, beside = lax.optimization_barrier((pieces[3], tuple(beside)))
    third = jump((onward.astype(F32) + middle.astype(F32)).astype(BF), axis, 1)
    return (pieces[0], first, third), beside


def swap_experts(values):
    return lax.all_to_all(values, ("ctx", "dp"), split_axis=0, concat_axis=0, tiled=True)


def swap_seq(values):
    return lax.all_to_all(values, "seq", split_axis=0, concat_axis=0, tiled=True)


def swap_all(values):
    return lax.all_to_all(values, ("seq", "ctx", "dp"), split_axis=0, concat_axis=0, tiled=True)


def gather_seq(values, back):
    place = lax.axis_index("seq")
    whole = jnp.zeros((NS,) + values.shape, values.dtype)
    for k, piece in enumerate(collect(values, "x")):
        whole = lax.dynamic_update_slice(whole, piece[None], ((place + back * k) % NS, 0, 0))
    return whole


def tile_of(refs, rows, j):
    return jnp.concatenate([ref[rows, j * T : (j + 1) * T] for ref in refs], axis=1)


def causal_tile(place_ref):
    z, y, back = place_ref[0], place_ref[1], place_ref[2]
    k_index = lax.broadcasted_iota(jnp.int32, (QR, QR), 0)
    q_index = lax.broadcasted_iota(jnp.int32, (QR, QR), 1)
    k_place = z * QR + (((y + back * (k_index >> 7)) & 3) << 7) + (k_index & 127)
    q_place = (((z + back * (q_index >> 7)) & 3) << 9) + y * T + (q_index & 127)
    return k_place <= q_place


def split3(values):
    high = values.astype(BF).astype(F32)
    middle = (values - high).astype(BF).astype(F32)
    return high, middle, values - high - middle


def attend_kernel(place_ref, *refs):
    q_refs, kv_refs, o_refs = refs[0:4], refs[4:8], refs[8:12]
    lse_ref, bias_ref = refs[12], refs[13]
    bias_ref[...] = jnp.where(causal_tile(place_ref), 0.0, MASKED)

    def head(h, carry):
        rows = pl.ds(pl.multiple_of(h * HD, HD), HD)
        v_rows = pl.ds(pl.multiple_of(HW + h * HD, HD), HD)
        for j in range(NS):
            q_tile = tile_of(q_refs, rows, j)
            top = total = acc = None
            for jp in range(j + 1):
                k_tile = tile_of(kv_refs, rows, jp)
                v_tile = tile_of(kv_refs, v_rows, jp)
                scores = dot(k_tile, q_tile, 0, 0)
                if jp == j:
                    scores = jnp.where(bias_ref[...] < 0.0, MASKED, scores)
                here = jnp.max(scores, axis=0, keepdims=True)
                if jp == 0:
                    top = here
                    probs = jnp.exp(scores - top)
                    total = jnp.sum(probs, axis=0, keepdims=True)
                    acc = dot(v_tile, probs.astype(BF), 1, 0)
                else:
                    higher = jnp.maximum(top, here)
                    fade = jnp.exp(top - higher)
                    probs = jnp.exp(scores - higher)
                    total = total * fade + jnp.sum(probs, axis=0, keepdims=True)
                    acc = acc * fade + dot(v_tile, probs.astype(BF), 1, 0)
                    top = higher
            out = (acc / total).astype(BF)
            lse = top + jnp.log(total)
            for i in range(NS):
                o_refs[i][rows, j * T : (j + 1) * T] = out[:, i * T : (i + 1) * T]
                lse_ref[h, i : i + 1, j * T : (j + 1) * T] = lse[:, i * T : (i + 1) * T]
        return carry

    lax.fori_loop(0, HL, head, 0)
    for i in range(NS):
        logs = jnp.concatenate([lse_ref[h, i : i + 1, :] for h in range(HL)], axis=0)
        high, middle, low = split3(logs)
        rest = jnp.zeros((PACK - HW - 3 * HL, QR), F32)
        o_refs[i][HW:PACK, :] = jnp.concatenate([high, middle, low, rest], axis=0).astype(BF)


def attend(place, queries, keyvals):
    return pl.pallas_call(
        attend_kernel,
        out_shape=[jax.ShapeDtypeStruct((PACK, QR), BF)] * NS,
        in_specs=[SMEM] + [VMEM] * 8,
        out_specs=[VMEM] * NS,
        scratch_shapes=[pltpu.VMEM((HL, 8, QR), F32), pltpu.VMEM((QR, QR), F32)],
        compiler_params=params(),
        cost_estimate=pl.CostEstimate(
            flops=4 * 30 * QR * QR * HD, bytes_accessed=4 << 20, transcendentals=30 * QR * QR
        ),
        name="attend",
    )(place, *queries, *keyvals)


def lse_of(stats):
    return stats[0:HL] + stats[HL : 2 * HL] + stats[2 * HL : 3 * HL]


def block_at(place_ref, k, size):
    return pl.ds(pl.multiple_of(((place_ref[3] + place_ref[2] * k) & 3) * size, 64), size)


def lanes_at(place_ref, k):
    return pl.ds(pl.multiple_of(((place_ref[3] + place_ref[2] * k) & 3) * T, T), T)


def merge_kernel(place_ref, *refs):
    parts, o_ref, stat_ref, piece_refs = refs[0:4], refs[4], refs[5], refs[6:10]
    logs = [lse_of(part[HW:PACK, :].astype(F32)) for part in parts]
    top = functools.reduce(jnp.maximum, logs)
    lse = top + jnp.log(functools.reduce(jnp.add, [jnp.exp(log - top) for log in logs]))
    shares = [jnp.exp(log - lse) for log in logs]
    for h in range(HL):
        rows = slice(h * HD, (h + 1) * HD)
        o_ref[rows, :] = functools.reduce(
            jnp.add,
            [part[rows, :].astype(F32) * share[h : h + 1] for part, share in zip(parts, shares)],
        ).astype(BF)
    stat_ref[...] = jnp.concatenate([lse, jnp.zeros((8 - HL, QR), F32)], axis=0)
    for i in range(NS):
        piece_refs[i][...] = o_ref[:, lanes_at(place_ref, -i)]


def merge(place, parts):
    out = pl.pallas_call(
        merge_kernel,
        out_shape=[jax.ShapeDtypeStruct((HW, QR), BF), jax.ShapeDtypeStruct((8, QR), F32)]
        + [jax.ShapeDtypeStruct((HW, T), BF)] * NS,
        in_specs=[SMEM] + [VMEM] * 4,
        out_specs=[VMEM] * 6,
        compiler_params=params(),
        name="merge",
    )(place, *parts)
    return out[0], out[1], out[2:]


def grad_heads_kernel(place_ref, *refs):
    piece_refs, o_ref, lse_ref, out_ref = refs[0:4], refs[4], refs[5], refs[6]
    for i in range(NS):
        out_ref[0:HW, lanes_at(place_ref, -i)] = piece_refs[i][0:HW, :]
    product = out_ref[0:HW, :].astype(F32) * o_ref[...].astype(F32)
    delta = jnp.concatenate(
        [jnp.sum(product[h * HD : (h + 1) * HD], axis=0, keepdims=True) for h in range(HL)], axis=0
    )
    high, middle, low = split3(lse_ref[0:HL, :])
    d_high, d_middle, unused = split3(delta)
    rest = jnp.zeros((PACK - HW - 5 * HL, QR), F32)
    out_ref[HW:PACK, :] = jnp.concatenate(
        [high, middle, low, d_high, d_middle, rest], axis=0
    ).astype(BF)


def grad_heads(place, pieces, attended, lse):
    return pl.pallas_call(
        grad_heads_kernel,
        out_shape=jax.ShapeDtypeStruct((PACK, QR), BF),
        in_specs=[SMEM] + [VMEM] * 6,
        out_specs=VMEM,
        compiler_params=params(),
        name="grad_heads",
    )(place, *pieces, attended, lse)


def out_grad_kernel(*refs):
    pieces, others, third_ref, out_ref = refs[0:4], refs[4:8], refs[8], refs[9]
    grads = functools.reduce(
        jnp.add,
        [dot(other[...], piece[HW:, :], 1, 1) for piece, other in zip(pieces, others)],
    ).astype(BF)
    for block in range(2):
        rows = grads[block * HALF : (block + 1) * HALF]
        for part in range(3):
            out_ref[block * QR : (block + 1) * QR, part * HW : (part + 1) * HW] = dot(
                third_ref[part], rows, 1, 0
            ).astype(BF)


def out_grad_of(pieces, others):
    return pl.pallas_call(
        out_grad_kernel,
        out_shape=jax.ShapeDtypeStruct((LINES_ALL, 3 * HW), BF),
        in_specs=[VMEM] * 9,
        out_specs=VMEM,
        compiler_params=params(),
        cost_estimate=pl.CostEstimate(
            flops=4 * D * D * QR, bytes_accessed=4 << 20, transcendentals=0
        ),
        name="out_grad",
    )(*pieces, *others, jnp.asarray(room_thirds(), BF))


def finish_kernel(
    place_ref, q0, q1, q3, k0, k1, k3, qkv_ref, x_ref, room_in_ref, og_ref, extra_ref,
    room_ref, line_ref, lane_ref, p0, p1, p2, p3, out_ref, first_ref, tail_ref,
):
    def total(refs):
        return functools.reduce(jnp.add, [ref[...].astype(F32) for ref in refs]).astype(BF)

    grads = jnp.concatenate([total((q0, q1, q3)), total((k0, k1, k3))], axis=0)
    first = dot(grads, qkv_ref[...], 0, 1)
    first_ref[...] = first.astype(BF)
    for k, piece in enumerate((p0, p1, p2, p3)):
        piece[...] = first_ref[block_at(place_ref, k, T), :]
    rows = x_ref[...].astype(F32)
    unit, factor = norm_two(rows)
    gain = jnp.sum(first * unit, axis=0, keepdims=True)
    main = dot(room_in_ref[...], grads, 1, 1) + og_ref[...].astype(F32)
    out_ref[:, 0:QR] = main[:, 0:QR].astype(BF)
    at_gain = lax.broadcasted_iota(jnp.int32, (64, D), 0) == CD
    gains = jnp.where(at_gain, gain, 0.0).astype(BF)
    for block in range(2):
        span = slice(block * QR, (block + 1) * QR)
        extra = extra_ref[span, :].astype(F32) + dot(
            room_ref[...], gains[:, block * HALF : (block + 1) * HALF], 1, 1
        )
        tail_ref[span, :] = jnp.concatenate([main[span, QR:], extra], axis=1)
    sums = jnp.sum(grads.astype(F32), axis=1, keepdims=True)
    biases = sums[0:HW] * lane_ref[0] + sums[2 * HW :] * lane_ref[1]
    own = pl.ds(pl.multiple_of(place_ref[3] * 256, 256), 256)
    tail_ref[own, :] += jnp.concatenate(
        [jnp.zeros((256, 64), F32), dot(line_ref[...], biases.astype(BF), 1, 0)], axis=1
    )
    out_ref[:, QR:] = tail_ref[...].astype(BF)


def finish(place, queries, keyvals, qkv, stream, room_in, out_grad, extra):
    lines, lanes = bias_constants()
    out = pl.pallas_call(
        finish_kernel,
        out_shape=[jax.ShapeDtypeStruct((T, D), BF)] * NS
        + [jax.ShapeDtypeStruct((LINES_ALL, 640), BF)],
        in_specs=[SMEM] + [VMEM] * 14,
        out_specs=[VMEM] * 5,
        scratch_shapes=[pltpu.VMEM((QR, D), BF), pltpu.VMEM((LINES_ALL, 128), F32)],
        compiler_params=params(),
        name="finish",
    )(
        place, *queries, *keyvals, qkv, stream, room_in, out_grad, extra,
        jnp.asarray(room_block(), BF), jnp.asarray(lines, BF), jnp.asarray(lanes, F32),
    )
    return list(out[0:4]), out[4]


def attend_back_kernel(place_ref, *refs):
    q_refs, kv_refs, do_refs = refs[0:4], refs[4:8], refs[8:12]
    dq_refs, dkv_refs = refs[12:16], refs[16:20]
    lse_ref, delta_ref, bias_ref, dq_ref = refs[20:24]
    bias_ref[...] = jnp.where(causal_tile(place_ref), 0.0, MASKED)
    for i in range(NS):
        stats = do_refs[i][HW:PACK, :].astype(F32)
        logs = lse_of(stats)
        deltas = stats[3 * HL : 4 * HL] + stats[4 * HL : 5 * HL]
        for h in range(HL):
            lse_ref[h, i : i + 1, :] = logs[h : h + 1]
            delta_ref[h, i : i + 1, :] = deltas[h : h + 1]

    def head(h, carry):
        rows = pl.ds(pl.multiple_of(h * HD, HD), HD)
        v_rows = pl.ds(pl.multiple_of(HW + h * HD, HD), HD)

        def stat(ref, j):
            return jnp.concatenate(
                [ref[h, i : i + 1, j * T : (j + 1) * T] for i in range(NS)], axis=1
            )

        for jp in range(NS):
            k_tile = tile_of(kv_refs, rows, jp)
            v_tile = tile_of(kv_refs, v_rows, jp)
            dk = dv = None
            for j in range(jp, NS):
                q_tile = tile_of(q_refs, rows, j)
                do_tile = tile_of(do_refs, rows, j)
                scores = dot(k_tile, q_tile, 0, 0)
                if jp == j:
                    scores = jnp.where(bias_ref[...] < 0.0, MASKED, scores)
                probs = jnp.exp(scores - stat(lse_ref, j))
                slopes = dot(v_tile, do_tile, 0, 0)
                ds = (probs * (slopes - stat(delta_ref, j))).astype(BF)
                dv_here = dot(do_tile, probs.astype(BF), 1, 1)
                dk_here = dot(q_tile, ds, 1, 1)
                dq_here = dot(k_tile, ds, 1, 0)
                dv = dv_here if dv is None else dv + dv_here
                dk = dk_here if dk is None else dk + dk_here
                if jp == 0:
                    dq_ref[j] = dq_here
                else:
                    dq_ref[j] += dq_here
            dk, dv = dk.astype(BF), dv.astype(BF)
            for i in range(NS):
                dkv_refs[i][rows, jp * T : (jp + 1) * T] = dk[:, i * T : (i + 1) * T]
                dkv_refs[i][v_rows, jp * T : (jp + 1) * T] = dv[:, i * T : (i + 1) * T]
        for j in range(NS):
            dq = (dq_ref[j] * HD ** (-0.5)).astype(BF)
            for i in range(NS):
                dq_refs[i][rows, j * T : (j + 1) * T] = dq[:, i * T : (i + 1) * T]
        return carry

    lax.fori_loop(0, HL, head, 0)


def attend_back(place, queries, keyvals, grads):
    out = pl.pallas_call(
        attend_back_kernel,
        out_shape=[jax.ShapeDtypeStruct((HW, QR), BF)] * NS
        + [jax.ShapeDtypeStruct((2 * HW, QR), BF)] * NS,
        in_specs=[SMEM] + [VMEM] * 12,
        out_specs=[VMEM] * 8,
        scratch_shapes=[
            pltpu.VMEM((HL, 8, QR), F32),
            pltpu.VMEM((HL, 8, QR), F32),
            pltpu.VMEM((QR, QR), F32),
            pltpu.VMEM((NS, HD, QR), F32),
        ],
        compiler_params=params(),
        cost_estimate=pl.CostEstimate(
            flops=10 * 30 * QR * QR * HD, bytes_accessed=6 << 20, transcendentals=30 * QR * QR
        ),
        name="attend_back",
    )(place, *queries, *keyvals, *grads)
    return out[0:NS], out[NS:]


def pick_rows(target, offset):
    lines = lax.broadcasted_iota(jnp.int32, (T, ROWS), 1)
    return (lines == target + offset).astype(F32).astype(BF)


def norm_two(middle):
    factor = lax.rsqrt(jnp.mean(middle * middle, axis=-1, keepdims=True) + EPS)
    return middle * factor, factor


def route_kernel(
    place_ref, x_ref, small_ref, router_ref, ids_ref, cot_ref, o0, o1, o2, o3, w0, w1, w2, w3,
    out_ref, m_ref, a_ref, gate_ref, target_ref, o_ref, w_ref,
):
    for k, (o_piece, w_piece) in enumerate(((o0, w0), (o1, w1), (o2, w2), (o3, w3))):
        o_ref[block_at(place_ref, k, HW), :] = o_piece[...]
        w_ref[block_at(place_ref, k, HW), :] = w_piece[...]
    branch = dot(o_ref[...], w_ref[...], 0, 1)
    middle = x_ref[...].astype(F32) + branch + small_ref[2:3, :]
    unit, factor = norm_two(middle)
    second = (unit * small_ref[1:2, :]).astype(BF)
    logits = dot(second, router_ref[...], 1, 0)
    cols = lax.broadcasted_iota(jnp.int32, (T, CD), 1)
    named = [(ids_ref[:, k : k + 1] == cols).astype(F32) for k in range(TOPK)]
    earlier = lax.broadcasted_iota(jnp.int32, (T, T), 1) < lax.broadcasted_iota(
        jnp.int32, (T, T), 0
    )
    counts = dot(earlier.astype(F32).astype(BF), (named[0] + named[1]).astype(BF), 1, 0)
    chosen = [jnp.sum(name * logits, axis=1, keepdims=True) for name in named]
    top = jnp.maximum(chosen[0], chosen[1])
    raw = [jnp.exp(value - top) for value in chosen]
    gates = [value / (raw[0] + raw[1]) for value in raw]
    slots = [jnp.sum(name * counts, axis=1, keepdims=True).astype(jnp.int32) for name in named]
    targets = [ids_ref[:, k : k + 1] * SLOTS + slots[k] for k in range(TOPK)]
    grads = cot_ref[...].astype(F32)
    places = jnp.concatenate(
        [pick_rows(targets[0], 0) + pick_rows(targets[1], 0)]
        + [pick_rows(targets[k], CAP) for k in range(TOPK)],
        axis=0,
    )
    values = jnp.concatenate([second] + [(gates[k] * grads).astype(BF) for k in range(TOPK)], axis=0)
    out_ref[...] = dot(places, values, 0, 0).astype(BF)
    m_ref[...] = middle
    a_ref[...] = second
    gate_ref[...] = jnp.concatenate(gates, axis=1)
    target_ref[...] = jnp.concatenate(targets, axis=1)


def route(place, rows, small, router, ids, cotangent, pieces, out_weights):
    return pl.pallas_call(
        route_kernel,
        out_shape=[
            jax.ShapeDtypeStruct((ROWS, D), BF),
            jax.ShapeDtypeStruct((T, D), F32),
            jax.ShapeDtypeStruct((T, D), BF),
            jax.ShapeDtypeStruct((T, TOPK), F32),
            jax.ShapeDtypeStruct((T, TOPK), jnp.int32),
            jax.ShapeDtypeStruct((D, T), BF),
            jax.ShapeDtypeStruct((D, D), BF),
        ],
        in_specs=[SMEM] + [VMEM] * 13,
        out_specs=[VMEM] * 7,
        compiler_params=params(),
        name="route",
    )(place, rows, small, router, ids, cotangent, *pieces, *out_weights)


GELU_A = float(np.sqrt(2.0 / np.pi))
GELU_B = 0.044715


def expert_kernel(
    rows_ref, pick_ref, win_ref, wout_ref, out_ref, gin_ref, gout_ref,
    a_ref, dy_ref, at_ref, dyt_ref, y_ref, da_ref,
):
    step = pl.program_id(0)

    @pl.when(step == 0)
    def first():
        both = dot(pick_ref[...], rows_ref[...], 1, 0).astype(BF)
        a_ref[...] = both[0:LINES]
        dy_ref[...] = both[LINES:]
        turned = dot(rows_ref[...], pick_ref[...], 0, 1).astype(BF)
        at_ref[...] = turned[:, 0:LINES]
        dyt_ref[...] = turned[:, LINES:]

    rows, grads = a_ref[...], dy_ref[...]
    inner, outer = win_ref[0], wout_ref[0]
    pre = dot(rows, inner, 1, 0)
    square = pre * pre
    bent = jnp.tanh(GELU_A * pre * (1.0 + GELU_B * square))
    act = (0.5 * pre * (1.0 + bent)).astype(BF)
    slope = 0.5 * (1.0 + bent) + 0.5 * pre * (1.0 - bent * bent) * (
        GELU_A * (1.0 + 3.0 * GELU_B * square)
    )
    pre_grad = (dot(grads, outer, 1, 0) * slope).astype(BF)
    made = dot(act, outer, 1, 1)
    back = dot(pre_grad, inner, 1, 1)
    gin_ref[0] = dot(at_ref[...], pre_grad, 1, 0).astype(BF)
    gout_ref[0] = dot(dyt_ref[...], act, 1, 0).astype(BF)

    @pl.when(step == 0)
    def start():
        y_ref[...] = made
        da_ref[...] = back

    @pl.when(step > 0)
    def more():
        y_ref[...] += made
        da_ref[...] += back

    @pl.when(step == pl.num_programs(0) - 1)
    def last():
        both = jnp.concatenate([y_ref[...].astype(BF), da_ref[...].astype(BF)], axis=0)
        out_ref[...] = dot(pick_ref[...], both, 0, 0).astype(BF)


def widen_kernel(in_ref, out_ref):
    out_ref[...] = in_ref[...].astype(F32)


def widen(values):
    rows, width = values.shape
    spec = pl.BlockSpec((rows // 4, width), lambda i: (i, 0))
    return pl.pallas_call(
        widen_kernel,
        grid=(4,),
        out_shape=jax.ShapeDtypeStruct(values.shape, F32),
        in_specs=[spec],
        out_specs=spec,
        cost_estimate=pl.CostEstimate(
            flops=rows * width, bytes_accessed=6 * rows * width, transcendentals=0
        ),
        name="widen",
    )(values)


def expert_pick():
    lines = np.arange(LINES)
    pick = np.zeros((2 * LINES, ROWS), np.float32)
    pick[lines, lines // CAP * SLOTS + lines % CAP] = 1.0
    pick[LINES + lines, lines // CAP * SLOTS + CAP + lines % CAP] = 1.0
    return pick


def expert(rows, inner, outer):
    tile = 768
    halves = D // tile

    def weight_spec():
        return pl.BlockSpec((1, D, tile), lambda i: (i // halves, 0, i % halves))

    def whole(*shape):
        return pl.BlockSpec(shape, lambda i: (0, 0))

    return pl.pallas_call(
        expert_kernel,
        grid=(NS * halves,),
        out_shape=[
            jax.ShapeDtypeStruct((ROWS, D), BF),
            jax.ShapeDtypeStruct((NS, D, D), BF),
            jax.ShapeDtypeStruct((NS, D, D), BF),
        ],
        in_specs=[whole(ROWS, D), whole(2 * LINES, ROWS), weight_spec(), weight_spec()],
        out_specs=[whole(ROWS, D), weight_spec(), weight_spec()],
        scratch_shapes=[
            pltpu.VMEM((LINES, D), BF),
            pltpu.VMEM((LINES, D), BF),
            pltpu.VMEM((D, LINES), BF),
            pltpu.VMEM((D, LINES), BF),
            pltpu.VMEM((LINES, D), F32),
            pltpu.VMEM((LINES, D), F32),
        ],
        compiler_params=params(dimension_semantics=("arbitrary",)),
        cost_estimate=pl.CostEstimate(
            flops=12 * LINES * D * 4 * D, bytes_accessed=20 << 20, transcendentals=LINES * 4 * D
        ),
        name="expert",
    )(rows, jnp.asarray(expert_pick(), BF), inner, outer)


def settle_kernel(
    place_ref, back_ref, m_ref, a_ref, gate_ref, target_ref, ids_ref, cot_ref, small_ref, router_ref,
    w_ref, mixed_ref, db_ref, dm_ref, rg_ref, sums_ref, d0, d1, d2, d3, turn_ref,
):
    back = back_ref[...]
    targets = [target_ref[:, k : k + 1] for k in range(TOPK)]
    picked = [dot(pick_rows(target, 0), back, 1, 0) for target in targets]
    returned = dot(pick_rows(targets[0], CAP) + pick_rows(targets[1], CAP), back, 1, 0)
    middle = m_ref[...]
    grads = cot_ref[...].astype(F32)
    gates = [gate_ref[:, k : k + 1] for k in range(TOPK)]
    mixed_ref[...] = (middle + gates[0] * picked[0] + gates[1] * picked[1]).astype(BF)
    gate_grads = [jnp.sum(grads * value, axis=1, keepdims=True) for value in picked]
    mean = gates[0] * gate_grads[0] + gates[1] * gate_grads[1]
    cols = lax.broadcasted_iota(jnp.int32, (T, CD), 1)
    logit_grad = functools.reduce(
        jnp.add,
        [
            jnp.where(ids_ref[:, k : k + 1] == cols, gates[k] * (gate_grads[k] - mean), 0.0)
            for k in range(TOPK)
        ],
    ).astype(BF)
    rg_ref[...] = dot(a_ref[...], logit_grad, 0, 0)
    second_grad = dot(logit_grad, router_ref[...], 1, 1) + returned
    unit, factor = norm_two(middle)
    weighted = second_grad * small_ref[1:2, :]
    whole = grads + factor * (weighted - unit * jnp.mean(weighted * unit, axis=-1, keepdims=True))
    dm_ref[...] = whole
    rounded = whole.astype(BF)
    db_ref[...] = rounded
    turn_ref[0] = dot(rounded, w_ref[...], 1, 0).T.astype(BF)
    turn_ref[1] = rounded.astype(F32).T.astype(BF)
    for k, d_ref in enumerate((d0, d1, d2, d3)):
        d_ref[0:HW, :] = turn_ref[0, block_at(place_ref, k, HW), :]
        d_ref[HW:, :] = turn_ref[1, block_at(place_ref, k, HW), :]
    sums_ref[...] = jnp.concatenate(
        [
            jnp.sum(second_grad * unit, axis=0, keepdims=True),
            jnp.sum(rounded.astype(F32), axis=0, keepdims=True),
            jnp.zeros((6, D), F32),
        ],
        axis=0,
    )


def settle(place, back, middle, second, gates, targets, ids, cotangent, small, router, weight):
    out = pl.pallas_call(
        settle_kernel,
        out_shape=[
            jax.ShapeDtypeStruct((T, D), BF),
            jax.ShapeDtypeStruct((T, D), BF),
            jax.ShapeDtypeStruct((T, D), F32),
            jax.ShapeDtypeStruct((D, CD), F32),
            jax.ShapeDtypeStruct((8, D), F32),
        ]
        + [jax.ShapeDtypeStruct((2 * HW, T), BF)] * NS,
        in_specs=[SMEM] + [VMEM] * 10,
        out_specs=[VMEM] * 9,
        scratch_shapes=[pltpu.VMEM((2, D, T), BF)],
        compiler_params=params(),
        name="settle",
    )(place, back, middle, second, gates, targets, ids, cotangent, small, router, weight)
    return out[0:5], out[5:9]


def arrival_constants():
    rows = np.zeros((D, LINES_ALL), np.float32)
    thirds = np.zeros((3, LINES_ALL, D), np.float32)
    for g in range(D):
        n, i = divmod(g, 6)
        start = (n % CD * NS + n // CD) * 8
        rows[g, start + i] = 1.0
        thirds[i % 3, start + 6 + i // 3, g] = 1.0
    return rows, thirds


def room_block():
    rows = np.zeros((QR, HALF), np.float32)
    for g in range(HALF):
        rows[g // 6 * 8 + g % 6, g] = 1.0
    return rows


def room_thirds():
    thirds = np.zeros((3, QR, HALF), np.float32)
    for g in range(HALF):
        n, i = divmod(g, 6)
        thirds[i % 3, n * 8 + 6 + i // 3, g] = 1.0
    return thirds


def bias_constants():
    lines = np.zeros((256, HW), np.float32)
    lanes = np.zeros((2, HW, 64), np.float32)
    for r in range(HW):
        n, i = divmod(r, 6)
        lines[n * 8 + 6, r] = 1.0
        lanes[0, r, CD + 3 + i] = 1.0
        lanes[1, r, CD + 9 + i] = 1.0
    return lines, lanes


def spread(rows, width):
    return jnp.pad(rows, [(0, 0)] * (rows.ndim - 1) + [(0, width - rows.shape[-1])])


def per_device(
    tokens,
    qkv_weight,
    out_weight,
    router_weight,
    attn_gain,
    ffn_gain,
    query_bias,
    value_bias,
    out_bias,
    expert_in,
    expert_out,
    expert_ids,
    cotangent,
):
    rows_at, thirds_at = [jnp.asarray(value, BF) for value in arrival_constants()]
    ctx, seq = lax.axis_index("ctx"), lax.axis_index("seq")
    back = 2 * lax.axis_index("dp") - 1
    place = jnp.stack([ctx // NS, ctx % NS, back, seq]).astype(jnp.int32)
    mine = (jnp.arange(NS) == seq).astype(BF)
    rows = tokens.reshape(T, D)
    ids = expert_ids.reshape(T, TOPK)
    cot = cotangent.reshape(T, D)

    inner = lax.all_gather(expert_in[0], "seq", axis=0, tiled=False)
    outer = lax.all_gather(expert_out[0], "seq", axis=0, tiled=False)

    columns = qkv_weight.reshape(6, 3, NS, HW).transpose(2, 0, 1, 3).reshape(NS, 6, 3 * HW)
    extras = jnp.concatenate(
        [router_weight, attn_gain[:, None], ffn_gain[:, None], out_bias[:, None]], axis=1
    )
    upper = jnp.concatenate(
        [columns, jnp.broadcast_to(spread(extras, 64)[None], (NS, 6, 64))], axis=2
    )
    quarters = out_weight.reshape(2, 3, NS, HW).transpose(2, 0, 1, 3).reshape(NS, 2, 3 * HW)
    biases = jnp.concatenate([query_bias, value_bias])[None, None] * mine[:, None, None]
    corner = jnp.pad(biases, ((0, 0), (0, 1), (0, 52)))
    lower = jnp.concatenate([quarters, corner], axis=2)
    sent = jnp.concatenate([upper, lower], axis=1)
    sent = swap_seq(sent).reshape(1, NS * 8, 640)
    arrived = swap_experts(jnp.broadcast_to(sent, (CD, NS * 8, 640)))
    weights = arrived.reshape(LINES_ALL, 640)
    sorted_weights = dot(rows_at, weights, 1, 0).astype(BF)
    qkv = sorted_weights[:, : 3 * HW]
    router = sorted_weights[:, 3 * HW : 3 * HW + CD]
    small = dot(weights[:, 608:616], rows_at, 0, 1)
    own_bias = jnp.sum(
        arrived.reshape(CD, NS, 8, 640)[:, :, 6, 576:588].astype(F32), axis=1
    )
    bias = jnp.concatenate(
        [own_bias[:, :6].reshape(HW), jnp.zeros((HW,), F32), own_bias[:, 6:].reshape(HW)]
    )

    stream = gather_seq(rows, back).reshape(QR, D)
    first_in = (norm_two(stream.astype(F32))[0] * small[0:1]).astype(BF)
    projected = (dot(qkv, first_in, 0, 1) + bias[:, None]).astype(BF)
    keyvals = collect(projected[HW:], "y")
    queries = collect(projected[:HW] * jnp.asarray(HD ** (-0.5), BF), "z")
    out_piece = sum(
        dot(weights[:, part * HW : (part + 1) * HW], thirds_at[part], 0, 0) for part in range(3)
    ).astype(BF)
    out_weights = collect(out_piece, "x")
    partial = attend(place, queries, keyvals)
    partial, out_weights = lax.optimization_barrier((partial, out_weights))
    attended, lse, pieces = merge(place, deliver(partial, "z"))
    heads = [pieces[0]] + [jump(pieces[k], "x", k) for k in range(1, NS)]

    outgoing, middle, second, gates, targets, whole_heads, weight = route(
        place, rows, small, router, ids, cot, heads, out_weights
    )
    received = swap_experts(outgoing.reshape(CD, SLOTS, D)).reshape(ROWS, D)
    others = deliver([whole_heads] * NS, "x")
    made, inner_grad, outer_grad = expert(received, inner, outer)
    returned = swap_experts(made.reshape(CD, SLOTS, D)).reshape(ROWS, D)
    inner_grad = lax.psum_scatter(inner_grad, "seq", scatter_dimension=0, tiled=False)
    outer_grad = lax.psum_scatter(outer_grad, "seq", scatter_dimension=0, tiled=False)
    (mixed, branch_grad, middle_grad, router_grad, sums), head_pieces = settle(
        place, returned, middle, second, gates, targets, ids, cot, small, router, weight
    )

    head_pieces = deliver(head_pieces, "x")
    heads_grad = collect(grad_heads(place, head_pieces, attended, lse), "z")
    query_parts, keyval_parts = attend_back(place, queries, keyvals, heads_grad)
    out_grad = out_grad_of(head_pieces, others)
    room = jnp.asarray(room_block(), BF)
    room_in = jnp.concatenate([dot(room, half, 1, 1) for half in jnp.split(first_in, 2, axis=1)])
    after = jnp.concatenate(
        [router_grad.astype(BF), jnp.zeros((D, 1), BF), sums[0:2].T.astype(BF)], axis=1
    )
    extra = spread(jnp.concatenate([dot(room, half, 1, 0) for half in jnp.split(after, 2)]), 64)
    keyval_grads, (out_grad, room_in, extra, inner_grad) = deliver_sum(
        keyval_parts, "y", (out_grad, room_in.astype(BF), extra.astype(BF), widen(inner_grad))
    )
    query_grads, unused = deliver_sum(query_parts, "z")
    parts, grads = finish(
        place, query_grads, keyval_grads, qkv, stream, room_in, out_grad, extra
    )
    mine_grad = sum(part.astype(F32) for part in deliver(parts, "x"))
    own_unit, own_factor = norm_two(rows.astype(F32))
    weighted = mine_grad * small[0:1]
    input_grad = middle_grad + own_factor * (
        weighted - own_unit * jnp.mean(weighted * own_unit, axis=-1, keepdims=True)
    )

    dealt = swap_all(grads.reshape(NS * CD, 8, 640)).reshape(NS, CD, 8, 640)
    totals = jnp.sum(dealt.astype(F32), axis=1)
    extra = jnp.sum(totals[:, :, 3 * HW :], axis=0)
    whole_qkv = (
        totals[:, :6, : 3 * HW].reshape(NS, 6, 3, HW).transpose(1, 2, 0, 3).reshape(6, 3 * D)
    )
    whole_out = totals[:, 6:, : 3 * HW].reshape(NS, 2, 3, HW).transpose(1, 2, 0, 3).reshape(6, D)
    return (
        mixed.reshape(tokens.shape),
        input_grad.astype(BF).reshape(tokens.shape),
        whole_qkv,
        whole_out,
        extra[:6, :CD],
        extra[:6, CD],
        extra[:6, CD + 1],
        extra[6, CD + 3 : CD + 9],
        extra[6, CD + 9 : CD + 15],
        extra[:6, CD + 2],
        inner_grad[None],
        widen(outer_grad)[None],
    )


def solution(mesh):
    return jax.shard_map(
        per_device,
        mesh=mesh,
        in_specs=(
            P("dp", ("seq", "ctx"), None),
            P(("seq", "ctx", "dp"), None),
            P(("seq", "ctx", "dp"), None),
            P(("seq", "ctx", "dp"), None),
            P(("seq", "ctx", "dp")),
            P(("seq", "ctx", "dp")),
            P(("seq", "ctx", "dp")),
            P(("seq", "ctx", "dp")),
            P(("seq", "ctx", "dp")),
            P(("ctx", "dp"), None, "seq"),
            P(("ctx", "dp"), None, "seq"),
            P("dp", ("seq", "ctx"), None),
            P("dp", ("seq", "ctx"), None),
        ),
        out_specs=(
            P("dp", ("seq", "ctx"), None),
            P("dp", ("seq", "ctx"), None),
            P(("seq", "ctx", "dp"), None),
            P(("seq", "ctx", "dp"), None),
            P(("seq", "ctx", "dp"), None),
            P(("seq", "ctx", "dp")),
            P(("seq", "ctx", "dp")),
            P(("seq", "ctx", "dp")),
            P(("seq", "ctx", "dp")),
            P(("seq", "ctx", "dp")),
            P(("ctx", "dp"), None, "seq"),
            P(("ctx", "dp"), None, "seq"),
        ),
        check_vma=False,
    )
```

```python
import functools

import jax
import jax.numpy as jnp
import numpy as np
from jax import lax
from jax.experimental import pallas as pl
from jax.experimental.pallas import tpu as pltpu
from jax.sharding import PartitionSpec as P

H = 12
HD = 64
TOPK = 2
D = 768
T = 128
NS = 4
HL = H // NS
HW = HL * HD
QR = NS * T
CD = 32
CAP = 9
SLOTS = 24
ROWS = CD * SLOTS
LINES = CD * CAP
LINES_ALL = 8 * 4 * CD
HALF = D // 2
PACK = 208

ALL = ("seq", "z", "y", "dp")

EPS = 1e-06
MASKED = -1e30
BF = jnp.bfloat16
F32 = jnp.float32

VMEM = pl.BlockSpec(memory_space=pltpu.VMEM)
SMEM = pl.BlockSpec(memory_space=pltpu.SMEM)


def dot(former, latter, former_dim, latter_dim):
    return lax.dot_general(
        former,
        latter,
        (((former_dim,), (latter_dim,)), ((), ())),
        preferred_element_type=F32,
    )


def params(**more):
    return pltpu.CompilerParams(vmem_limit_bytes=56 * 1024 * 1024, **more)


def jump(values, axis, steps):
    pairs = []
    for x in range(NS):
        for z in range(NS):
            for y in range(NS):
                for core in range(2):
                    far = {"x": x, "z": z, "y": y}
                    far[axis] += -steps if core else steps
                    there = (far["x"] % NS * NS + far["z"] % NS) * NS + far["y"] % NS
                    pairs.append((((x * NS + z) * NS + y) * 2 + core, there * 2 + core))
    return lax.ppermute(values, ALL, pairs)


def collect(values, axis):
    return [values] + [jump(values, axis, k) for k in range(1, NS)]


def deliver(pieces, axis):
    return [pieces[0]] + [jump(pieces[k], axis, -k) for k in range(1, NS)]


def deliver_sum(pieces, axis, beside=()):
    middle = jump(pieces[2], axis, 1)
    first = jump(pieces[1], axis, -1)
    onward, beside = lax.optimization_barrier((pieces[3], tuple(beside)))
    third = jump((onward.astype(F32) + middle.astype(F32)).astype(BF), axis, 1)
    return (pieces[0], first, third), beside


def swap_experts(values):
    return lax.all_to_all(values, ALL[1:], split_axis=0, concat_axis=0, tiled=True)


def swap_plane(values):
    return lax.all_to_all(values, ("seq", "z"), split_axis=0, concat_axis=0, tiled=True)


def swap_seq(values):
    return lax.all_to_all(values, "seq", split_axis=0, concat_axis=0, tiled=True)


def swap_all(values):
    return lax.all_to_all(values, ALL, split_axis=0, concat_axis=0, tiled=True)


def gather_seq(values, back):
    place = lax.axis_index("seq")
    whole = jnp.zeros((NS,) + values.shape, values.dtype)
    for k, piece in enumerate(collect(values, "x")):
        whole = lax.dynamic_update_slice(whole, piece[None], ((place + back * k) % NS, 0, 0))
    return whole


def tile_of(refs, rows, j):
    return jnp.concatenate([ref[rows, j * T : (j + 1) * T] for ref in refs], axis=1)


def causal_tile(place_ref):
    z, y, back = place_ref[0], place_ref[1], place_ref[2]
    k_index = lax.broadcasted_iota(jnp.int32, (QR, QR), 0)
    q_index = lax.broadcasted_iota(jnp.int32, (QR, QR), 1)
    k_place = z * QR + (((y + back * (k_index >> 7)) & 3) << 7) + (k_index & 127)
    q_place = (((z + back * (q_index >> 7)) & 3) << 9) + y * T + (q_index & 127)
    return k_place <= q_place


def split3(values):
    high = values.astype(BF).astype(F32)
    middle = (values - high).astype(BF).astype(F32)
    return high, middle, values - high - middle


def z_at(place_ref, k):
    return (place_ref[0] + place_ref[2] * k) & 3


def attend_kernel(place_ref, *refs):
    q_refs, kv_refs, o_refs, lse_ref, bias_ref = refs[0:4], refs[4:8], refs[8:12], refs[12], refs[13]
    bias_ref[...] = jnp.where(causal_tile(place_ref), 0.0, MASKED)
    work = [(j, jp) for j in range(NS) for jp in range(j + 1)]

    def head(h, carry):
        rows = pl.ds(pl.multiple_of(h * HD, HD), HD)
        v_rows = pl.ds(pl.multiple_of(HW + h * HD, HD), HD)
        k_tiles = [tile_of(kv_refs, rows, jp) for jp in range(NS)]
        v_tiles = [tile_of(kv_refs, v_rows, jp) for jp in range(NS)]

        def scores_of(j, jp):
            scores = dot(k_tiles[jp], tile_of(q_refs, rows, j), 0, 0)
            return jnp.where(bias_ref[...] < 0.0, MASKED, scores) if jp == j else scores

        following = scores_of(*work[0])
        for n, (j, jp) in enumerate(work):
            scores = following
            if n + 1 < len(work):
                following = scores_of(*work[n + 1])
            here = jnp.max(scores, axis=0, keepdims=True)
            if jp == 0:
                top = here
                probs = jnp.exp(scores - top)
                total = jnp.sum(probs, axis=0, keepdims=True)
                acc = dot(v_tiles[jp], probs.astype(BF), 1, 0)
            else:
                higher = jnp.maximum(top, here)
                fade = jnp.exp(top - higher)
                probs = jnp.exp(scores - higher)
                total = total * fade + jnp.sum(probs, axis=0, keepdims=True)
                acc = acc * fade + dot(v_tiles[jp], probs.astype(BF), 1, 0)
                top = higher
            if jp == j:
                out = (acc / total).astype(BF)
                lse = top + jnp.log(total)
                for k in range(NS):
                    o_refs[k][rows, j * T : (j + 1) * T] = out[:, k * T : (k + 1) * T]
                    lse_ref[h, k : k + 1, j * T : (j + 1) * T] = lse[:, k * T : (k + 1) * T]
        return carry

    lax.fori_loop(0, HL, head, 0)
    for k in range(NS):
        logs = jnp.concatenate([lse_ref[h, k : k + 1, :] for h in range(HL)], axis=0)
        o_refs[k][HW:PACK, :] = log_rows(logs)


def log_rows(logs):
    rest = jnp.zeros((PACK - HW - 3 * HL, logs.shape[1]), F32)
    return jnp.concatenate([*split3(logs), rest], axis=0).astype(BF)


def attend(place, queries, keyvals):
    return pl.pallas_call(
        attend_kernel,
        out_shape=[jax.ShapeDtypeStruct((PACK, QR), BF)] * NS,
        in_specs=[SMEM] + [VMEM] * 8,
        out_specs=[VMEM] * NS,
        scratch_shapes=[pltpu.VMEM((HL, 8, QR), F32), pltpu.VMEM((QR, QR), F32)],
        compiler_params=params(),
        cost_estimate=pl.CostEstimate(
            flops=4 * 30 * QR * QR * HD, bytes_accessed=4 << 20, transcendentals=30 * QR * QR
        ),
        name="attend",
    )(place, *queries, *keyvals)


def lse_of(stats):
    return stats[0:HL] + stats[HL : 2 * HL] + stats[2 * HL : 3 * HL]


def block_at(place_ref, k, size):
    return pl.ds(pl.multiple_of(((place_ref[3] + place_ref[2] * k) & 3) * size, 64), size)


def merge_kernel(place_ref, *refs):
    parts, piece_refs, o_ref = refs[0:4], refs[4:8], refs[8]
    logs = [lse_of(part[HW:PACK, :].astype(F32)) for part in parts]
    top = functools.reduce(jnp.maximum, logs)
    lse = top + jnp.log(functools.reduce(jnp.add, [jnp.exp(log - top) for log in logs]))
    shares = [jnp.exp(log - lse) for log in logs]
    for h in range(HL):
        rows = slice(h * HD, (h + 1) * HD)
        o_ref[rows, :] = functools.reduce(
            jnp.add,
            [part[rows, :].astype(F32) * share[h : h + 1] for part, share in zip(parts, shares)],
        ).astype(BF)
    o_ref[HW:PACK, :] = log_rows(lse)
    for k, piece in enumerate(piece_refs):
        block = (place_ref[3] - place_ref[2] * k) & 3
        piece[...] = o_ref[:, pl.ds(pl.multiple_of(block * T, T), T)]


def merge(place, parts):
    return pl.pallas_call(
        merge_kernel,
        out_shape=[jax.ShapeDtypeStruct((PACK, T), BF)] * NS,
        in_specs=[SMEM] + [VMEM] * 4,
        out_specs=[VMEM] * NS,
        scratch_shapes=[pltpu.VMEM((PACK, QR), BF)],
        compiler_params=params(),
        name="merge",
    )(place, *parts)


def out_grad_kernel(*refs):
    pieces, others, third_ref, out_ref = refs[0:4], refs[4:8], refs[8], refs[9]
    grads = functools.reduce(
        jnp.add,
        [dot(other[...], piece[...], 1, 1) for piece, other in zip(pieces, others)],
    ).astype(BF)
    for block in range(2):
        rows = grads[block * HALF : (block + 1) * HALF]
        for part in range(3):
            out_ref[block * QR : (block + 1) * QR, part * HW : (part + 1) * HW] = dot(
                third_ref[part], rows, 1, 0
            ).astype(BF)


def out_grad_of(pieces, others):
    return pl.pallas_call(
        out_grad_kernel,
        out_shape=jax.ShapeDtypeStruct((LINES_ALL, 3 * HW), BF),
        in_specs=[VMEM] * 9,
        out_specs=VMEM,
        compiler_params=params(),
        cost_estimate=pl.CostEstimate(
            flops=4 * D * D * QR, bytes_accessed=4 << 20, transcendentals=0
        ),
        name="out_grad",
    )(*pieces, *others, jnp.asarray(room_thirds(), BF))


def first_grad_kernel(
    place_ref, q0, q1, q3, k0, k1, k3, qkv_ref, x_ref,
    p0, p1, p2, p3, grads_ref, gain_ref, first_ref,
):
    def total(refs):
        return functools.reduce(jnp.add, [ref[...].astype(F32) for ref in refs]).astype(BF)

    grads = jnp.concatenate([total((q0, q1, q3)), total((k0, k1, k3))], axis=0)
    grads_ref[...] = grads
    first = dot(grads, qkv_ref[...], 0, 1)
    first_ref[...] = first.astype(BF)
    for k, piece in enumerate((p0, p1, p2, p3)):
        piece[...] = first_ref[block_at(place_ref, k, T), :]
    unit, factor = norm_two(x_ref[...].astype(F32))
    gain = jnp.sum(first * unit, axis=0, keepdims=True)
    gain_ref[...] = jnp.broadcast_to(gain, (8, D))


def first_grad(place, queries, keyvals, qkv, stream):
    out = pl.pallas_call(
        first_grad_kernel,
        out_shape=[jax.ShapeDtypeStruct((T, D), BF)] * NS
        + [jax.ShapeDtypeStruct((3 * HW, QR), BF), jax.ShapeDtypeStruct((8, D), F32)],
        in_specs=[SMEM] + [VMEM] * 8,
        out_specs=[VMEM] * 6,
        scratch_shapes=[pltpu.VMEM((QR, D), BF)],
        compiler_params=params(),
        name="first_grad",
    )(place, *queries, *keyvals, qkv, stream)
    return list(out[0:4]), out[4], out[5]


def finish_kernel(
    place_ref, grads_ref, gain_ref, room_in_ref, og_ref, extra_ref,
    room_ref, line_ref, lane_ref, out_ref, tail_ref,
):
    grads = grads_ref[...]
    main = dot(room_in_ref[...], grads, 1, 1) + og_ref[...].astype(F32)
    out_ref[:, 0:QR] = main[:, 0:QR].astype(BF)
    at_gain = lax.broadcasted_iota(jnp.int32, (64, D), 0) == CD
    gains = jnp.where(at_gain, gain_ref[0:1, :], 0.0).astype(BF)
    for block in range(2):
        span = slice(block * QR, (block + 1) * QR)
        extra = extra_ref[span, :].astype(F32) + dot(
            room_ref[...], gains[:, block * HALF : (block + 1) * HALF], 1, 1
        )
        tail_ref[span, :] = jnp.concatenate([main[span, QR:], extra], axis=1)
    sums = jnp.sum(grads.astype(F32), axis=1, keepdims=True)
    biases = sums[0:HW] * lane_ref[0] + sums[2 * HW :] * lane_ref[1]
    own = pl.ds(pl.multiple_of(place_ref[3] * 256, 256), 256)
    tail_ref[own, :] += jnp.concatenate(
        [jnp.zeros((256, 64), F32), dot(line_ref[...], biases.astype(BF), 1, 0)], axis=1
    )
    out_ref[:, QR:] = tail_ref[...].astype(BF)


def finish(place, grads, gain, room_in, out_grad, extra):
    lines, lanes = bias_constants()
    return pl.pallas_call(
        finish_kernel,
        out_shape=jax.ShapeDtypeStruct((LINES_ALL, 640), BF),
        in_specs=[SMEM] + [VMEM] * 8,
        out_specs=VMEM,
        scratch_shapes=[pltpu.VMEM((LINES_ALL, 128), F32)],
        compiler_params=params(),
        name="finish",
    )(
        place, grads, gain, room_in, out_grad, extra,
        jnp.asarray(room_block(), BF), jnp.asarray(lines, BF), jnp.asarray(lanes, F32),
    )


def attend_back_kernel(place_ref, *refs):
    q_refs, kv_refs, do_ref = refs[0:4], refs[4:8], refs[8]
    dq_refs, dkv_refs = refs[9:13], refs[13:17]
    lse_ref, delta_ref, bias_ref, dq_ref = refs[17:21]
    bias_ref[...] = jnp.where(causal_tile(place_ref), 0.0, MASKED)
    for k in range(NS):
        for j in range(NS):
            stats = do_ref[j * NS + z_at(place_ref, k), HW:PACK, :].astype(F32)
            logs = lse_of(stats)
            deltas = stats[3 * HL : 4 * HL] + stats[4 * HL : 5 * HL]
            for h in range(HL):
                lse_ref[h, k : k + 1, j * T : (j + 1) * T] = logs[h : h + 1]
                delta_ref[h, k : k + 1, j * T : (j + 1) * T] = deltas[h : h + 1]

    def head(h, carry):
        rows = pl.ds(pl.multiple_of(h * HD, HD), HD)
        v_rows = pl.ds(pl.multiple_of(HW + h * HD, HD), HD)

        def stat(ref, j):
            return jnp.concatenate(
                [ref[h, i : i + 1, j * T : (j + 1) * T] for i in range(NS)], axis=1
            )

        for jp in range(NS):
            k_tile = tile_of(kv_refs, rows, jp)
            v_tile = tile_of(kv_refs, v_rows, jp)
            dk = dv = None
            for j in range(jp, NS):
                q_tile = tile_of(q_refs, rows, j)
                do_tile = jnp.concatenate(
                    [do_ref[j * NS + z_at(place_ref, k), rows, :] for k in range(NS)], axis=1
                )
                scores = dot(k_tile, q_tile, 0, 0)
                if jp == j:
                    scores = jnp.where(bias_ref[...] < 0.0, MASKED, scores)
                probs = jnp.exp(scores - stat(lse_ref, j))
                slopes = dot(v_tile, do_tile, 0, 0)
                ds = (probs * (slopes - stat(delta_ref, j))).astype(BF)
                dv_here = dot(do_tile, probs.astype(BF), 1, 1)
                dk_here = dot(q_tile, ds, 1, 1)
                dq_here = dot(k_tile, ds, 1, 0)
                dv = dv_here if dv is None else dv + dv_here
                dk = dk_here if dk is None else dk + dk_here
                if jp == 0:
                    dq_ref[j] = dq_here
                else:
                    dq_ref[j] += dq_here
            dk, dv = dk.astype(BF), dv.astype(BF)
            for i in range(NS):
                dkv_refs[i][rows, jp * T : (jp + 1) * T] = dk[:, i * T : (i + 1) * T]
                dkv_refs[i][v_rows, jp * T : (jp + 1) * T] = dv[:, i * T : (i + 1) * T]
        for j in range(NS):
            dq = (dq_ref[j] * HD ** (-0.5)).astype(BF)
            for i in range(NS):
                dq_refs[i][rows, j * T : (j + 1) * T] = dq[:, i * T : (i + 1) * T]
        return carry

    lax.fori_loop(0, HL, head, 0)


def attend_back(place, queries, keyvals, grads):
    out = pl.pallas_call(
        attend_back_kernel,
        out_shape=[jax.ShapeDtypeStruct((HW, QR), BF)] * NS
        + [jax.ShapeDtypeStruct((2 * HW, QR), BF)] * NS,
        in_specs=[SMEM] + [VMEM] * 9,
        out_specs=[VMEM] * 8,
        scratch_shapes=[
            pltpu.VMEM((HL, 8, QR), F32),
            pltpu.VMEM((HL, 8, QR), F32),
            pltpu.VMEM((QR, QR), F32),
            pltpu.VMEM((NS, HD, QR), F32),
        ],
        compiler_params=params(),
        cost_estimate=pl.CostEstimate(
            flops=10 * 30 * QR * QR * HD, bytes_accessed=6 << 20, transcendentals=30 * QR * QR
        ),
        name="attend_back",
    )(place, *queries, *keyvals, grads)
    return out[0:NS], out[NS:]


def pick_rows(target, offset):
    lines = lax.broadcasted_iota(jnp.int32, (T, ROWS), 1)
    return (lines == target + offset).astype(F32).astype(BF)


def norm_two(middle):
    factor = lax.rsqrt(jnp.mean(middle * middle, axis=-1, keepdims=True) + EPS)
    return middle * factor, factor


def route_kernel(
    place_ref, x_ref, small_ref, router_ref, ids_ref, cot_ref, o0, o1, o2, o3, w0, w1, w2, w3,
    out_ref, m_ref, a_ref, gate_ref, target_ref, o_ref, w_ref, lse_ref,
):
    for k, (o_piece, w_piece) in enumerate(((o0, w0), (o1, w1), (o2, w2), (o3, w3))):
        o_ref[block_at(place_ref, k, HW), :] = o_piece[0:HW, :]
        w_ref[block_at(place_ref, k, HW), :] = w_piece[...]
        logs = lse_of(o_piece[HW:PACK, :].astype(F32))
        lse_ref[(place_ref[3] + place_ref[2] * k) & 3] = jnp.concatenate(
            [logs, jnp.zeros((8 - HL, T), F32)], axis=0
        )
    branch = dot(o_ref[...], w_ref[...], 0, 1)
    middle = x_ref[...].astype(F32) + branch + small_ref[2:3, :]
    unit, factor = norm_two(middle)
    second = (unit * small_ref[1:2, :]).astype(BF)
    logits = dot(second, router_ref[...], 1, 0)
    cols = lax.broadcasted_iota(jnp.int32, (T, CD), 1)
    named = [(ids_ref[:, k : k + 1] == cols).astype(F32) for k in range(TOPK)]
    earlier = lax.broadcasted_iota(jnp.int32, (T, T), 1) < lax.broadcasted_iota(
        jnp.int32, (T, T), 0
    )
    counts = dot(earlier.astype(F32).astype(BF), (named[0] + named[1]).astype(BF), 1, 0)
    chosen = [jnp.sum(name * logits, axis=1, keepdims=True) for name in named]
    top = jnp.maximum(chosen[0], chosen[1])
    raw = [jnp.exp(value - top) for value in chosen]
    gates = [value / (raw[0] + raw[1]) for value in raw]
    slots = [jnp.sum(name * counts, axis=1, keepdims=True).astype(jnp.int32) for name in named]
    targets = [ids_ref[:, k : k + 1] * SLOTS + slots[k] for k in range(TOPK)]
    grads = cot_ref[...].astype(F32)
    places = jnp.concatenate(
        [pick_rows(targets[0], 0) + pick_rows(targets[1], 0)]
        + [pick_rows(targets[k], CAP) for k in range(TOPK)],
        axis=0,
    )
    values = jnp.concatenate([second] + [(gates[k] * grads).astype(BF) for k in range(TOPK)], axis=0)
    out_ref[...] = dot(places, values, 0, 0).astype(BF)
    m_ref[...] = middle
    a_ref[...] = second
    gate_ref[...] = jnp.concatenate(gates, axis=1)
    target_ref[...] = jnp.concatenate(targets, axis=1)


def route(place, rows, small, router, ids, cotangent, pieces, out_weights):
    return pl.pallas_call(
        route_kernel,
        out_shape=[
            jax.ShapeDtypeStruct((ROWS, D), BF),
            jax.ShapeDtypeStruct((T, D), F32),
            jax.ShapeDtypeStruct((T, D), BF),
            jax.ShapeDtypeStruct((T, TOPK), F32),
            jax.ShapeDtypeStruct((T, TOPK), jnp.int32),
            jax.ShapeDtypeStruct((D, T), BF),
            jax.ShapeDtypeStruct((D, D), BF),
            jax.ShapeDtypeStruct((NS, 8, T), F32),
        ],
        in_specs=[SMEM] + [VMEM] * 13,
        out_specs=[VMEM] * 8,
        compiler_params=params(),
        name="route",
    )(place, rows, small, router, ids, cotangent, *pieces, *out_weights)


GELU_A = float(np.sqrt(2.0 / np.pi))
GELU_B = 0.044715


def expert_kernel(
    rows_ref, pick_ref, win_ref, wout_ref, out_ref, gin_ref, gout_ref,
    a_ref, dy_ref, y_ref, da_ref,
):
    step = pl.program_id(0)

    @pl.when(step == 0)
    def first():
        both = dot(pick_ref[...], rows_ref[...], 1, 0).astype(BF)
        a_ref[...] = both[0:LINES]
        dy_ref[...] = both[LINES:]

    rows, grads = a_ref[...], dy_ref[...]
    inner, outer = win_ref[0], wout_ref[0]
    pre = dot(rows, inner, 1, 0)
    square = pre * pre
    bent = jnp.tanh(GELU_A * pre * (1.0 + GELU_B * square))
    act = (0.5 * pre * (1.0 + bent)).astype(BF)
    slope = 0.5 * (1.0 + bent) + 0.5 * pre * (1.0 - bent * bent) * (
        GELU_A * (1.0 + 3.0 * GELU_B * square)
    )
    pre_grad = (dot(grads, outer, 1, 0) * slope).astype(BF)
    made = dot(act, outer, 1, 1)
    back = dot(pre_grad, inner, 1, 1)
    gin_ref[0] = dot(rows, pre_grad, 0, 0).astype(BF)
    gout_ref[0] = dot(grads, act, 0, 0).astype(BF)

    @pl.when(step == 0)
    def start():
        y_ref[...] = made
        da_ref[...] = back

    @pl.when(step > 0)
    def more():
        y_ref[...] += made
        da_ref[...] += back

    @pl.when(step == pl.num_programs(0) - 1)
    def last():
        both = jnp.concatenate([y_ref[...].astype(BF), da_ref[...].astype(BF)], axis=0)
        out_ref[...] = dot(pick_ref[...], both, 0, 0).astype(BF)


def widen_kernel(in_ref, out_ref):
    out_ref[...] = in_ref[...].astype(F32)


def widen(values):
    rows, width = values.shape
    spec = pl.BlockSpec((rows // 4, width), lambda i: (i, 0))
    return pl.pallas_call(
        widen_kernel,
        grid=(4,),
        out_shape=jax.ShapeDtypeStruct(values.shape, F32),
        in_specs=[spec],
        out_specs=spec,
        cost_estimate=pl.CostEstimate(
            flops=rows * width, bytes_accessed=6 * rows * width, transcendentals=0
        ),
        name="widen",
    )(values)


def expert_pick():
    lines = np.arange(LINES)
    pick = np.zeros((2 * LINES, ROWS), np.float32)
    pick[lines, lines // CAP * SLOTS + lines % CAP] = 1.0
    pick[LINES + lines, lines // CAP * SLOTS + CAP + lines % CAP] = 1.0
    return pick


def expert(rows, inner, outer):
    tile = 768
    halves = D // tile

    def weight_spec():
        return pl.BlockSpec((1, D, tile), lambda i: (i // halves, 0, i % halves))

    def whole(*shape):
        return pl.BlockSpec(shape, lambda i: (0, 0))

    return pl.pallas_call(
        expert_kernel,
        grid=(NS * halves,),
        out_shape=[
            jax.ShapeDtypeStruct((ROWS, D), BF),
            jax.ShapeDtypeStruct((NS, D, D), BF),
            jax.ShapeDtypeStruct((NS, D, D), BF),
        ],
        in_specs=[whole(ROWS, D), whole(2 * LINES, ROWS), weight_spec(), weight_spec()],
        out_specs=[whole(ROWS, D), weight_spec(), weight_spec()],
        scratch_shapes=[
            pltpu.VMEM((LINES, D), BF),
            pltpu.VMEM((LINES, D), BF),
            pltpu.VMEM((LINES, D), F32),
            pltpu.VMEM((LINES, D), F32),
        ],
        compiler_params=params(dimension_semantics=("arbitrary",)),
        cost_estimate=pl.CostEstimate(
            flops=12 * LINES * D * 4 * D, bytes_accessed=20 << 20, transcendentals=LINES * 4 * D
        ),
        name="expert",
    )(rows, jnp.asarray(expert_pick(), BF), inner, outer)


def settle_kernel(
    place_ref, back_ref, m_ref, a_ref, gate_ref, target_ref, ids_ref, cot_ref, small_ref, router_ref,
    w_ref, o_ref, lse_ref,
    mixed_ref, dm_ref, rg_ref, sums_ref, out_ref, d0, d1, d2, d3, turn_ref,
):
    back = back_ref[...]
    targets = [target_ref[:, k : k + 1] for k in range(TOPK)]
    picked = [dot(pick_rows(target, 0), back, 1, 0) for target in targets]
    returned = dot(pick_rows(targets[0], CAP) + pick_rows(targets[1], CAP), back, 1, 0)
    middle = m_ref[...]
    grads = cot_ref[...].astype(F32)
    gates = [gate_ref[:, k : k + 1] for k in range(TOPK)]
    mixed_ref[...] = (middle + gates[0] * picked[0] + gates[1] * picked[1]).astype(BF)
    gate_grads = [jnp.sum(grads * value, axis=1, keepdims=True) for value in picked]
    mean = gates[0] * gate_grads[0] + gates[1] * gate_grads[1]
    cols = lax.broadcasted_iota(jnp.int32, (T, CD), 1)
    logit_grad = functools.reduce(
        jnp.add,
        [
            jnp.where(ids_ref[:, k : k + 1] == cols, gates[k] * (gate_grads[k] - mean), 0.0)
            for k in range(TOPK)
        ],
    ).astype(BF)
    rg_ref[...] = dot(a_ref[...], logit_grad, 0, 0)
    second_grad = dot(logit_grad, router_ref[...], 1, 1) + returned
    unit, factor = norm_two(middle)
    weighted = second_grad * small_ref[1:2, :]
    whole = grads + factor * (weighted - unit * jnp.mean(weighted * unit, axis=-1, keepdims=True))
    dm_ref[...] = whole
    rounded = whole.astype(BF)
    head_grads = dot(rounded, w_ref[...], 1, 0).T.astype(BF)
    product = head_grads.astype(F32) * o_ref[...].astype(F32)
    rest = jnp.zeros((PACK - HW - 5 * HL, T), F32)
    for s in range(NS):
        delta = [
            jnp.sum(product[s * HW + h * HD : s * HW + (h + 1) * HD], axis=0, keepdims=True)
            for h in range(HL)
        ]
        high, middle, low = split3(lse_ref[s][0:HL])
        d_high, d_middle, unused = split3(jnp.concatenate(delta, axis=0))
        stats = jnp.concatenate([high, middle, low, d_high, d_middle, rest], axis=0).astype(BF)
        for z in range(NS):
            out_ref[s * NS + z, 0:HW, :] = head_grads[s * HW : (s + 1) * HW]
            out_ref[s * NS + z, HW:PACK, :] = stats
    turn_ref[...] = rounded.astype(F32).T.astype(BF)
    for k, d_ref in enumerate((d0, d1, d2, d3)):
        d_ref[...] = turn_ref[block_at(place_ref, k, HW), :]
    sums_ref[...] = jnp.concatenate(
        [
            jnp.sum(second_grad * unit, axis=0, keepdims=True),
            jnp.sum(rounded.astype(F32), axis=0, keepdims=True),
            jnp.zeros((6, D), F32),
        ],
        axis=0,
    )


def settle(place, back, middle, second, gates, targets, ids, cotangent, small, router, weight, heads, lse):
    out = pl.pallas_call(
        settle_kernel,
        out_shape=[
            jax.ShapeDtypeStruct((T, D), BF),
            jax.ShapeDtypeStruct((T, D), F32),
            jax.ShapeDtypeStruct((D, CD), F32),
            jax.ShapeDtypeStruct((8, D), F32),
            jax.ShapeDtypeStruct((NS * NS, PACK, T), BF),
        ]
        + [jax.ShapeDtypeStruct((HW, T), BF)] * NS,
        in_specs=[SMEM] + [VMEM] * 12,
        out_specs=[VMEM] * 9,
        scratch_shapes=[pltpu.VMEM((D, T), BF)],
        compiler_params=params(),
        name="settle",
    )(
        place, back, middle, second, gates, targets, ids, cotangent, small, router, weight, heads, lse
    )
    return out[0:5], out[5:9]


def arrival_constants():
    rows = np.zeros((D, LINES_ALL), np.float32)
    thirds = np.zeros((3, LINES_ALL, D), np.float32)
    for g in range(D):
        n, i = divmod(g, 6)
        start = (n % CD * NS + n // CD) * 8
        rows[g, start + i] = 1.0
        thirds[i % 3, start + 6 + i // 3, g] = 1.0
    return rows, thirds


def room_block():
    rows = np.zeros((QR, HALF), np.float32)
    for g in range(HALF):
        rows[g // 6 * 8 + g % 6, g] = 1.0
    return rows


def room_thirds():
    thirds = np.zeros((3, QR, HALF), np.float32)
    for g in range(HALF):
        n, i = divmod(g, 6)
        thirds[i % 3, n * 8 + 6 + i // 3, g] = 1.0
    return thirds


def bias_constants():
    lines = np.zeros((256, HW), np.float32)
    lanes = np.zeros((2, HW, 64), np.float32)
    for r in range(HW):
        n, i = divmod(r, 6)
        lines[n * 8 + 6, r] = 1.0
        lanes[0, r, CD + 3 + i] = 1.0
        lanes[1, r, CD + 9 + i] = 1.0
    return lines, lanes


def spread(rows, width):
    return jnp.pad(rows, [(0, 0)] * (rows.ndim - 1) + [(0, width - rows.shape[-1])])


def per_device(
    tokens,
    qkv_weight,
    out_weight,
    router_weight,
    attn_gain,
    ffn_gain,
    query_bias,
    value_bias,
    out_bias,
    expert_in,
    expert_out,
    expert_ids,
    cotangent,
):
    rows_at, thirds_at = [jnp.asarray(value, BF) for value in arrival_constants()]
    seq = lax.axis_index("seq")
    back = 2 * lax.axis_index("dp") - 1
    place = jnp.stack([lax.axis_index("z"), lax.axis_index("y"), back, seq]).astype(jnp.int32)
    mine = (jnp.arange(NS) == seq).astype(BF)
    rows = tokens.reshape(T, D)
    ids = expert_ids.reshape(T, TOPK)
    cot = cotangent.reshape(T, D)

    inner = lax.all_gather(expert_in[0], "seq", axis=0, tiled=False)
    outer = lax.all_gather(expert_out[0], "seq", axis=0, tiled=False)

    columns = qkv_weight.reshape(6, 3, NS, HW).transpose(2, 0, 1, 3).reshape(NS, 6, 3 * HW)
    extras = jnp.concatenate(
        [router_weight, attn_gain[:, None], ffn_gain[:, None], out_bias[:, None]], axis=1
    )
    upper = jnp.concatenate(
        [columns, jnp.broadcast_to(spread(extras, 64)[None], (NS, 6, 64))], axis=2
    )
    quarters = out_weight.reshape(2, 3, NS, HW).transpose(2, 0, 1, 3).reshape(NS, 2, 3 * HW)
    biases = jnp.concatenate([query_bias, value_bias])[None, None] * mine[:, None, None]
    corner = jnp.pad(biases, ((0, 0), (0, 1), (0, 52)))
    lower = jnp.concatenate([quarters, corner], axis=2)
    sent = jnp.concatenate([upper, lower], axis=1)
    sent = swap_seq(sent).reshape(1, NS * 8, 640)
    arrived = swap_experts(jnp.broadcast_to(sent, (CD, NS * 8, 640)))
    weights = arrived.reshape(LINES_ALL, 640)
    sorted_weights = dot(rows_at, weights, 1, 0).astype(BF)
    qkv = sorted_weights[:, : 3 * HW]
    router = sorted_weights[:, 3 * HW : 3 * HW + CD]
    small = dot(weights[:, 608:616], rows_at, 0, 1)
    own_bias = jnp.sum(
        arrived.reshape(CD, NS, 8, 640)[:, :, 6, 576:588].astype(F32), axis=1
    )
    bias = jnp.concatenate(
        [own_bias[:, :6].reshape(HW), jnp.zeros((HW,), F32), own_bias[:, 6:].reshape(HW)]
    )

    stream = gather_seq(rows, back).reshape(QR, D)
    first_in = (norm_two(stream.astype(F32))[0] * small[0:1]).astype(BF)
    projected = (dot(qkv, first_in, 0, 1) + bias[:, None]).astype(BF)
    keyvals = collect(projected[HW:], "y")
    queries = collect(projected[:HW] * jnp.asarray(HD ** (-0.5), BF), "z")
    out_piece = sum(
        dot(weights[:, part * HW : (part + 1) * HW], thirds_at[part], 0, 0) for part in range(3)
    ).astype(BF)
    out_weights = collect(out_piece, "x")
    partial = attend(place, queries, keyvals)
    partial, out_weights = lax.optimization_barrier((partial, out_weights))
    pieces = merge(place, deliver(partial, "z"))
    pieces = [pieces[0]] + [jump(pieces[k], "x", k) for k in range(1, NS)]

    outgoing, middle, second, gates, targets, whole_heads, weight, lse = route(
        place, rows, small, router, ids, cot, pieces, out_weights
    )
    received = swap_experts(outgoing.reshape(CD, SLOTS, D)).reshape(ROWS, D)
    others = deliver([whole_heads] * NS, "x")
    made, inner_grad, outer_grad = expert(received, inner, outer)
    returned = swap_experts(made.reshape(CD, SLOTS, D)).reshape(ROWS, D)
    inner_grad = lax.psum_scatter(inner_grad, "seq", scatter_dimension=0, tiled=False)
    outer_grad = lax.psum_scatter(outer_grad, "seq", scatter_dimension=0, tiled=False)
    (mixed, middle_grad, router_grad, sums, heads_grad), column_pieces = settle(
        place, returned, middle, second, gates, targets, ids, cot, small, router, weight,
        whole_heads, lse,
    )

    heads_grad = swap_plane(heads_grad)
    column_pieces, heads_grad = lax.optimization_barrier((column_pieces, heads_grad))
    column_pieces = deliver(column_pieces, "x")
    query_parts, keyval_parts = attend_back(place, queries, keyvals, heads_grad)
    out_grad = out_grad_of(column_pieces, others)
    room = jnp.asarray(room_block(), BF)
    room_in = jnp.concatenate([dot(room, half, 1, 1) for half in jnp.split(first_in, 2, axis=1)])
    after = jnp.concatenate(
        [router_grad.astype(BF), jnp.zeros((D, 1), BF), sums[0:2].T.astype(BF)], axis=1
    )
    extra = spread(jnp.concatenate([dot(room, half, 1, 0) for half in jnp.split(after, 2)]), 64)
    keyval_grads, unused = deliver_sum(keyval_parts, "y")
    query_grads, (out_grad, room_in, extra) = deliver_sum(
        query_parts, "z", (out_grad, room_in.astype(BF), extra.astype(BF))
    )
    keyval_grads, inner_grad = lax.optimization_barrier((keyval_grads, widen(inner_grad)))
    parts, grads, gain = first_grad(place, query_grads, keyval_grads, qkv, stream)
    grads = finish(place, grads, gain, room_in, out_grad, extra)
    mine_grad = sum(part.astype(F32) for part in deliver(parts, "x"))
    own_unit, own_factor = norm_two(rows.astype(F32))
    weighted = mine_grad * small[0:1]
    input_grad = middle_grad + own_factor * (
        weighted - own_unit * jnp.mean(weighted * own_unit, axis=-1, keepdims=True)
    )

    dealt = swap_all(grads.reshape(NS * CD, 8, 640)).reshape(NS, CD, 8, 640)
    totals = jnp.sum(dealt.astype(F32), axis=1)
    extra = jnp.sum(totals[:, :, 3 * HW :], axis=0)
    whole_qkv = (
        totals[:, :6, : 3 * HW].reshape(NS, 6, 3, HW).transpose(1, 2, 0, 3).reshape(6, 3 * D)
    )
    whole_out = totals[:, 6:, : 3 * HW].reshape(NS, 2, 3, HW).transpose(1, 2, 0, 3).reshape(6, D)
    return (
        mixed.reshape(tokens.shape),
        input_grad.astype(BF).reshape(tokens.shape),
        whole_qkv,
        whole_out,
        extra[:6, :CD],
        extra[:6, CD],
        extra[:6, CD + 1],
        extra[6, CD + 3 : CD + 9],
        extra[6, CD + 9 : CD + 15],
        extra[:6, CD + 2],
        inner_grad[None],
        widen(outer_grad)[None],
    )


def solution(mesh):
    sizes = (mesh.shape["seq"], NS, mesh.shape["ctx"] // NS, mesh.shape["dp"])
    return jax.shard_map(
        per_device,
        mesh=jax.sharding.Mesh(mesh.devices.reshape(sizes), ALL),
        in_specs=(
            P("dp", ALL[:3], None),
            P(ALL, None),
            P(ALL, None),
            P(ALL, None),
            P(ALL),
            P(ALL),
            P(ALL),
            P(ALL),
            P(ALL),
            P(ALL[1:], None, "seq"),
            P(ALL[1:], None, "seq"),
            P("dp", ALL[:3], None),
            P("dp", ALL[:3], None),
        ),
        out_specs=(
            P("dp", ALL[:3], None),
            P("dp", ALL[:3], None),
            P(ALL, None),
            P(ALL, None),
            P(ALL, None),
            P(ALL),
            P(ALL),
            P(ALL),
            P(ALL),
            P(ALL),
            P(ALL[1:], None, "seq"),
            P(ALL[1:], None, "seq"),
        ),
        check_vma=False,
    )
```

```python
import functools

import jax
import jax.numpy as jnp
import numpy as np
from jax import lax
from jax.experimental import pallas as pl
from jax.experimental.pallas import tpu as pltpu
from jax.sharding import PartitionSpec as P

H = 12
HD = 64
TOPK = 2
D = 768
T = 128
NS = 4
HL = H // NS
HW = HL * HD
QR = NS * T
CD = 32
CAP = 9
SLOTS = 24
ROWS = CD * SLOTS
LINES = CD * CAP
LINES_ALL = 8 * 4 * CD
HALF = D // 2
PACK = 208

ALL = ("seq", "z", "y", "dp")

EPS = 1e-06
MASKED = -1e30
BF = jnp.bfloat16
F32 = jnp.float32

VMEM = pl.BlockSpec(memory_space=pltpu.VMEM)
SMEM = pl.BlockSpec(memory_space=pltpu.SMEM)


def dot(former, latter, former_dim, latter_dim):
    return lax.dot_general(
        former,
        latter,
        (((former_dim,), (latter_dim,)), ((), ())),
        preferred_element_type=F32,
    )


def params(**more):
    return pltpu.CompilerParams(vmem_limit_bytes=56 * 1024 * 1024, **more)


def jump(values, axis, steps):
    pairs = []
    for x in range(NS):
        for z in range(NS):
            for y in range(NS):
                for core in range(2):
                    far = {"x": x, "z": z, "y": y}
                    far[axis] += -steps if core else steps
                    there = (far["x"] % NS * NS + far["z"] % NS) * NS + far["y"] % NS
                    pairs.append((((x * NS + z) * NS + y) * 2 + core, there * 2 + core))
    return lax.ppermute(values, ALL, pairs)


def collect(values, axis):
    return [values] + [jump(values, axis, k) for k in range(1, NS)]


def deliver(pieces, axis):
    return [pieces[0]] + [jump(pieces[k], axis, -k) for k in range(1, NS)]


def deliver_sum(pieces, axis, beside=()):
    middle = jump(pieces[2], axis, 1)
    first = jump(pieces[1], axis, -1)
    onward, beside = lax.optimization_barrier((pieces[3], tuple(beside)))
    third = jump((onward.astype(F32) + middle.astype(F32)).astype(BF), axis, 1)
    return (pieces[0], first, third), beside


def swap_experts(values):
    return lax.all_to_all(values, ALL[1:], split_axis=0, concat_axis=0, tiled=True)


def swap_plane(values):
    return lax.all_to_all(values, ("seq", "z"), split_axis=0, concat_axis=0, tiled=True)


def swap_seq(values):
    return lax.all_to_all(values, "seq", split_axis=0, concat_axis=0, tiled=True)


def swap_all(values):
    return lax.all_to_all(values, ALL, split_axis=0, concat_axis=0, tiled=True)


def gather_seq(values, back):
    place = lax.axis_index("seq")
    whole = jnp.zeros((NS,) + values.shape, values.dtype)
    for k, piece in enumerate(collect(values, "x")):
        whole = lax.dynamic_update_slice(whole, piece[None], ((place + back * k) % NS, 0, 0))
    return whole


def tile_of(refs, rows, j):
    return jnp.concatenate([ref[rows, j * T : (j + 1) * T] for ref in refs], axis=1)


def causal_tile(place_ref):
    z, y, back = place_ref[0], place_ref[1], place_ref[2]
    k_index = lax.broadcasted_iota(jnp.int32, (QR, QR), 0)
    q_index = lax.broadcasted_iota(jnp.int32, (QR, QR), 1)
    k_place = z * QR + (((y + back * (k_index >> 7)) & 3) << 7) + (k_index & 127)
    q_place = (((z + back * (q_index >> 7)) & 3) << 9) + y * T + (q_index & 127)
    return k_place <= q_place


def split3(values):
    high = values.astype(BF).astype(F32)
    middle = (values - high).astype(BF).astype(F32)
    return high, middle, values - high - middle


def z_at(place_ref, k):
    return (place_ref[0] + place_ref[2] * k) & 3


def attend_kernel(place_ref, *refs):
    q_refs, kv_refs, o_refs, lse_ref, bias_ref = refs[0:4], refs[4:8], refs[8:12], refs[12], refs[13]
    bias_ref[...] = jnp.where(causal_tile(place_ref), 0.0, MASKED)
    work = [(j, jp) for j in range(NS) for jp in range(j + 1)]

    def head(h, carry):
        rows = pl.ds(pl.multiple_of(h * HD, HD), HD)
        v_rows = pl.ds(pl.multiple_of(HW + h * HD, HD), HD)
        k_tiles = [tile_of(kv_refs, rows, jp) for jp in range(NS)]
        v_tiles = [tile_of(kv_refs, v_rows, jp) for jp in range(NS)]

        def scores_of(j, jp):
            scores = dot(k_tiles[jp], tile_of(q_refs, rows, j), 0, 0)
            return jnp.where(bias_ref[...] < 0.0, MASKED, scores) if jp == j else scores

        following = scores_of(*work[0])
        for n, (j, jp) in enumerate(work):
            scores = following
            if n + 1 < len(work):
                following = scores_of(*work[n + 1])
            here = jnp.max(scores, axis=0, keepdims=True)
            if jp == 0:
                top = here
                probs = jnp.exp(scores - top)
                total = jnp.sum(probs, axis=0, keepdims=True)
                acc = dot(v_tiles[jp], probs.astype(BF), 1, 0)
            else:
                higher = jnp.maximum(top, here)
                fade = jnp.exp(top - higher)
                probs = jnp.exp(scores - higher)
                total = total * fade + jnp.sum(probs, axis=0, keepdims=True)
                acc = acc * fade + dot(v_tiles[jp], probs.astype(BF), 1, 0)
                top = higher
            if jp == j:
                out = (acc / total).astype(BF)
                lse = top + jnp.log(total)
                for k in range(NS):
                    o_refs[k][rows, j * T : (j + 1) * T] = out[:, k * T : (k + 1) * T]
                    lse_ref[h, k : k + 1, j * T : (j + 1) * T] = lse[:, k * T : (k + 1) * T]
        return carry

    lax.fori_loop(0, HL, head, 0)
    for k in range(NS):
        logs = jnp.concatenate([lse_ref[h, k : k + 1, :] for h in range(HL)], axis=0)
        o_refs[k][HW:PACK, :] = log_rows(logs)


def log_rows(logs):
    rest = jnp.zeros((PACK - HW - 3 * HL, logs.shape[1]), F32)
    return jnp.concatenate([*split3(logs), rest], axis=0).astype(BF)


def attend(place, queries, keyvals):
    return pl.pallas_call(
        attend_kernel,
        out_shape=[jax.ShapeDtypeStruct((PACK, QR), BF)] * NS,
        in_specs=[SMEM] + [VMEM] * 8,
        out_specs=[VMEM] * NS,
        scratch_shapes=[pltpu.VMEM((HL, 8, QR), F32), pltpu.VMEM((QR, QR), F32)],
        compiler_params=params(),
        cost_estimate=pl.CostEstimate(
            flops=4 * 30 * QR * QR * HD, bytes_accessed=4 << 20, transcendentals=30 * QR * QR
        ),
        name="attend",
    )(place, *queries, *keyvals)


def lse_of(stats):
    return stats[0:HL] + stats[HL : 2 * HL] + stats[2 * HL : 3 * HL]


def block_at(place_ref, k, size):
    return pl.ds(pl.multiple_of(((place_ref[3] + place_ref[2] * k) & 3) * size, 64), size)


def merge_kernel(place_ref, *refs):
    parts, piece_refs, o_ref = refs[0:4], refs[4:8], refs[8]
    logs = [lse_of(part[HW:PACK, :].astype(F32)) for part in parts]
    top = functools.reduce(jnp.maximum, logs)
    lse = top + jnp.log(functools.reduce(jnp.add, [jnp.exp(log - top) for log in logs]))
    shares = [jnp.exp(log - lse) for log in logs]
    for h in range(HL):
        rows = slice(h * HD, (h + 1) * HD)
        o_ref[rows, :] = functools.reduce(
            jnp.add,
            [part[rows, :].astype(F32) * share[h : h + 1] for part, share in zip(parts, shares)],
        ).astype(BF)
    o_ref[HW:PACK, :] = log_rows(lse)
    for k, piece in enumerate(piece_refs):
        block = (place_ref[3] - place_ref[2] * k) & 3
        piece[...] = o_ref[:, pl.ds(pl.multiple_of(block * T, T), T)]


def merge(place, parts):
    return pl.pallas_call(
        merge_kernel,
        out_shape=[jax.ShapeDtypeStruct((PACK, T), BF)] * NS,
        in_specs=[SMEM] + [VMEM] * 4,
        out_specs=[VMEM] * NS,
        scratch_shapes=[pltpu.VMEM((PACK, QR), BF)],
        compiler_params=params(),
        name="merge",
    )(place, *parts)


def out_grad_kernel(*refs):
    pieces, others, third_ref, out_ref = refs[0:4], refs[4:8], refs[8], refs[9]
    grads = functools.reduce(
        jnp.add,
        [dot(other[...], piece[...], 1, 1) for piece, other in zip(pieces, others)],
    ).astype(BF)
    for block in range(2):
        rows = grads[block * HALF : (block + 1) * HALF]
        for part in range(3):
            out_ref[block * QR : (block + 1) * QR, part * HW : (part + 1) * HW] = dot(
                third_ref[part], rows, 1, 0
            ).astype(BF)


def out_grad_of(pieces, others):
    return pl.pallas_call(
        out_grad_kernel,
        out_shape=jax.ShapeDtypeStruct((LINES_ALL, 3 * HW), BF),
        in_specs=[VMEM] * 9,
        out_specs=VMEM,
        compiler_params=params(),
        cost_estimate=pl.CostEstimate(
            flops=4 * D * D * QR, bytes_accessed=4 << 20, transcendentals=0
        ),
        name="out_grad",
    )(*pieces, *others, jnp.asarray(room_thirds(), BF))


def first_grad_kernel(
    place_ref, q0, q1, q3, k0, k1, k3, qkv_ref, x_ref,
    p0, p1, p2, p3, grads_ref, gain_ref, first_ref,
):
    def total(refs):
        return functools.reduce(jnp.add, [ref[...].astype(F32) for ref in refs]).astype(BF)

    grads = jnp.concatenate([total((q0, q1, q3)), total((k0, k1, k3))], axis=0)
    grads_ref[...] = grads
    first = dot(grads, qkv_ref[...], 0, 1)
    first_ref[...] = first.astype(BF)
    for k, piece in enumerate((p0, p1, p2, p3)):
        piece[...] = first_ref[block_at(place_ref, k, T), :]
    unit, factor = norm_two(x_ref[...].astype(F32))
    gain = jnp.sum(first * unit, axis=0, keepdims=True)
    gain_ref[...] = jnp.broadcast_to(gain, (8, D))


def first_grad(place, queries, keyvals, qkv, stream):
    out = pl.pallas_call(
        first_grad_kernel,
        out_shape=[jax.ShapeDtypeStruct((T, D), BF)] * NS
        + [jax.ShapeDtypeStruct((3 * HW, QR), BF), jax.ShapeDtypeStruct((8, D), F32)],
        in_specs=[SMEM] + [VMEM] * 8,
        out_specs=[VMEM] * 6,
        scratch_shapes=[pltpu.VMEM((QR, D), BF)],
        compiler_params=params(),
        name="first_grad",
    )(place, *queries, *keyvals, qkv, stream)
    return list(out[0:4]), out[4], out[5]


def finish_kernel(
    place_ref, grads_ref, gain_ref, room_in_ref, og_ref, extra_ref,
    room_ref, line_ref, lane_ref, out_ref, tail_ref,
):
    grads = grads_ref[...]
    main = dot(room_in_ref[...], grads, 1, 1) + og_ref[...].astype(F32)
    out_ref[:, 0:QR] = main[:, 0:QR].astype(BF)
    at_gain = lax.broadcasted_iota(jnp.int32, (64, D), 0) == CD
    gains = jnp.where(at_gain, gain_ref[0:1, :], 0.0).astype(BF)
    for block in range(2):
        span = slice(block * QR, (block + 1) * QR)
        extra = extra_ref[span, :].astype(F32) + dot(
            room_ref[...], gains[:, block * HALF : (block + 1) * HALF], 1, 1
        )
        tail_ref[span, :] = jnp.concatenate([main[span, QR:], extra], axis=1)
    sums = jnp.sum(grads.astype(F32), axis=1, keepdims=True)
    biases = sums[0:HW] * lane_ref[0] + sums[2 * HW :] * lane_ref[1]
    own = pl.ds(pl.multiple_of(place_ref[3] * 256, 256), 256)
    tail_ref[own, :] += jnp.concatenate(
        [jnp.zeros((256, 64), F32), dot(line_ref[...], biases.astype(BF), 1, 0)], axis=1
    )
    out_ref[:, QR:] = tail_ref[...].astype(BF)


def finish(place, grads, gain, room_in, out_grad, extra):
    lines, lanes = bias_constants()
    return pl.pallas_call(
        finish_kernel,
        out_shape=jax.ShapeDtypeStruct((LINES_ALL, 640), BF),
        in_specs=[SMEM] + [VMEM] * 8,
        out_specs=VMEM,
        scratch_shapes=[pltpu.VMEM((LINES_ALL, 128), F32)],
        compiler_params=params(),
        name="finish",
    )(
        place, grads, gain, room_in, out_grad, extra,
        jnp.asarray(room_block(), BF), jnp.asarray(lines, BF), jnp.asarray(lanes, F32),
    )


def attend_back_kernel(place_ref, *refs):
    q_refs, kv_refs, do_ref = refs[0:4], refs[4:8], refs[8]
    dq_refs, dkv_refs = refs[9:13], refs[13:17]
    lse_ref, delta_ref, bias_ref, dq_ref = refs[17:21]
    bias_ref[...] = jnp.where(causal_tile(place_ref), 0.0, MASKED)
    for k in range(NS):
        for j in range(NS):
            stats = do_ref[j * NS + z_at(place_ref, k), HW:PACK, :].astype(F32)
            logs = lse_of(stats)
            deltas = stats[3 * HL : 4 * HL] + stats[4 * HL : 5 * HL]
            for h in range(HL):
                lse_ref[h, k : k + 1, j * T : (j + 1) * T] = logs[h : h + 1]
                delta_ref[h, k : k + 1, j * T : (j + 1) * T] = deltas[h : h + 1]

    def head(h, carry):
        rows = pl.ds(pl.multiple_of(h * HD, HD), HD)
        v_rows = pl.ds(pl.multiple_of(HW + h * HD, HD), HD)

        def stat(ref, j):
            return jnp.concatenate(
                [ref[h, i : i + 1, j * T : (j + 1) * T] for i in range(NS)], axis=1
            )

        for jp in range(NS):
            k_tile = tile_of(kv_refs, rows, jp)
            v_tile = tile_of(kv_refs, v_rows, jp)
            dk = dv = None
            for j in range(jp, NS):
                q_tile = tile_of(q_refs, rows, j)
                do_tile = jnp.concatenate(
                    [do_ref[j * NS + z_at(place_ref, k), rows, :] for k in range(NS)], axis=1
                )
                scores = dot(k_tile, q_tile, 0, 0)
                if jp == j:
                    scores = jnp.where(bias_ref[...] < 0.0, MASKED, scores)
                probs = jnp.exp(scores - stat(lse_ref, j))
                slopes = dot(v_tile, do_tile, 0, 0)
                ds = (probs * (slopes - stat(delta_ref, j))).astype(BF)
                dv_here = dot(do_tile, probs.astype(BF), 1, 1)
                dk_here = dot(q_tile, ds, 1, 1)
                dq_here = dot(k_tile, ds, 1, 0)
                dv = dv_here if dv is None else dv + dv_here
                dk = dk_here if dk is None else dk + dk_here
                if jp == 0:
                    dq_ref[j] = dq_here
                else:
                    dq_ref[j] += dq_here
            dk, dv = dk.astype(BF), dv.astype(BF)
            for i in range(NS):
                dkv_refs[i][rows, jp * T : (jp + 1) * T] = dk[:, i * T : (i + 1) * T]
                dkv_refs[i][v_rows, jp * T : (jp + 1) * T] = dv[:, i * T : (i + 1) * T]
        for j in range(NS):
            dq = (dq_ref[j] * HD ** (-0.5)).astype(BF)
            for i in range(NS):
                dq_refs[i][rows, j * T : (j + 1) * T] = dq[:, i * T : (i + 1) * T]
        return carry

    lax.fori_loop(0, HL, head, 0)


def attend_back(place, queries, keyvals, grads):
    out = pl.pallas_call(
        attend_back_kernel,
        out_shape=[jax.ShapeDtypeStruct((HW, QR), BF)] * NS
        + [jax.ShapeDtypeStruct((2 * HW, QR), BF)] * NS,
        in_specs=[SMEM] + [VMEM] * 9,
        out_specs=[VMEM] * 8,
        scratch_shapes=[
            pltpu.VMEM((HL, 8, QR), F32),
            pltpu.VMEM((HL, 8, QR), F32),
            pltpu.VMEM((QR, QR), F32),
            pltpu.VMEM((NS, HD, QR), F32),
        ],
        compiler_params=params(),
        cost_estimate=pl.CostEstimate(
            flops=10 * 30 * QR * QR * HD, bytes_accessed=6 << 20, transcendentals=30 * QR * QR
        ),
        name="attend_back",
    )(place, *queries, *keyvals, grads)
    return out[0:NS], out[NS:]


def pick_rows(target, offset):
    lines = lax.broadcasted_iota(jnp.int32, (T, ROWS), 1)
    return (lines == target + offset).astype(F32).astype(BF)


def norm_two(middle):
    factor = lax.rsqrt(jnp.mean(middle * middle, axis=-1, keepdims=True) + EPS)
    return middle * factor, factor


def route_kernel(
    place_ref, x_ref, small_ref, router_ref, ids_ref, cot_ref, o0, o1, o2, o3, w0, w1, w2, w3,
    out_ref, m_ref, a_ref, gate_ref, target_ref, o_ref, w_ref, lse_ref,
):
    for k, (o_piece, w_piece) in enumerate(((o0, w0), (o1, w1), (o2, w2), (o3, w3))):
        o_ref[block_at(place_ref, k, HW), :] = o_piece[0:HW, :]
        w_ref[block_at(place_ref, k, HW), :] = w_piece[...]
        logs = lse_of(o_piece[HW:PACK, :].astype(F32))
        lse_ref[(place_ref[3] + place_ref[2] * k) & 3] = jnp.concatenate(
            [logs, jnp.zeros((8 - HL, T), F32)], axis=0
        )
    branch = dot(o_ref[...], w_ref[...], 0, 1)
    middle = x_ref[...].astype(F32) + branch + small_ref[2:3, :]
    unit, factor = norm_two(middle)
    second = (unit * small_ref[1:2, :]).astype(BF)
    logits = dot(second, router_ref[...], 1, 0)
    cols = lax.broadcasted_iota(jnp.int32, (T, CD), 1)
    named = [(ids_ref[:, k : k + 1] == cols).astype(F32) for k in range(TOPK)]
    earlier = lax.broadcasted_iota(jnp.int32, (T, T), 1) < lax.broadcasted_iota(
        jnp.int32, (T, T), 0
    )
    counts = dot(earlier.astype(F32).astype(BF), (named[0] + named[1]).astype(BF), 1, 0)
    chosen = [jnp.sum(name * logits, axis=1, keepdims=True) for name in named]
    top = jnp.maximum(chosen[0], chosen[1])
    raw = [jnp.exp(value - top) for value in chosen]
    gates = [value / (raw[0] + raw[1]) for value in raw]
    slots = [jnp.sum(name * counts, axis=1, keepdims=True).astype(jnp.int32) for name in named]
    targets = [ids_ref[:, k : k + 1] * SLOTS + slots[k] for k in range(TOPK)]
    grads = cot_ref[...].astype(F32)
    places = jnp.concatenate(
        [pick_rows(targets[0], 0) + pick_rows(targets[1], 0)]
        + [pick_rows(targets[k], CAP) for k in range(TOPK)],
        axis=0,
    )
    values = jnp.concatenate([second] + [(gates[k] * grads).astype(BF) for k in range(TOPK)], axis=0)
    out_ref[...] = dot(places, values, 0, 0).astype(BF)
    m_ref[...] = middle
    a_ref[...] = second
    gate_ref[...] = jnp.concatenate(gates, axis=1)
    target_ref[...] = jnp.concatenate(targets, axis=1)


def route(place, rows, small, router, ids, cotangent, pieces, out_weights):
    return pl.pallas_call(
        route_kernel,
        out_shape=[
            jax.ShapeDtypeStruct((ROWS, D), BF),
            jax.ShapeDtypeStruct((T, D), F32),
            jax.ShapeDtypeStruct((T, D), BF),
            jax.ShapeDtypeStruct((T, TOPK), F32),
            jax.ShapeDtypeStruct((T, TOPK), jnp.int32),
            jax.ShapeDtypeStruct((D, T), BF),
            jax.ShapeDtypeStruct((D, D), BF),
            jax.ShapeDtypeStruct((NS, 8, T), F32),
        ],
        in_specs=[SMEM] + [VMEM] * 13,
        out_specs=[VMEM] * 8,
        compiler_params=params(),
        name="route",
    )(place, rows, small, router, ids, cotangent, *pieces, *out_weights)


GELU_A = float(np.sqrt(2.0 / np.pi))
GELU_B = 0.044715


def expert_kernel(
    rows_ref, pick_ref, win_ref, wout_ref, out_ref, gin_ref, act_ref, dy_ref, a_ref, y_ref, da_ref
):
    step = pl.program_id(0)

    @pl.when(step == 0)
    def first():
        both = dot(pick_ref[...], rows_ref[...], 1, 0).astype(BF)
        a_ref[...] = both[0:LINES]
        dy_ref[...] = both[LINES:]

    inner, outer = win_ref[0], wout_ref[0]
    pre = dot(a_ref[...], inner, 1, 0)
    act_grad = dot(dy_ref[...], outer, 1, 0)
    square = pre * pre
    bent = jnp.tanh(GELU_A * pre * (1.0 + GELU_B * square))
    act = (0.5 * pre * (1.0 + bent)).astype(BF)
    slope = 0.5 * (1.0 + bent) + 0.5 * pre * (1.0 - bent * bent) * (
        GELU_A * (1.0 + 3.0 * GELU_B * square)
    )
    pre_grad = (act_grad * slope).astype(BF)
    act_ref[...] = act
    gin_ref[0] = dot(a_ref[...], pre_grad, 0, 0).astype(BF)
    made = dot(act, outer, 1, 1)
    back = dot(pre_grad, inner, 1, 1)

    @pl.when(step == 0)
    def start():
        y_ref[...] = made
        da_ref[...] = back

    @pl.when(step > 0)
    def more():
        y_ref[...] += made
        da_ref[...] += back

    @pl.when(step == pl.num_programs(0) - 1)
    def last():
        both = jnp.concatenate([y_ref[...].astype(BF), da_ref[...].astype(BF)], axis=0)
        out_ref[...] = dot(pick_ref[...], both, 0, 0).astype(BF)


def expert(rows, inner, outer):
    def whole(*shape):
        return pl.BlockSpec(shape, lambda i: (0, 0))

    weight = pl.BlockSpec((1, D, D), lambda i: (i, 0, 0))
    hidden = pl.BlockSpec((LINES, D), lambda i: (0, i))
    return pl.pallas_call(
        expert_kernel,
        grid=(NS,),
        out_shape=[
            jax.ShapeDtypeStruct((ROWS, D), BF),
            jax.ShapeDtypeStruct((NS, D, D), BF),
            jax.ShapeDtypeStruct((LINES, NS * D), BF),
            jax.ShapeDtypeStruct((LINES, D), BF),
        ],
        in_specs=[whole(ROWS, D), whole(2 * LINES, ROWS), weight, weight],
        out_specs=[whole(ROWS, D), weight, hidden, whole(LINES, D)],
        scratch_shapes=[
            pltpu.VMEM((LINES, D), BF),
            pltpu.VMEM((LINES, D), F32),
            pltpu.VMEM((LINES, D), F32),
        ],
        compiler_params=params(dimension_semantics=("arbitrary",)),
        cost_estimate=pl.CostEstimate(
            flops=10 * LINES * D * 4 * D, bytes_accessed=18 << 20, transcendentals=LINES * 4 * D
        ),
        name="expert",
    )(rows, jnp.asarray(expert_pick(), BF), inner, outer)


def outer_grad_kernel(dy_ref, act_ref, gout_ref):
    gout_ref[0] = dot(dy_ref[...], act_ref[...], 0, 0).astype(BF)


def outer_grad_of(grads, act):
    return pl.pallas_call(
        outer_grad_kernel,
        grid=(NS,),
        out_shape=jax.ShapeDtypeStruct((NS, D, D), BF),
        in_specs=[
            pl.BlockSpec((LINES, D), lambda i: (0, 0)),
            pl.BlockSpec((LINES, D), lambda i: (0, i)),
        ],
        out_specs=pl.BlockSpec((1, D, D), lambda i: (i, 0, 0)),
        compiler_params=params(dimension_semantics=("arbitrary",)),
        cost_estimate=pl.CostEstimate(
            flops=2 * LINES * D * 4 * D, bytes_accessed=7 << 20, transcendentals=0
        ),
        name="outer_grad",
    )(grads, act)


def widen_kernel(in_ref, out_ref):
    out_ref[...] = in_ref[...].astype(F32)


def widen(values):
    rows, width = values.shape
    spec = pl.BlockSpec((rows // 4, width), lambda i: (i, 0))
    return pl.pallas_call(
        widen_kernel,
        grid=(4,),
        out_shape=jax.ShapeDtypeStruct(values.shape, F32),
        in_specs=[spec],
        out_specs=spec,
        cost_estimate=pl.CostEstimate(
            flops=rows * width, bytes_accessed=6 * rows * width, transcendentals=0
        ),
        name="widen",
    )(values)


def expert_pick():
    lines = np.arange(LINES)
    pick = np.zeros((2 * LINES, ROWS), np.float32)
    pick[lines, lines // CAP * SLOTS + lines % CAP] = 1.0
    pick[LINES + lines, lines // CAP * SLOTS + CAP + lines % CAP] = 1.0
    return pick


def settle_kernel(
    place_ref, back_ref, m_ref, a_ref, gate_ref, target_ref, ids_ref, cot_ref, small_ref, router_ref,
    w_ref, o_ref, lse_ref,
    mixed_ref, dm_ref, rg_ref, sums_ref, out_ref, d0, d1, d2, d3, turn_ref,
):
    back = back_ref[...]
    targets = [target_ref[:, k : k + 1] for k in range(TOPK)]
    picked = [dot(pick_rows(target, 0), back, 1, 0) for target in targets]
    returned = dot(pick_rows(targets[0], CAP) + pick_rows(targets[1], CAP), back, 1, 0)
    middle = m_ref[...]
    grads = cot_ref[...].astype(F32)
    gates = [gate_ref[:, k : k + 1] for k in range(TOPK)]
    mixed_ref[...] = (middle + gates[0] * picked[0] + gates[1] * picked[1]).astype(BF)
    gate_grads = [jnp.sum(grads * value, axis=1, keepdims=True) for value in picked]
    mean = gates[0] * gate_grads[0] + gates[1] * gate_grads[1]
    cols = lax.broadcasted_iota(jnp.int32, (T, CD), 1)
    logit_grad = functools.reduce(
        jnp.add,
        [
            jnp.where(ids_ref[:, k : k + 1] == cols, gates[k] * (gate_grads[k] - mean), 0.0)
            for k in range(TOPK)
        ],
    ).astype(BF)
    rg_ref[...] = dot(a_ref[...], logit_grad, 0, 0)
    second_grad = dot(logit_grad, router_ref[...], 1, 1) + returned
    unit, factor = norm_two(middle)
    weighted = second_grad * small_ref[1:2, :]
    whole = grads + factor * (weighted - unit * jnp.mean(weighted * unit, axis=-1, keepdims=True))
    dm_ref[...] = whole
    rounded = whole.astype(BF)
    head_grads = dot(rounded, w_ref[...], 1, 0).T.astype(BF)
    product = head_grads.astype(F32) * o_ref[...].astype(F32)
    rest = jnp.zeros((PACK - HW - 5 * HL, T), F32)
    for s in range(NS):
        delta = [
            jnp.sum(product[s * HW + h * HD : s * HW + (h + 1) * HD], axis=0, keepdims=True)
            for h in range(HL)
        ]
        high, middle, low = split3(lse_ref[s][0:HL])
        d_high, d_middle, unused = split3(jnp.concatenate(delta, axis=0))
        stats = jnp.concatenate([high, middle, low, d_high, d_middle, rest], axis=0).astype(BF)
        for z in range(NS):
            out_ref[s * NS + z, 0:HW, :] = head_grads[s * HW : (s + 1) * HW]
            out_ref[s * NS + z, HW:PACK, :] = stats
    turn_ref[...] = rounded.astype(F32).T.astype(BF)
    for k, d_ref in enumerate((d0, d1, d2, d3)):
        d_ref[...] = turn_ref[block_at(place_ref, k, HW), :]
    sums_ref[...] = jnp.concatenate(
        [
            jnp.sum(second_grad * unit, axis=0, keepdims=True),
            jnp.sum(rounded.astype(F32), axis=0, keepdims=True),
            jnp.zeros((6, D), F32),
        ],
        axis=0,
    )


def settle(place, back, middle, second, gates, targets, ids, cotangent, small, router, weight, heads, lse):
    out = pl.pallas_call(
        settle_kernel,
        out_shape=[
            jax.ShapeDtypeStruct((T, D), BF),
            jax.ShapeDtypeStruct((T, D), F32),
            jax.ShapeDtypeStruct((D, CD), F32),
            jax.ShapeDtypeStruct((8, D), F32),
            jax.ShapeDtypeStruct((NS * NS, PACK, T), BF),
        ]
        + [jax.ShapeDtypeStruct((HW, T), BF)] * NS,
        in_specs=[SMEM] + [VMEM] * 12,
        out_specs=[VMEM] * 9,
        scratch_shapes=[pltpu.VMEM((D, T), BF)],
        compiler_params=params(),
        name="settle",
    )(
        place, back, middle, second, gates, targets, ids, cotangent, small, router, weight, heads, lse
    )
    return out[0:5], out[5:9]


def arrival_constants():
    rows = np.zeros((D, LINES_ALL), np.float32)
    thirds = np.zeros((3, LINES_ALL, D), np.float32)
    for g in range(D):
        n, i = divmod(g, 6)
        start = (n % CD * NS + n // CD) * 8
        rows[g, start + i] = 1.0
        thirds[i % 3, start + 6 + i // 3, g] = 1.0
    return rows, thirds


def room_block():
    rows = np.zeros((QR, HALF), np.float32)
    for g in range(HALF):
        rows[g // 6 * 8 + g % 6, g] = 1.0
    return rows


def room_thirds():
    thirds = np.zeros((3, QR, HALF), np.float32)
    for g in range(HALF):
        n, i = divmod(g, 6)
        thirds[i % 3, n * 8 + 6 + i // 3, g] = 1.0
    return thirds


def bias_constants():
    lines = np.zeros((256, HW), np.float32)
    lanes = np.zeros((2, HW, 64), np.float32)
    for r in range(HW):
        n, i = divmod(r, 6)
        lines[n * 8 + 6, r] = 1.0
        lanes[0, r, CD + 3 + i] = 1.0
        lanes[1, r, CD + 9 + i] = 1.0
    return lines, lanes


def spread(rows, width):
    return jnp.pad(rows, [(0, 0)] * (rows.ndim - 1) + [(0, width - rows.shape[-1])])


def per_device(
    tokens,
    qkv_weight,
    out_weight,
    router_weight,
    attn_gain,
    ffn_gain,
    query_bias,
    value_bias,
    out_bias,
    expert_in,
    expert_out,
    expert_ids,
    cotangent,
):
    rows_at, thirds_at = [jnp.asarray(value, BF) for value in arrival_constants()]
    seq = lax.axis_index("seq")
    back = 2 * lax.axis_index("dp") - 1
    place = jnp.stack([lax.axis_index("z"), lax.axis_index("y"), back, seq]).astype(jnp.int32)
    mine = (jnp.arange(NS) == seq).astype(BF)
    rows = tokens.reshape(T, D)
    ids = expert_ids.reshape(T, TOPK)
    cot = cotangent.reshape(T, D)

    inner = lax.all_gather(expert_in[0], "seq", axis=0, tiled=False)
    outer = lax.all_gather(expert_out[0], "seq", axis=0, tiled=False)

    columns = qkv_weight.reshape(6, 3, NS, HW).transpose(2, 0, 1, 3).reshape(NS, 6, 3 * HW)
    extras = jnp.concatenate(
        [router_weight, attn_gain[:, None], ffn_gain[:, None], out_bias[:, None]], axis=1
    )
    upper = jnp.concatenate(
        [columns, jnp.broadcast_to(spread(extras, 64)[None], (NS, 6, 64))], axis=2
    )
    quarters = out_weight.reshape(2, 3, NS, HW).transpose(2, 0, 1, 3).reshape(NS, 2, 3 * HW)
    biases = jnp.concatenate([query_bias, value_bias])[None, None] * mine[:, None, None]
    corner = jnp.pad(biases, ((0, 0), (0, 1), (0, 52)))
    lower = jnp.concatenate([quarters, corner], axis=2)
    sent = jnp.concatenate([upper, lower], axis=1)
    sent = swap_seq(sent).reshape(1, NS * 8, 640)
    arrived = swap_experts(jnp.broadcast_to(sent, (CD, NS * 8, 640)))
    weights = arrived.reshape(LINES_ALL, 640)
    sorted_weights = dot(rows_at, weights, 1, 0).astype(BF)
    qkv = sorted_weights[:, : 3 * HW]
    router = sorted_weights[:, 3 * HW : 3 * HW + CD]
    small = dot(weights[:, 608:616], rows_at, 0, 1)
    own_bias = jnp.sum(
        arrived.reshape(CD, NS, 8, 640)[:, :, 6, 576:588].astype(F32), axis=1
    )
    bias = jnp.concatenate(
        [own_bias[:, :6].reshape(HW), jnp.zeros((HW,), F32), own_bias[:, 6:].reshape(HW)]
    )

    stream = gather_seq(rows, back).reshape(QR, D)
    first_in = (norm_two(stream.astype(F32))[0] * small[0:1]).astype(BF)
    projected = (dot(qkv, first_in, 0, 1) + bias[:, None]).astype(BF)
    keyvals = collect(projected[HW:], "y")
    queries = collect(projected[:HW] * jnp.asarray(HD ** (-0.5), BF), "z")
    out_piece = sum(
        dot(weights[:, part * HW : (part + 1) * HW], thirds_at[part], 0, 0) for part in range(3)
    ).astype(BF)
    out_weights = collect(out_piece, "x")
    partial = attend(place, queries, keyvals)
    partial, out_weights = lax.optimization_barrier((partial, out_weights))
    pieces = merge(place, deliver(partial, "z"))
    pieces = [pieces[0]] + [jump(pieces[k], "x", k) for k in range(1, NS)]

    outgoing, middle, second, gates, targets, whole_heads, weight, lse = route(
        place, rows, small, router, ids, cot, pieces, out_weights
    )
    received = swap_experts(outgoing.reshape(CD, SLOTS, D)).reshape(ROWS, D)
    others = deliver([whole_heads] * NS, "x")
    made, inner_grad, act, expert_dy = expert(received, inner, outer)
    returned = swap_experts(made.reshape(CD, SLOTS, D))
    returned, outer_grad = lax.optimization_barrier((returned, outer_grad_of(expert_dy, act)))
    returned = returned.reshape(ROWS, D)
    inner_grad = lax.psum_scatter(inner_grad, "seq", scatter_dimension=0, tiled=False)
    outer_grad = lax.psum_scatter(outer_grad, "seq", scatter_dimension=0, tiled=False)
    (mixed, middle_grad, router_grad, sums, heads_grad), column_pieces = settle(
        place, returned, middle, second, gates, targets, ids, cot, small, router, weight,
        whole_heads, lse,
    )

    heads_grad = swap_plane(heads_grad)
    column_pieces, heads_grad = lax.optimization_barrier((column_pieces, heads_grad))
    column_pieces = deliver(column_pieces, "x")
    query_parts, keyval_parts = attend_back(place, queries, keyvals, heads_grad)
    out_grad = out_grad_of(column_pieces, others)
    room = jnp.asarray(room_block(), BF)
    room_in = jnp.concatenate([dot(room, half, 1, 1) for half in jnp.split(first_in, 2, axis=1)])
    after = jnp.concatenate(
        [router_grad.astype(BF), jnp.zeros((D, 1), BF), sums[0:2].T.astype(BF)], axis=1
    )
    extra = spread(jnp.concatenate([dot(room, half, 1, 0) for half in jnp.split(after, 2)]), 64)
    keyval_grads, unused = deliver_sum(keyval_parts, "y")
    query_grads, (out_grad, room_in, extra) = deliver_sum(
        query_parts, "z", (out_grad, room_in.astype(BF), extra.astype(BF))
    )
    keyval_grads, inner_grad = lax.optimization_barrier((keyval_grads, widen(inner_grad)))
    parts, grads, gain = first_grad(place, query_grads, keyval_grads, qkv, stream)
    grads = finish(place, grads, gain, room_in, out_grad, extra)
    parts = deliver(parts, "x")

    dealt = swap_all(grads.reshape(NS * CD, 8, 640))
    dealt = dealt.reshape(NS, CD, 8, 640)
    totals = jnp.sum(dealt.astype(F32), axis=1)
    extra = jnp.sum(totals[:, :, 3 * HW :], axis=0)
    whole_qkv = (
        totals[:, :6, : 3 * HW].reshape(NS, 6, 3, HW).transpose(1, 2, 0, 3).reshape(6, 3 * D)
    )
    whole_out = totals[:, 6:, : 3 * HW].reshape(NS, 2, 3, HW).transpose(1, 2, 0, 3).reshape(6, D)
    parts, whole_qkv, whole_out, extra = lax.optimization_barrier(
        (parts, whole_qkv, whole_out, extra)
    )
    mine_grad = sum(part.astype(F32) for part in parts)
    own_unit, own_factor = norm_two(rows.astype(F32))
    weighted = mine_grad * small[0:1]
    input_grad = middle_grad + own_factor * (
        weighted - own_unit * jnp.mean(weighted * own_unit, axis=-1, keepdims=True)
    )
    return (
        mixed.reshape(tokens.shape),
        input_grad.astype(BF).reshape(tokens.shape),
        whole_qkv,
        whole_out,
        extra[:6, :CD],
        extra[:6, CD],
        extra[:6, CD + 1],
        extra[6, CD + 3 : CD + 9],
        extra[6, CD + 9 : CD + 15],
        extra[:6, CD + 2],
        inner_grad[None],
        widen(outer_grad)[None],
    )


def solution(mesh):
    sizes = (mesh.shape["seq"], NS, mesh.shape["ctx"] // NS, mesh.shape["dp"])
    return jax.shard_map(
        per_device,
        mesh=jax.sharding.Mesh(mesh.devices.reshape(sizes), ALL),
        in_specs=(
            P("dp", ALL[:3], None),
            P(ALL, None),
            P(ALL, None),
            P(ALL, None),
            P(ALL),
            P(ALL),
            P(ALL),
            P(ALL),
            P(ALL),
            P(ALL[1:], None, "seq"),
            P(ALL[1:], None, "seq"),
            P("dp", ALL[:3], None),
            P("dp", ALL[:3], None),
        ),
        out_specs=(
            P("dp", ALL[:3], None),
            P("dp", ALL[:3], None),
            P(ALL, None),
            P(ALL, None),
            P(ALL, None),
            P(ALL),
            P(ALL),
            P(ALL),
            P(ALL),
            P(ALL),
            P(ALL[1:], None, "seq"),
            P(ALL[1:], None, "seq"),
        ),
        check_vma=False,
    )
```

```python
import functools

import jax
import jax.numpy as jnp
import numpy as np
from jax import lax
from jax.experimental import pallas as pl
from jax.experimental.pallas import tpu as pltpu
from jax.sharding import PartitionSpec as P

H = 12
HD = 64
TOPK = 2
D = 768
T = 128
NS = 4
HL = H // NS
HW = HL * HD
QR = NS * T
CD = 32
CAP = 9
SLOTS = 24
ROWS = CD * SLOTS
LINES = CD * CAP
LINES_ALL = 8 * 4 * CD
HALF = D // 2
PACK = 208

ALL = ("seq", "z", "y", "dp")

EPS = 1e-06
MASKED = -1e30
BF = jnp.bfloat16
F32 = jnp.float32

VMEM = pl.BlockSpec(memory_space=pltpu.VMEM)
SMEM = pl.BlockSpec(memory_space=pltpu.SMEM)


def dot(former, latter, former_dim, latter_dim):
    return lax.dot_general(
        former,
        latter,
        (((former_dim,), (latter_dim,)), ((), ())),
        preferred_element_type=F32,
    )


def params(**more):
    return pltpu.CompilerParams(vmem_limit_bytes=56 * 1024 * 1024, **more)


def jump(values, axis, steps):
    pairs = []
    for x in range(NS):
        for z in range(NS):
            for y in range(NS):
                for core in range(2):
                    far = {"x": x, "z": z, "y": y}
                    far[axis] += -steps if core else steps
                    there = (far["x"] % NS * NS + far["z"] % NS) * NS + far["y"] % NS
                    pairs.append((((x * NS + z) * NS + y) * 2 + core, there * 2 + core))
    return lax.ppermute(values, ALL, pairs)


def collect(values, axis):
    return [values] + [jump(values, axis, k) for k in range(1, NS)]


def deliver(pieces, axis):
    return [pieces[0]] + [jump(pieces[k], axis, -k) for k in range(1, NS)]


def deliver_sum(pieces, axis, beside=()):
    middle = jump(pieces[2], axis, 1)
    first = jump(pieces[1], axis, -1)
    onward, beside = lax.optimization_barrier((pieces[3], tuple(beside)))
    third = jump((onward.astype(F32) + middle.astype(F32)).astype(BF), axis, 1)
    return (pieces[0], first, third), beside


def swap_experts(values):
    return lax.all_to_all(values, ALL[1:], split_axis=0, concat_axis=0, tiled=True)


def swap_plane(values):
    return lax.all_to_all(values, ("seq", "z"), split_axis=0, concat_axis=0, tiled=True)


def swap_seq(values):
    return lax.all_to_all(values, "seq", split_axis=0, concat_axis=0, tiled=True)


def swap_all(values):
    return lax.all_to_all(values, ALL, split_axis=0, concat_axis=0, tiled=True)


def gather_seq(values, back):
    place = lax.axis_index("seq")
    whole = jnp.zeros((NS,) + values.shape, values.dtype)
    for k, piece in enumerate(collect(values, "x")):
        whole = lax.dynamic_update_slice(whole, piece[None], ((place + back * k) % NS, 0, 0))
    return whole


def tile_of(refs, rows, j):
    return jnp.concatenate([ref[rows, j * T : (j + 1) * T] for ref in refs], axis=1)


def causal_tile(place_ref):
    z, y, back = place_ref[0], place_ref[1], place_ref[2]
    k_index = lax.broadcasted_iota(jnp.int32, (QR, QR), 0)
    q_index = lax.broadcasted_iota(jnp.int32, (QR, QR), 1)
    k_place = z * QR + (((y + back * (k_index >> 7)) & 3) << 7) + (k_index & 127)
    q_place = (((z + back * (q_index >> 7)) & 3) << 9) + y * T + (q_index & 127)
    return k_place <= q_place


def split3(values):
    high = values.astype(BF).astype(F32)
    middle = (values - high).astype(BF).astype(F32)
    return high, middle, values - high - middle


def z_at(place_ref, k):
    return (place_ref[0] + place_ref[2] * k) & 3


def attend_kernel(place_ref, *refs):
    q_refs, kv_refs, o_refs, lse_ref, bias_ref = refs[0:4], refs[4:8], refs[8:12], refs[12], refs[13]
    bias_ref[...] = jnp.where(causal_tile(place_ref), 0.0, MASKED)
    work = [(j, jp) for j in range(NS) for jp in range(j + 1)]

    def head(h, carry):
        rows = pl.ds(pl.multiple_of(h * HD, HD), HD)
        v_rows = pl.ds(pl.multiple_of(HW + h * HD, HD), HD)
        k_tiles = [tile_of(kv_refs, rows, jp) for jp in range(NS)]
        v_tiles = [tile_of(kv_refs, v_rows, jp) for jp in range(NS)]

        def scores_of(j, jp):
            scores = dot(k_tiles[jp], tile_of(q_refs, rows, j), 0, 0)
            return jnp.where(bias_ref[...] < 0.0, MASKED, scores) if jp == j else scores

        following = scores_of(*work[0])
        for n, (j, jp) in enumerate(work):
            scores = following
            if n + 1 < len(work):
                following = scores_of(*work[n + 1])
            here = jnp.max(scores, axis=0, keepdims=True)
            if jp == 0:
                top = here
                probs = jnp.exp(scores - top)
                total = jnp.sum(probs, axis=0, keepdims=True)
                acc = dot(v_tiles[jp], probs.astype(BF), 1, 0)
            else:
                higher = jnp.maximum(top, here)
                fade = jnp.exp(top - higher)
                probs = jnp.exp(scores - higher)
                total = total * fade + jnp.sum(probs, axis=0, keepdims=True)
                acc = acc * fade + dot(v_tiles[jp], probs.astype(BF), 1, 0)
                top = higher
            if jp == j:
                out = (acc / total).astype(BF)
                lse = top + jnp.log(total)
                for k in range(NS):
                    o_refs[k][rows, j * T : (j + 1) * T] = out[:, k * T : (k + 1) * T]
                    lse_ref[h, k : k + 1, j * T : (j + 1) * T] = lse[:, k * T : (k + 1) * T]
        return carry

    lax.fori_loop(0, HL, head, 0)
    for k in range(NS):
        logs = jnp.concatenate([lse_ref[h, k : k + 1, :] for h in range(HL)], axis=0)
        o_refs[k][HW:PACK, :] = log_rows(logs)


def log_rows(logs):
    rest = jnp.zeros((PACK - HW - 3 * HL, logs.shape[1]), F32)
    return jnp.concatenate([*split3(logs), rest], axis=0).astype(BF)


def attend(place, queries, keyvals):
    return pl.pallas_call(
        attend_kernel,
        out_shape=[jax.ShapeDtypeStruct((PACK, QR), BF)] * NS,
        in_specs=[SMEM] + [VMEM] * 8,
        out_specs=[VMEM] * NS,
        scratch_shapes=[pltpu.VMEM((HL, 8, QR), F32), pltpu.VMEM((QR, QR), F32)],
        compiler_params=params(),
        cost_estimate=pl.CostEstimate(
            flops=4 * 30 * QR * QR * HD, bytes_accessed=4 << 20, transcendentals=30 * QR * QR
        ),
        name="attend",
    )(place, *queries, *keyvals)


def lse_of(stats):
    return stats[0:HL] + stats[HL : 2 * HL] + stats[2 * HL : 3 * HL]


def block_at(place_ref, k, size):
    return pl.ds(pl.multiple_of(((place_ref[3] + place_ref[2] * k) & 3) * size, 64), size)


def merge_kernel(place_ref, *refs):
    parts, piece_refs, o_ref = refs[0:4], refs[4:8], refs[8]
    logs = [lse_of(part[HW:PACK, :].astype(F32)) for part in parts]
    top = functools.reduce(jnp.maximum, logs)
    lse = top + jnp.log(functools.reduce(jnp.add, [jnp.exp(log - top) for log in logs]))
    shares = [jnp.exp(log - lse) for log in logs]
    for h in range(HL):
        rows = slice(h * HD, (h + 1) * HD)
        o_ref[rows, :] = functools.reduce(
            jnp.add,
            [part[rows, :].astype(F32) * share[h : h + 1] for part, share in zip(parts, shares)],
        ).astype(BF)
    o_ref[HW:PACK, :] = log_rows(lse)
    for k, piece in enumerate(piece_refs):
        block = (place_ref[3] - place_ref[2] * k) & 3
        piece[...] = o_ref[:, pl.ds(pl.multiple_of(block * T, T), T)]


def merge(place, parts):
    return pl.pallas_call(
        merge_kernel,
        out_shape=[jax.ShapeDtypeStruct((PACK, T), BF)] * NS,
        in_specs=[SMEM] + [VMEM] * 4,
        out_specs=[VMEM] * NS,
        scratch_shapes=[pltpu.VMEM((PACK, QR), BF)],
        compiler_params=params(),
        name="merge",
    )(place, *parts)


def out_grad_kernel(*refs):
    pieces, others, third_ref, out_ref = refs[0:4], refs[4:8], refs[8], refs[9]
    grads = functools.reduce(
        jnp.add,
        [dot(other[...], piece[...], 1, 1) for piece, other in zip(pieces, others)],
    ).astype(BF)
    for block in range(2):
        rows = grads[block * HALF : (block + 1) * HALF]
        for part in range(3):
            out_ref[block * QR : (block + 1) * QR, part * HW : (part + 1) * HW] = dot(
                third_ref[part], rows, 1, 0
            ).astype(BF)


def out_grad_of(pieces, others):
    return pl.pallas_call(
        out_grad_kernel,
        out_shape=jax.ShapeDtypeStruct((LINES_ALL, 3 * HW), BF),
        in_specs=[VMEM] * 9,
        out_specs=VMEM,
        compiler_params=params(),
        cost_estimate=pl.CostEstimate(
            flops=4 * D * D * QR, bytes_accessed=4 << 20, transcendentals=0
        ),
        name="out_grad",
    )(*pieces, *others, jnp.asarray(room_thirds(), BF))


def first_grad_kernel(
    place_ref, q0, q1, q3, k0, k1, k3, qkv_ref, x_ref,
    p0, p1, p2, p3, grads_ref, gain_ref, first_ref,
):
    def total(refs):
        return functools.reduce(jnp.add, [ref[...].astype(F32) for ref in refs]).astype(BF)

    grads = jnp.concatenate([total((q0, q1, q3)), total((k0, k1, k3))], axis=0)
    grads_ref[...] = grads
    first = dot(grads, qkv_ref[...], 0, 1)
    first_ref[...] = first.astype(BF)
    for k, piece in enumerate((p0, p1, p2, p3)):
        piece[...] = first_ref[block_at(place_ref, k, T), :]
    unit, factor = norm_two(x_ref[...].astype(F32))
    gain = jnp.sum(first * unit, axis=0, keepdims=True)
    gain_ref[...] = jnp.broadcast_to(gain, (8, D))


def first_grad(place, queries, keyvals, qkv, stream):
    out = pl.pallas_call(
        first_grad_kernel,
        out_shape=[jax.ShapeDtypeStruct((T, D), BF)] * NS
        + [jax.ShapeDtypeStruct((3 * HW, QR), BF), jax.ShapeDtypeStruct((8, D), F32)],
        in_specs=[SMEM] + [VMEM] * 8,
        out_specs=[VMEM] * 6,
        scratch_shapes=[pltpu.VMEM((QR, D), BF)],
        compiler_params=params(),
        name="first_grad",
    )(place, *queries, *keyvals, qkv, stream)
    return list(out[0:4]), out[4], out[5]


def finish_kernel(
    place_ref, grads_ref, gain_ref, room_in_ref, og_ref, extra_ref,
    room_ref, line_ref, lane_ref, out_ref, tail_ref,
):
    grads = grads_ref[...]
    main = dot(room_in_ref[...], grads, 1, 1) + og_ref[...].astype(F32)
    out_ref[:, 0:QR] = main[:, 0:QR].astype(BF)
    at_gain = lax.broadcasted_iota(jnp.int32, (64, D), 0) == CD
    gains = jnp.where(at_gain, gain_ref[0:1, :], 0.0).astype(BF)
    for block in range(2):
        span = slice(block * QR, (block + 1) * QR)
        extra = extra_ref[span, :].astype(F32) + dot(
            room_ref[...], gains[:, block * HALF : (block + 1) * HALF], 1, 1
        )
        tail_ref[span, :] = jnp.concatenate([main[span, QR:], extra], axis=1)
    sums = jnp.sum(grads.astype(F32), axis=1, keepdims=True)
    biases = sums[0:HW] * lane_ref[0] + sums[2 * HW :] * lane_ref[1]
    own = pl.ds(pl.multiple_of(place_ref[3] * 256, 256), 256)
    tail_ref[own, :] += jnp.concatenate(
        [jnp.zeros((256, 64), F32), dot(line_ref[...], biases.astype(BF), 1, 0)], axis=1
    )
    out_ref[:, QR:] = tail_ref[...].astype(BF)


def finish(place, grads, gain, room_in, out_grad, extra):
    lines, lanes = bias_constants()
    return pl.pallas_call(
        finish_kernel,
        out_shape=jax.ShapeDtypeStruct((LINES_ALL, 640), BF),
        in_specs=[SMEM] + [VMEM] * 8,
        out_specs=VMEM,
        scratch_shapes=[pltpu.VMEM((LINES_ALL, 128), F32)],
        compiler_params=params(),
        name="finish",
    )(
        place, grads, gain, room_in, out_grad, extra,
        jnp.asarray(room_block(), BF), jnp.asarray(lines, BF), jnp.asarray(lanes, F32),
    )


TILES = [(jp, j) for jp in range(NS) for j in range(jp, NS)]


def weigh_kernel(place_ref, *refs):
    q_refs, kv_refs, part_refs = refs[0:4], refs[4:8], refs[8:12]
    out_ref, lse_ref, bias_ref = refs[12], refs[13], refs[14]
    h = pl.program_id(0)

    @pl.when(h == 0)
    def first():
        bias_ref[...] = jnp.where(causal_tile(place_ref), 0.0, MASKED)
        keep_logs(part_refs, lse_ref)

    rows = pl.ds(pl.multiple_of(h * HD, HD), HD)
    for n, (jp, j) in enumerate(TILES):
        scores = dot(tile_of(kv_refs, rows, jp), tile_of(q_refs, rows, j), 0, 0)
        if jp == j:
            scores = jnp.where(bias_ref[...] < 0.0, MASKED, scores)
        above = scores - row_of(lse_ref, h, j)
        if jp == j:
            above = jnp.minimum(above, 0.0)
        out_ref[n] = jnp.exp(above).astype(BF)


def keep_logs(part_refs, lse_ref):
    for k in range(NS):
        logs = lse_of(part_refs[k][HW:PACK, :].astype(F32))
        for h in range(HL):
            lse_ref[h, k : k + 1, :] = logs[h : h + 1]


def row_of(ref, h, j):
    return jnp.concatenate(
        [ref[h, k : k + 1, j * T : (j + 1) * T] for k in range(NS)], axis=1
    )


def weigh(place, queries, keyvals, partial):
    tiles = len(TILES)
    return pl.pallas_call(
        weigh_kernel,
        grid=(HL,),
        out_shape=jax.ShapeDtypeStruct((HL * tiles, QR, QR), BF),
        in_specs=[SMEM] + [VMEM] * 12,
        out_specs=pl.BlockSpec((tiles, QR, QR), lambda h: (h, 0, 0)),
        scratch_shapes=[pltpu.VMEM((HL, 8, QR), F32), pltpu.VMEM((QR, QR), F32)],
        compiler_params=params(dimension_semantics=("arbitrary",)),
        cost_estimate=pl.CostEstimate(
            flops=2 * 30 * QR * QR * HD, bytes_accessed=18 << 20, transcendentals=30 * QR * QR
        ),
        name="weigh",
    )(place, *queries, *keyvals, *partial)


def attend_back_kernel(place_ref, *refs):
    q_refs, kv_refs, part_refs, do_ref, probs_ref = refs[0:4], refs[4:8], refs[8:12], refs[12], refs[13]
    dq_refs, dkv_refs = refs[14:18], refs[18:22]
    share_ref, delta_ref, dq_ref, held_ref, sems = refs[22:27]
    tiles = len(TILES)

    def fetch(n):
        return pltpu.make_async_copy(probs_ref.at[n], held_ref.at[n], sems.at[n])

    for n in range(HL * tiles):
        fetch(n).start()
    for k in range(NS):
        logs = lse_of(part_refs[k][HW:PACK, :].astype(F32))
        for j in range(NS):
            lanes = slice(j * T, (j + 1) * T)
            stats = do_ref[j * NS + z_at(place_ref, k), HW:PACK, :].astype(F32)
            shares = jnp.exp(logs[:, lanes] - lse_of(stats))
            deltas = shares * (stats[3 * HL : 4 * HL] + stats[4 * HL : 5 * HL])
            for h in range(HL):
                share_ref[h, k : k + 1, lanes] = shares[h : h + 1]
                delta_ref[h, k : k + 1, lanes] = deltas[h : h + 1]

    def head(h, carry):
        rows = pl.ds(pl.multiple_of(h * HD, HD), HD)
        v_rows = pl.ds(pl.multiple_of(HW + h * HD, HD), HD)
        do_tiles = []
        for j in range(NS):
            do_tile = jnp.concatenate(
                [do_ref[j * NS + z_at(place_ref, k), rows, :] for k in range(NS)], axis=1
            )
            do_tiles.append((do_tile.astype(F32) * row_of(share_ref, h, j)).astype(BF))
        for n, (jp, j) in enumerate(TILES):
            if j == jp:
                k_tile = tile_of(kv_refs, rows, jp)
                v_tile = tile_of(kv_refs, v_rows, jp)
                dk = jnp.zeros((HD, QR), F32)
                dv = jnp.zeros((HD, QR), F32)
            fetch(h * tiles + n).wait()
            probs = held_ref[h * tiles + n]
            slopes = dot(v_tile, do_tiles[j], 0, 0)
            ds = (probs.astype(F32) * (slopes - row_of(delta_ref, h, j))).astype(BF)
            dv += dot(do_tiles[j], probs, 1, 1)
            dk += dot(tile_of(q_refs, rows, j), ds, 1, 1)
            dq_here = dot(k_tile, ds, 1, 0)
            if jp == 0:
                dq_ref[j] = dq_here
            else:
                dq_ref[j] += dq_here
            if j == NS - 1:
                for k in range(NS):
                    span = slice(k * T, (k + 1) * T)
                    dkv_refs[k][rows, jp * T : (jp + 1) * T] = dk.astype(BF)[:, span]
                    dkv_refs[k][v_rows, jp * T : (jp + 1) * T] = dv.astype(BF)[:, span]
        for j in range(NS):
            dq = (dq_ref[j] * HD ** (-0.5)).astype(BF)
            for k in range(NS):
                dq_refs[k][rows, j * T : (j + 1) * T] = dq[:, k * T : (k + 1) * T]
        return carry

    lax.fori_loop(0, HL, head, 0)


def attend_back(place, queries, keyvals, partial, grads, probs):
    tiles = len(TILES)
    out = pl.pallas_call(
        attend_back_kernel,
        out_shape=[jax.ShapeDtypeStruct((HW, QR), BF)] * NS
        + [jax.ShapeDtypeStruct((2 * HW, QR), BF)] * NS,
        in_specs=[SMEM] + [VMEM] * 13 + [pl.BlockSpec(memory_space=pl.ANY)],
        out_specs=[VMEM] * 8,
        scratch_shapes=[
            pltpu.VMEM((HL, 8, QR), F32),
            pltpu.VMEM((HL, 8, QR), F32),
            pltpu.VMEM((NS, HD, QR), F32),
            pltpu.VMEM((HL * tiles, QR, QR), BF),
            pltpu.SemaphoreType.DMA((HL * tiles,)),
        ],
        compiler_params=params(),
        cost_estimate=pl.CostEstimate(
            flops=8 * 30 * QR * QR * HD, bytes_accessed=22 << 20, transcendentals=0
        ),
        name="attend_back",
    )(place, *queries, *keyvals, *partial, grads, probs)
    return out[0:NS], out[NS:]


def pick_rows(target, offset):
    lines = lax.broadcasted_iota(jnp.int32, (T, ROWS), 1)
    return (lines == target + offset).astype(F32).astype(BF)


def norm_two(middle):
    factor = lax.rsqrt(jnp.mean(middle * middle, axis=-1, keepdims=True) + EPS)
    return middle * factor, factor


def route_kernel(
    place_ref, x_ref, small_ref, router_ref, ids_ref, cot_ref, o0, o1, o2, o3, w0, w1, w2, w3,
    out_ref, m_ref, a_ref, gate_ref, target_ref, o_ref, w_ref, lse_ref,
):
    for k, (o_piece, w_piece) in enumerate(((o0, w0), (o1, w1), (o2, w2), (o3, w3))):
        o_ref[block_at(place_ref, k, HW), :] = o_piece[0:HW, :]
        w_ref[block_at(place_ref, k, HW), :] = w_piece[...]
        logs = lse_of(o_piece[HW:PACK, :].astype(F32))
        lse_ref[(place_ref[3] + place_ref[2] * k) & 3] = jnp.concatenate(
            [logs, jnp.zeros((8 - HL, T), F32)], axis=0
        )
    branch = dot(o_ref[...], w_ref[...], 0, 1)
    middle = x_ref[...].astype(F32) + branch + small_ref[2:3, :]
    unit, factor = norm_two(middle)
    second = (unit * small_ref[1:2, :]).astype(BF)
    logits = dot(second, router_ref[...], 1, 0)
    cols = lax.broadcasted_iota(jnp.int32, (T, CD), 1)
    named = [(ids_ref[:, k : k + 1] == cols).astype(F32) for k in range(TOPK)]
    earlier = lax.broadcasted_iota(jnp.int32, (T, T), 1) < lax.broadcasted_iota(
        jnp.int32, (T, T), 0
    )
    counts = dot(earlier.astype(F32).astype(BF), (named[0] + named[1]).astype(BF), 1, 0)
    chosen = [jnp.sum(name * logits, axis=1, keepdims=True) for name in named]
    top = jnp.maximum(chosen[0], chosen[1])
    raw = [jnp.exp(value - top) for value in chosen]
    gates = [value / (raw[0] + raw[1]) for value in raw]
    slots = [jnp.sum(name * counts, axis=1, keepdims=True).astype(jnp.int32) for name in named]
    targets = [ids_ref[:, k : k + 1] * SLOTS + slots[k] for k in range(TOPK)]
    grads = cot_ref[...].astype(F32)
    places = jnp.concatenate(
        [pick_rows(targets[0], 0) + pick_rows(targets[1], 0)]
        + [pick_rows(targets[k], CAP) for k in range(TOPK)],
        axis=0,
    )
    values = jnp.concatenate([second] + [(gates[k] * grads).astype(BF) for k in range(TOPK)], axis=0)
    out_ref[...] = dot(places, values, 0, 0).astype(BF)
    m_ref[...] = middle
    a_ref[...] = second
    gate_ref[...] = jnp.concatenate(gates, axis=1)
    target_ref[...] = jnp.concatenate(targets, axis=1)


def route(place, rows, small, router, ids, cotangent, pieces, out_weights):
    return pl.pallas_call(
        route_kernel,
        out_shape=[
            jax.ShapeDtypeStruct((ROWS, D), BF),
            jax.ShapeDtypeStruct((T, D), F32),
            jax.ShapeDtypeStruct((T, D), BF),
            jax.ShapeDtypeStruct((T, TOPK), F32),
            jax.ShapeDtypeStruct((T, TOPK), jnp.int32),
            jax.ShapeDtypeStruct((D, T), BF),
            jax.ShapeDtypeStruct((D, D), BF),
            jax.ShapeDtypeStruct((NS, 8, T), F32),
        ],
        in_specs=[SMEM] + [VMEM] * 13,
        out_specs=[VMEM] * 8,
        compiler_params=params(),
        name="route",
    )(place, rows, small, router, ids, cotangent, *pieces, *out_weights)


GELU_A = float(np.sqrt(2.0 / np.pi))
GELU_B = 0.044715


def expert_kernel(
    rows_ref, pick_ref, win_ref, wout_ref, out_ref, gin_ref, act_ref, dy_ref, a_ref, y_ref, da_ref
):
    step = pl.program_id(0)

    @pl.when(step == 0)
    def first():
        both = dot(pick_ref[...], rows_ref[...], 1, 0).astype(BF)
        a_ref[...] = both[0:LINES]
        dy_ref[...] = both[LINES:]

    inner, outer = win_ref[0], wout_ref[0]
    pre = dot(a_ref[...], inner, 1, 0)
    act_grad = dot(dy_ref[...], outer, 1, 0)
    square = pre * pre
    bent = jnp.tanh(GELU_A * pre * (1.0 + GELU_B * square))
    act = (0.5 * pre * (1.0 + bent)).astype(BF)
    slope = 0.5 * (1.0 + bent) + 0.5 * pre * (1.0 - bent * bent) * (
        GELU_A * (1.0 + 3.0 * GELU_B * square)
    )
    pre_grad = (act_grad * slope).astype(BF)
    act_ref[...] = act
    gin_ref[0] = dot(a_ref[...], pre_grad, 0, 0).astype(BF)
    made = dot(act, outer, 1, 1)
    back = dot(pre_grad, inner, 1, 1)

    @pl.when(step == 0)
    def start():
        y_ref[...] = made
        da_ref[...] = back

    @pl.when(step > 0)
    def more():
        y_ref[...] += made
        da_ref[...] += back

    @pl.when(step == pl.num_programs(0) - 1)
    def last():
        both = jnp.concatenate([y_ref[...].astype(BF), da_ref[...].astype(BF)], axis=0)
        out_ref[...] = dot(pick_ref[...], both, 0, 0).astype(BF)


def expert(rows, inner, outer):
    def whole(*shape):
        return pl.BlockSpec(shape, lambda i: (0, 0))

    weight = pl.BlockSpec((1, D, D), lambda i: (i, 0, 0))
    hidden = pl.BlockSpec((LINES, D), lambda i: (0, i))
    return pl.pallas_call(
        expert_kernel,
        grid=(NS,),
        out_shape=[
            jax.ShapeDtypeStruct((ROWS, D), BF),
            jax.ShapeDtypeStruct((NS, D, D), BF),
            jax.ShapeDtypeStruct((LINES, NS * D), BF),
            jax.ShapeDtypeStruct((LINES, D), BF),
        ],
        in_specs=[whole(ROWS, D), whole(2 * LINES, ROWS), weight, weight],
        out_specs=[whole(ROWS, D), weight, hidden, whole(LINES, D)],
        scratch_shapes=[
            pltpu.VMEM((LINES, D), BF),
            pltpu.VMEM((LINES, D), F32),
            pltpu.VMEM((LINES, D), F32),
        ],
        compiler_params=params(dimension_semantics=("arbitrary",)),
        cost_estimate=pl.CostEstimate(
            flops=10 * LINES * D * 4 * D, bytes_accessed=18 << 20, transcendentals=LINES * 4 * D
        ),
        name="expert",
    )(rows, jnp.asarray(expert_pick(), BF), inner, outer)


def outer_grad_kernel(dy_ref, act_ref, gout_ref):
    gout_ref[0] = dot(dy_ref[...], act_ref[...], 0, 0).astype(BF)


def outer_grad_of(grads, act):
    return pl.pallas_call(
        outer_grad_kernel,
        grid=(NS,),
        out_shape=jax.ShapeDtypeStruct((NS, D, D), BF),
        in_specs=[
            pl.BlockSpec((LINES, D), lambda i: (0, 0)),
            pl.BlockSpec((LINES, D), lambda i: (0, i)),
        ],
        out_specs=pl.BlockSpec((1, D, D), lambda i: (i, 0, 0)),
        compiler_params=params(dimension_semantics=("arbitrary",)),
        cost_estimate=pl.CostEstimate(
            flops=2 * LINES * D * 4 * D, bytes_accessed=7 << 20, transcendentals=0
        ),
        name="outer_grad",
    )(grads, act)


def widen_kernel(in_ref, out_ref):
    out_ref[...] = in_ref[...].astype(F32)


def widen(values):
    rows, width = values.shape
    spec = pl.BlockSpec((rows // 4, width), lambda i: (i, 0))
    return pl.pallas_call(
        widen_kernel,
        grid=(4,),
        out_shape=jax.ShapeDtypeStruct(values.shape, F32),
        in_specs=[spec],
        out_specs=spec,
        cost_estimate=pl.CostEstimate(
            flops=rows * width, bytes_accessed=6 * rows * width, transcendentals=0
        ),
        name="widen",
    )(values)


def expert_pick():
    lines = np.arange(LINES)
    pick = np.zeros((2 * LINES, ROWS), np.float32)
    pick[lines, lines // CAP * SLOTS + lines % CAP] = 1.0
    pick[LINES + lines, lines // CAP * SLOTS + CAP + lines % CAP] = 1.0
    return pick


def settle_kernel(
    place_ref, back_ref, m_ref, a_ref, gate_ref, target_ref, ids_ref, cot_ref, small_ref, router_ref,
    w_ref, o_ref, lse_ref,
    mixed_ref, dm_ref, rg_ref, sums_ref, out_ref, d0, d1, d2, d3, turn_ref,
):
    back = back_ref[...]
    targets = [target_ref[:, k : k + 1] for k in range(TOPK)]
    picked = [dot(pick_rows(target, 0), back, 1, 0) for target in targets]
    returned = dot(pick_rows(targets[0], CAP) + pick_rows(targets[1], CAP), back, 1, 0)
    middle = m_ref[...]
    grads = cot_ref[...].astype(F32)
    gates = [gate_ref[:, k : k + 1] for k in range(TOPK)]
    mixed_ref[...] = (middle + gates[0] * picked[0] + gates[1] * picked[1]).astype(BF)
    gate_grads = [jnp.sum(grads * value, axis=1, keepdims=True) for value in picked]
    mean = gates[0] * gate_grads[0] + gates[1] * gate_grads[1]
    cols = lax.broadcasted_iota(jnp.int32, (T, CD), 1)
    logit_grad = functools.reduce(
        jnp.add,
        [
            jnp.where(ids_ref[:, k : k + 1] == cols, gates[k] * (gate_grads[k] - mean), 0.0)
            for k in range(TOPK)
        ],
    ).astype(BF)
    rg_ref[...] = dot(a_ref[...], logit_grad, 0, 0)
    second_grad = dot(logit_grad, router_ref[...], 1, 1) + returned
    unit, factor = norm_two(middle)
    weighted = second_grad * small_ref[1:2, :]
    whole = grads + factor * (weighted - unit * jnp.mean(weighted * unit, axis=-1, keepdims=True))
    dm_ref[...] = whole
    rounded = whole.astype(BF)
    head_grads = dot(rounded, w_ref[...], 1, 0).T.astype(BF)
    product = head_grads.astype(F32) * o_ref[...].astype(F32)
    rest = jnp.zeros((PACK - HW - 5 * HL, T), F32)
    for s in range(NS):
        delta = [
            jnp.sum(product[s * HW + h * HD : s * HW + (h + 1) * HD], axis=0, keepdims=True)
            for h in range(HL)
        ]
        high, middle, low = split3(lse_ref[s][0:HL])
        d_high, d_middle, unused = split3(jnp.concatenate(delta, axis=0))
        stats = jnp.concatenate([high, middle, low, d_high, d_middle, rest], axis=0).astype(BF)
        for z in range(NS):
            out_ref[s * NS + z, 0:HW, :] = head_grads[s * HW : (s + 1) * HW]
            out_ref[s * NS + z, HW:PACK, :] = stats
    turn_ref[...] = rounded.astype(F32).T.astype(BF)
    for k, d_ref in enumerate((d0, d1, d2, d3)):
        d_ref[...] = turn_ref[block_at(place_ref, k, HW), :]
    sums_ref[...] = jnp.concatenate(
        [
            jnp.sum(second_grad * unit, axis=0, keepdims=True),
            jnp.sum(rounded.astype(F32), axis=0, keepdims=True),
            jnp.zeros((6, D), F32),
        ],
        axis=0,
    )


def settle(place, back, middle, second, gates, targets, ids, cotangent, small, router, weight, heads, lse):
    out = pl.pallas_call(
        settle_kernel,
        out_shape=[
            jax.ShapeDtypeStruct((T, D), BF),
            jax.ShapeDtypeStruct((T, D), F32),
            jax.ShapeDtypeStruct((D, CD), F32),
            jax.ShapeDtypeStruct((8, D), F32),
            jax.ShapeDtypeStruct((NS * NS, PACK, T), BF),
        ]
        + [jax.ShapeDtypeStruct((HW, T), BF)] * NS,
        in_specs=[SMEM] + [VMEM] * 12,
        out_specs=[VMEM] * 9,
        scratch_shapes=[pltpu.VMEM((D, T), BF)],
        compiler_params=params(),
        name="settle",
    )(
        place, back, middle, second, gates, targets, ids, cotangent, small, router, weight, heads, lse
    )
    return out[0:5], out[5:9]


def arrival_constants():
    rows = np.zeros((D, LINES_ALL), np.float32)
    thirds = np.zeros((3, LINES_ALL, D), np.float32)
    for g in range(D):
        n, i = divmod(g, 6)
        start = (n % CD * NS + n // CD) * 8
        rows[g, start + i] = 1.0
        thirds[i % 3, start + 6 + i // 3, g] = 1.0
    return rows, thirds


def room_block():
    rows = np.zeros((QR, HALF), np.float32)
    for g in range(HALF):
        rows[g // 6 * 8 + g % 6, g] = 1.0
    return rows


def room_thirds():
    thirds = np.zeros((3, QR, HALF), np.float32)
    for g in range(HALF):
        n, i = divmod(g, 6)
        thirds[i % 3, n * 8 + 6 + i // 3, g] = 1.0
    return thirds


def bias_constants():
    lines = np.zeros((256, HW), np.float32)
    lanes = np.zeros((2, HW, 64), np.float32)
    for r in range(HW):
        n, i = divmod(r, 6)
        lines[n * 8 + 6, r] = 1.0
        lanes[0, r, CD + 3 + i] = 1.0
        lanes[1, r, CD + 9 + i] = 1.0
    return lines, lanes


def spread(rows, width):
    return jnp.pad(rows, [(0, 0)] * (rows.ndim - 1) + [(0, width - rows.shape[-1])])


def per_device(
    tokens,
    qkv_weight,
    out_weight,
    router_weight,
    attn_gain,
    ffn_gain,
    query_bias,
    value_bias,
    out_bias,
    expert_in,
    expert_out,
    expert_ids,
    cotangent,
):
    rows_at, thirds_at = [jnp.asarray(value, BF) for value in arrival_constants()]
    seq = lax.axis_index("seq")
    back = 2 * lax.axis_index("dp") - 1
    place = jnp.stack([lax.axis_index("z"), lax.axis_index("y"), back, seq]).astype(jnp.int32)
    mine = (jnp.arange(NS) == seq).astype(BF)
    rows = tokens.reshape(T, D)
    ids = expert_ids.reshape(T, TOPK)
    cot = cotangent.reshape(T, D)

    inner = lax.all_gather(expert_in[0], "seq", axis=0, tiled=False)
    outer = lax.all_gather(expert_out[0], "seq", axis=0, tiled=False)

    columns = qkv_weight.reshape(6, 3, NS, HW).transpose(2, 0, 1, 3).reshape(NS, 6, 3 * HW)
    extras = jnp.concatenate(
        [router_weight, attn_gain[:, None], ffn_gain[:, None], out_bias[:, None]], axis=1
    )
    upper = jnp.concatenate(
        [columns, jnp.broadcast_to(spread(extras, 64)[None], (NS, 6, 64))], axis=2
    )
    quarters = out_weight.reshape(2, 3, NS, HW).transpose(2, 0, 1, 3).reshape(NS, 2, 3 * HW)
    biases = jnp.concatenate([query_bias, value_bias])[None, None] * mine[:, None, None]
    corner = jnp.pad(biases, ((0, 0), (0, 1), (0, 52)))
    lower = jnp.concatenate([quarters, corner], axis=2)
    sent = jnp.concatenate([upper, lower], axis=1)
    sent = swap_seq(sent).reshape(1, NS * 8, 640)
    arrived = swap_experts(jnp.broadcast_to(sent, (CD, NS * 8, 640)))
    weights = arrived.reshape(LINES_ALL, 640)
    sorted_weights = dot(rows_at, weights, 1, 0).astype(BF)
    qkv = sorted_weights[:, : 3 * HW]
    router = sorted_weights[:, 3 * HW : 3 * HW + CD]
    small = sorted_weights[:, 608:616].astype(F32).T
    own_bias = jnp.sum(
        arrived.reshape(CD, NS, 8, 640)[:, :, 6, 576:588].astype(F32), axis=1
    )
    bias = jnp.concatenate(
        [own_bias[:, :6].reshape(HW), jnp.zeros((HW,), F32), own_bias[:, 6:].reshape(HW)]
    )

    stream = gather_seq(rows, back).reshape(QR, D)
    first_in = (norm_two(stream.astype(F32))[0] * small[0:1]).astype(BF)
    projected = (dot(qkv, first_in, 0, 1) + bias[:, None]).astype(BF)
    keyvals = collect(projected[HW:], "y")
    queries = collect(projected[:HW] * jnp.asarray(HD ** (-0.5), BF), "z")
    out_piece = sum(
        dot(weights[:, part * HW : (part + 1) * HW], thirds_at[part], 0, 0) for part in range(3)
    ).astype(BF)
    out_weights = collect(out_piece, "x")
    partial = attend(place, queries, keyvals)
    partial, out_weights = lax.optimization_barrier((partial, out_weights))
    pieces = merge(place, deliver(partial, "z"))
    pieces = [pieces[0]] + [jump(pieces[k], "x", k) for k in range(1, NS)]

    outgoing, middle, second, gates, targets, whole_heads, weight, lse = route(
        place, rows, small, router, ids, cot, pieces, out_weights
    )
    received = swap_experts(outgoing.reshape(CD, SLOTS, D))
    after, own_parts = lax.optimization_barrier((middle, partial))
    probs = weigh(place, queries, keyvals, own_parts)
    received, probs = lax.optimization_barrier((received, probs))
    received = received.reshape(ROWS, D)
    others = deliver([whole_heads] * NS, "x")
    made, inner_grad, act, expert_dy = expert(received, inner, outer)
    returned = swap_experts(made.reshape(CD, SLOTS, D))
    returned, outer_grad = lax.optimization_barrier((returned, outer_grad_of(expert_dy, act)))
    returned = returned.reshape(ROWS, D)
    inner_grad = lax.psum_scatter(inner_grad, "seq", scatter_dimension=0, tiled=False)
    outer_grad = lax.psum_scatter(outer_grad, "seq", scatter_dimension=0, tiled=False)
    (mixed, middle_grad, router_grad, sums, heads_grad), column_pieces = settle(
        place, returned, middle, second, gates, targets, ids, cot, small, router, weight,
        whole_heads, lse,
    )

    heads_grad = swap_plane(heads_grad)
    column_pieces, heads_grad = lax.optimization_barrier((column_pieces, heads_grad))
    column_pieces = deliver(column_pieces, "x")
    query_parts, keyval_parts = attend_back(place, queries, keyvals, partial, heads_grad, probs)
    out_grad = out_grad_of(column_pieces, others)
    room = jnp.asarray(room_block(), BF)
    room_in = jnp.concatenate([dot(room, half, 1, 1) for half in jnp.split(first_in, 2, axis=1)])
    after = jnp.concatenate(
        [router_grad.astype(BF), jnp.zeros((D, 1), BF), sums[0:2].T.astype(BF)], axis=1
    )
    extra = spread(jnp.concatenate([dot(room, half, 1, 0) for half in jnp.split(after, 2)]), 64)
    keyval_grads, unused = deliver_sum(keyval_parts, "y")
    query_grads, (out_grad, room_in, extra) = deliver_sum(
        query_parts, "z", (out_grad, room_in.astype(BF), extra.astype(BF))
    )
    keyval_grads, inner_grad = lax.optimization_barrier((keyval_grads, widen(inner_grad)))
    parts, grads, gain = first_grad(place, query_grads, keyval_grads, qkv, stream)
    grads = finish(place, grads, gain, room_in, out_grad, extra)
    parts = deliver(parts, "x")

    dealt = swap_all(grads.reshape(NS * CD, 8, 640))
    dealt = dealt.reshape(NS, CD, 8, 640)
    totals = jnp.sum(dealt.astype(F32), axis=1)
    extra = jnp.sum(totals[:, :, 3 * HW :], axis=0)
    whole_qkv = (
        totals[:, :6, : 3 * HW].reshape(NS, 6, 3, HW).transpose(1, 2, 0, 3).reshape(6, 3 * D)
    )
    whole_out = totals[:, 6:, : 3 * HW].reshape(NS, 2, 3, HW).transpose(1, 2, 0, 3).reshape(6, D)
    parts, whole_qkv, whole_out, extra = lax.optimization_barrier(
        (parts, whole_qkv, whole_out, extra)
    )
    mine_grad = sum(part.astype(F32) for part in parts)
    own_unit, own_factor = norm_two(rows.astype(F32))
    weighted = mine_grad * small[0:1]
    input_grad = middle_grad + own_factor * (
        weighted - own_unit * jnp.mean(weighted * own_unit, axis=-1, keepdims=True)
    )
    return (
        mixed.reshape(tokens.shape),
        input_grad.astype(BF).reshape(tokens.shape),
        whole_qkv,
        whole_out,
        extra[:6, :CD],
        extra[:6, CD],
        extra[:6, CD + 1],
        extra[6, CD + 3 : CD + 9],
        extra[6, CD + 9 : CD + 15],
        extra[:6, CD + 2],
        inner_grad[None],
        widen(outer_grad)[None],
    )


def solution(mesh):
    sizes = (mesh.shape["seq"], NS, mesh.shape["ctx"] // NS, mesh.shape["dp"])
    return jax.shard_map(
        per_device,
        mesh=jax.sharding.Mesh(mesh.devices.reshape(sizes), ALL),
        in_specs=(
            P("dp", ALL[:3], None),
            P(ALL, None),
            P(ALL, None),
            P(ALL, None),
            P(ALL),
            P(ALL),
            P(ALL),
            P(ALL),
            P(ALL),
            P(ALL[1:], None, "seq"),
            P(ALL[1:], None, "seq"),
            P("dp", ALL[:3], None),
            P("dp", ALL[:3], None),
        ),
        out_specs=(
            P("dp", ALL[:3], None),
            P("dp", ALL[:3], None),
            P(ALL, None),
            P(ALL, None),
            P(ALL, None),
            P(ALL),
            P(ALL),
            P(ALL),
            P(ALL),
            P(ALL),
            P(ALL[1:], None, "seq"),
            P(ALL[1:], None, "seq"),
        ),
        check_vma=False,
    )
```
